32 devices in a mesh: section: 2 (over core), ctx: 4 (over z), dp: 4 (over y, x).
Axes of the slice: x: 2, y: 2, z: 4, core: 2. Of those that a mesh axis runs over, the one named last changes fastest.
Arguments:
- tokens: bfloat16 [3, 4, 1024, 896], P(None, 'dp', 'ctx'), may hold values from -6 to 6
- doc_starts: int32 [3, 4, 4], P(None, 'dp'), may hold values from 0 to 1023, as said below
- cotangent: bfloat16 [3, 4, 1024, 896], P(None, 'dp', 'ctx'), may hold values from -6 to 6
- norm_one: bfloat16 [2, 896], P('section', 'dp'), may hold values from 0.25 to 1.75
- w_query: bfloat16 [2, 896, 896], P('section', 'dp'), may hold values from -0.1875 to 0.1875
- b_query: bfloat16 [2, 896], P('section', 'dp'), may hold values from -3 to 3
- w_key: bfloat16 [2, 896, 128], P('section', 'dp'), may hold values from -0.1875 to 0.1875
- b_key: bfloat16 [2, 128], P('section', 'dp'), may hold values from -3 to 3
- w_value: bfloat16 [2, 896, 128], P('section', 'dp'), may hold values from -0.1875 to 0.1875
- b_value: bfloat16 [2, 128], P('section', 'dp'), may hold values from -3 to 3
- w_out: bfloat16 [2, 896, 896], P('section', 'dp'), may hold values from -0.75 to 0.75
- norm_two: bfloat16 [2, 896], P('section', 'dp'), may hold values from 0.25 to 1.75
- w_gate: bfloat16 [2, 896, 4864], P('section', 'dp'), may hold values from -0.1875 to 0.1875
- w_up: bfloat16 [2, 896, 4864], P('section', 'dp'), may hold values from -0.1875 to 0.1875
- w_down: bfloat16 [2, 4864, 896], P('section', 'dp'), may hold values from -0.078125 to 0.078125
Outputs:
- section_out: bfloat16 [2, 3, 4, 1024, 896], P('section', None, 'dp', 'ctx')
- section_grad: float32 [2, 3, 4, 1024, 896], P('section', None, 'dp', 'ctx')
- grad_norm_one: float32 [2, 896], P('section', 'dp')
- grad_w_query: float32 [2, 896, 896], P('section', 'dp')
- grad_b_query: float32 [2, 896], P('section', 'dp')
- grad_w_key: float32 [2, 896, 128], P('section', 'dp')
- grad_b_key: float32 [2, 128], P('section', 'dp')
- grad_w_value: float32 [2, 896, 128], P('section', 'dp')
- grad_b_value: float32 [2, 128], P('section', 'dp')
- grad_w_out: float32 [2, 896, 896], P('section', 'dp')
- grad_norm_two: float32 [2, 896], P('section', 'dp')
- grad_w_gate: float32 [2, 896, 4864], P('section', 'dp')
- grad_w_up: float32 [2, 896, 4864], P('section', 'dp')
- grad_w_down: float32 [2, 4864, 896], P('section', 'dp')
The draws below stay inside these ranges and needn't reach their ends.
Inputs may be any that keep to these rules, and one draw needn't show every extreme that they name: `doc_starts`: each stream's starts rise strictly from 0; its second document begins within the first 256 tokens and its third within the last 256 tokens, so the second document spans tokens held by every index of ctx. In some stream the last document is its final token alone.
All inputs are finite; a program needn't handle non-finite values.
Results may differ from the reference program's by a relative error of at most 0.03.
Values may be sent and summed in bfloat16 or wider, within the bound.
No kernel may reach another device: no remote copies, remote signals or barrier semaphores. Data moves between devices by JAX's collectives and lax.ppermute only.
A program may use at most 320 MiB of HBM per device.

```python
import jax
import jax.numpy as jnp
from jax import lax

D = 896
HEADS = 14
KV_HEADS = 2
HEAD = 64
FF = 4864
LEN_DEV = 256
MICRO = 3
DOCS = 4
QW = 896
KVW = 128
SEQ = 1024
STREAMS = 4


def draw_doc_starts(key, part):
    key = jax.random.fold_in(key, 7)
    key_one, key_two, key_three = jax.random.split(key, 3)
    shape_rows = (MICRO, STREAMS)
    second = jax.random.randint(key_one, shape_rows, 1, LEN_DEV)
    third_start = jax.random.randint(key_two, shape_rows, SEQ - LEN_DEV + 1, SEQ - 1)
    spread = jax.random.randint(key_three, shape_rows, 0, 1048576)
    fourth = third_start + 1 + spread % (SEQ - 1 - third_start)
    first_row = (jnp.arange(MICRO)[:, None] == 0) & (jnp.arange(STREAMS)[None, :] == 0)
    fourth = jnp.where(first_row, SEQ - 1, fourth)
    return jnp.stack([jnp.zeros(shape_rows, jnp.int32), second, third_start, fourth], axis=-1).astype(jnp.int32)


def shard_levels(rng, dims, cuts, smallest, high):
    factor_of, own = 1.0, jax.random.fold_in(rng, 6)
    for dim, blocks in cuts:
        draws = jnp.exp(jax.random.uniform(jax.random.fold_in(own, dim), (blocks,), jnp.float32, smallest / len(cuts), high / len(cuts)))
        factor_of = factor_of * jnp.repeat(draws, dims[dim] // blocks).reshape([-1 if axis == dim else 1 for axis in range(len(dims))])
    return factor_of


def gaussian(rng, shape, deviation, bound, cuts=(), kind=jnp.bfloat16):
    factor_of = shard_levels(rng, shape, cuts, -0.22, 0.18) if cuts else 1.0
    values = jax.random.normal(rng, shape, jnp.float32) * deviation * factor_of
    return jnp.minimum(jnp.maximum(values, -bound), bound).astype(kind)


def setup_inputs(seed: int = 0) -> dict:
    key_of = jax.random.split(jax.random.key(seed), 16)
    tokens = gaussian(key_of[0], (MICRO, STREAMS, SEQ, D), 1.0, 6.0, ((1, 4), (2, 4)))
    doc_starts = draw_doc_starts(jax.random.fold_in(key_of[15], 71), 0)
    cotangent = gaussian(key_of[2], (MICRO, STREAMS, SEQ, D), 1.0, 6.0, ((1, 4), (2, 4)))
    norm_one = jnp.clip(1.0 + 0.15 * jax.random.normal(key_of[3], (2, D), jnp.float32), 0.25, 1.75).astype(jnp.bfloat16)
    w_query = gaussian(key_of[4], (2, D, QW), D ** -0.5, 0.1875, ((0, 2), (1, 4)))
    b_query = gaussian(key_of[5], (2, QW), 0.5, 3.0, ((0, 2), (1, 4)))
    w_key = gaussian(key_of[6], (2, D, KVW), D ** -0.5, 0.1875, ((0, 2), (1, 4)))
    b_key = gaussian(key_of[7], (2, KVW), 0.5, 3.0, ((0, 2), (1, 4)))
    w_value = gaussian(key_of[8], (2, D, KVW), D ** -0.5, 0.1875, ((0, 2), (1, 4)))
    b_value = gaussian(key_of[9], (2, KVW), 0.5, 3.0, ((0, 2), (1, 4)))
    w_out = gaussian(key_of[10], (2, QW, D), (QW // 16) ** -0.5, 0.75, ((0, 2), (1, 4)))
    norm_two = jnp.clip(1.0 + 0.15 * jax.random.normal(key_of[11], (2, D), jnp.float32), 0.25, 1.75).astype(jnp.bfloat16)
    w_gate = gaussian(key_of[12], (2, D, FF), D ** -0.5, 0.1875, ((0, 2), (1, 4)))
    w_up = gaussian(key_of[13], (2, D, FF), D ** -0.5, 0.1875, ((0, 2), (1, 4)))
    w_down = gaussian(key_of[14], (2, FF, D), FF ** -0.5, 0.078125, ((0, 2), (1, 4)))
    return dict(tokens=tokens, doc_starts=doc_starts, cotangent=cotangent, norm_one=norm_one, w_query=w_query, b_query=b_query, w_key=w_key, b_key=b_key, w_value=w_value, b_value=b_value, w_out=w_out, norm_two=norm_two, w_gate=w_gate, w_up=w_up, w_down=w_down)


rope_base = 1000000.0
norm_eps = 1e-06
masked = -1e+30

@jax.custom_vjp
def low(v):
    return lax.optimization_barrier(v.astype(jnp.bfloat16)).astype(jnp.float32)

@jax.custom_vjp
def low_back(v):
    return v

def low_keep(v):
    return (low(v), None)

def low_pass(kept, grad):
    return (grad,)

def back_keep(v):
    return (v, None)

def back_low(kept, grad):
    return (low(grad),)
low.defvjp(low_keep, low_pass)
low_back.defvjp(back_keep, back_low)

def product(left, right):
    return jnp.dot(left, right, precision=lax.Precision.HIGHEST, preferred_element_type=jnp.float32)

def norm_scale(values, gain):
    inverse = lax.rsqrt(lax.optimization_barrier(jnp.mean(values * values, axis=-1, keepdims=True)) + norm_eps)
    return values * inverse * gain

def rotate(values, cos_table, sin_table):
    row_count = values.shape[0]
    by_head = values.reshape(row_count, -1, HEAD)
    half_size = HEAD // 2
    turned = jnp.concatenate([-by_head[..., half_size:], by_head[..., :half_size]], axis=-1)
    return (by_head * cos_table[:, None, :] + turned * sin_table[:, None, :]).reshape(row_count, -1)

def tables(starts, places):
    begins = lax.optimization_barrier(jnp.max(jnp.where(starts[None, :] <= places[:, None], starts[None, :], 0), axis=1)).astype(jnp.int32)
    offsets = (places - begins).astype(jnp.float32)
    frequency = rope_base ** (-jnp.arange(0, HEAD, 2, dtype=jnp.float32) / HEAD)
    angles = offsets[:, None] * frequency[None, :]
    angles = jnp.concatenate([angles, angles], axis=-1)
    return (begins, jnp.cos(angles), jnp.sin(angles))

def section_fn(values, layer, cos_table, sin_table, places, begins):
    gain_one, w_query, b_query, w_key, b_key, w_value, b_value, w_out, gain_two, w_gate, w_up, w_down = layer
    length_all = values.shape[0]
    group_size = HEADS // KV_HEADS
    normed = low(norm_scale(values, gain_one))
    queries = low(rotate(low_back(product(normed, w_query) + b_query), cos_table, sin_table))
    key_rows = low(rotate(low_back(product(normed, w_key) + b_key), cos_table, sin_table))
    value_rows = low(low_back(product(normed, w_value) + b_value))
    query_heads = queries.reshape(length_all, KV_HEADS, group_size, HEAD)
    key_heads = key_rows.reshape(length_all, KV_HEADS, HEAD)
    value_heads = value_rows.reshape(length_all, KV_HEADS, HEAD)
    scores = low_back(jnp.einsum('qhgd,khd->hgqk', query_heads, key_heads, precision=lax.Precision.HIGHEST) * HEAD ** (-0.5))
    visible = (places[None, :] <= places[:, None]) & (places[None, :] >= begins[:, None])
    probs = low(jax.nn.softmax(jnp.where(visible, scores, masked), axis=-1))
    output = jnp.einsum('hgqk,khd->qhgd', probs, value_heads, precision=lax.Precision.HIGHEST).reshape(length_all, QW)
    attended = low(low_back(output))
    residual = values + low_back(product(attended, w_out))
    mixing = low(norm_scale(residual, gain_two))
    gate_rows = low_back(product(mixing, w_gate))
    up_rows = low_back(product(mixing, w_up))
    hidden = low(jax.nn.silu(gate_rows) * up_rows)
    return residual + low_back(product(hidden, w_down))

def reference(tokens, doc_starts, cotangent, norm_one, w_query, b_query, w_key, b_key, w_value, b_value, w_out, norm_two, w_gate, w_up, w_down):
    weights = tuple((array.astype(jnp.float32) for array in (norm_one, w_query, b_query, w_key, b_key, w_value, b_value, w_out, norm_two, w_gate, w_up, w_down)))
    places = jnp.arange(SEQ, dtype=jnp.int32)
    inputs = tokens.astype(jnp.float32).reshape(MICRO * STREAMS, SEQ, D)
    starts_all = doc_starts.reshape(MICRO * STREAMS, DOCS)
    upstream = cotangent.astype(jnp.float32).reshape(MICRO * STREAMS, SEQ, D)
    layer_one = tuple((array[0] for array in weights))
    layer_two = tuple((array[1] for array in weights))

    def visit(totals, record):
        values, starts, grad_rows = record
        begins, cos_table, sin_table = tables(starts, places)

        def one_section(rows_in, layer):
            return low(section_fn(rows_in, layer, cos_table, sin_table, places, begins))
        middle, pull_one = jax.vjp(one_section, values, layer_one)
        final_rows, pull_two = jax.vjp(one_section, middle, layer_two)
        grad_middle, grads_two = pull_two(grad_rows)
        grad_input, grads_one = pull_one(grad_middle)
        totals = tuple((total + jnp.stack([term_one, term_two]) for total, term_one, term_two in zip(totals, grads_one, grads_two)))
        return (totals, (middle, final_rows, grad_input, grad_middle))
    zero_grads = tuple((jnp.zeros(array.shape, jnp.float32) for array in weights))
    totals, (middles, finals, grads_input, grads_middle) = lax.scan(visit, zero_grads, (inputs, starts_all, upstream))
    section_out = jnp.stack([middles, finals]).reshape(2, MICRO, STREAMS, SEQ, D).astype(jnp.bfloat16)
    section_grad = jnp.stack([grads_input, grads_middle]).reshape(2, MICRO, STREAMS, SEQ, D)
    return (section_out, section_grad, totals[0], totals[1], totals[2], totals[3], totals[4], totals[5], totals[6], totals[7], totals[8], totals[9], totals[10], totals[11])
```

```python
import functools

import jax
import jax.numpy as jnp
from jax import lax
from jax.experimental import pallas as pl
from jax.experimental.pallas import tpu as pltpu
from jax.sharding import PartitionSpec as P

HEAD = 64
rope_base = 1000000.0
norm_eps = 1e-06
masked = -1e30
bf16 = jnp.bfloat16
f32 = jnp.float32


def matmul(left, right):
    return jnp.dot(left, right, preferred_element_type=f32)


def matmul_nt(left, right):
    return lax.dot_general(left, right, (((1,), (1,)), ((), ())), preferred_element_type=f32)


def inverse_rms(values):
    return lax.rsqrt(jnp.mean(values * values, axis=-1, keepdims=True) + norm_eps)


def step_masks(axis):
    size = lax.axis_size(axis)
    assert size & (size - 1) == 0
    ahead = [1 << n for n in range(size.bit_length() - 1)]
    return list(zip(ahead, ahead[::-1] if axis == "dp" else ahead))


def step(block, axis, masks):
    size = lax.axis_size(axis)
    route = [
        (core * size + i, core * size + (i ^ mask))
        for core, mask in enumerate(masks)
        for i in range(size)
    ]
    return lax.ppermute(block, ("section", axis), route)


def gather_parts(rows, axis):
    for masks in step_masks(axis)[:-1]:
        rows = jnp.concatenate([rows, step(rows, axis, masks)])
    return rows, step(rows, axis, step_masks(axis)[-1])


def gather_blocks(rows, axis):
    return jnp.concatenate(gather_parts(rows, axis)).reshape((-1,) + rows.shape)


def scatter_parts(lower, upper, axis):
    masks = step_masks(axis)
    for pair in masks[:0:-1]:
        total = lower.astype(f32) + step(upper.astype(bf16), axis, pair).astype(f32)
        half = total.shape[0] // 2
        lower, upper = total[:half], total[half:]
    return lower.astype(f32), step(upper.astype(bf16), axis, masks[0])


def reorder(blocks, axis, back=False):
    me = lax.axis_index(axis)
    masks = step_masks(axis)

    def moved(i, core):
        if back:
            return sum(pair[core] for n, pair in enumerate(masks) if i & (1 << n)) ^ me
        return sum(
            jnp.where(((me ^ i) & pair[core]) != 0, 1 << n, 0) for n, pair in enumerate(masks)
        )

    places = [by_section(moved(i, 0), moved(i, 1)) for i in range(blocks.shape[0])]
    return jnp.stack([lax.dynamic_index_in_dim(blocks, place, 0, False) for place in places])


def exchange(blocks, axis):
    blocks = reorder(blocks, axis, back=True)
    count = blocks.shape[0]
    for n, masks in enumerate(step_masks(axis)):
        cut = blocks.reshape((count >> (n + 1), 2, 1 << n) + blocks.shape[1:])
        got = step(cut[:, 1], axis, masks)
        blocks = jnp.stack([cut[:, 0], got], axis=1).reshape(blocks.shape)
    return reorder(blocks, axis)


def other(block):
    return lax.ppermute(block, "section", [(0, 1), (1, 0)])


def by_section(first, second):
    return jnp.where(lax.axis_index("section") == 0, first, second)


def both(mine, axis):
    theirs = other(mine)
    return by_section(jnp.stack([mine, theirs], axis), jnp.stack([theirs, mine], axis))


def after(value, first):
    return lax.optimization_barrier((value, first))[0]


def tables(starts, places):
    begins = jnp.max(jnp.where(starts[None, :] <= places[:, None], starts[None, :], 0), axis=1)
    offsets = (places - begins).astype(f32)
    frequency = rope_base ** (-jnp.arange(0, HEAD, 2, dtype=f32) / HEAD)
    angles = offsets[:, None] * frequency[None, :]
    sines = jnp.sin(angles)
    cos_table = jnp.tile(jnp.cos(angles), (1, lanes * 2 // HEAD))
    sin_table = jnp.tile(jnp.concatenate([-sines, sines], axis=1), (1, lanes // HEAD))
    return (begins, cos_table, sin_table)


vmem_bytes = 56 * 1024 * 1024
lanes = 128


def call(kernel, outs, args, scratch=(), flops=0, grid=None, in_specs=None, out_specs=None):
    moved = sum(a.size * a.dtype.itemsize for a in args)
    moved += sum(o.size * o.dtype.itemsize for o in outs)
    whole = pl.BlockSpec(memory_space=pltpu.VMEM)
    return pl.pallas_call(
        kernel,
        out_shape=outs,
        grid=grid or (),
        in_specs=in_specs or [whole] * len(args),
        out_specs=out_specs or [whole] * len(outs),
        scratch_shapes=scratch,
        cost_estimate=pl.CostEstimate(flops=int(flops), bytes_accessed=int(moved), transcendentals=0),
        compiler_params=pltpu.CompilerParams(vmem_limit_bytes=vmem_bytes),
    )(*args)


def shape(rows, columns, kind):
    return jax.ShapeDtypeStruct((rows, columns), kind)


def lane_of(block):
    return lax.broadcasted_iota(jnp.int32, block.shape, 1)


def turn(block, cos_table, sin_table):
    quarter = HEAD // 2
    first = lax.rem(lane_of(block), HEAD) < quarter
    turned = jnp.where(first, pltpu.roll(block, lanes - quarter, 1), pltpu.roll(block, quarter, 1))
    return block * cos_table + turned * sin_table


def qkv_kernel(x_ref, gain_ref, w_ref, bias_ref, cos_ref, sin_ref, normed_ref, q_ref, kv_ref):
    x = x_ref[...].astype(f32)
    normed = (x * inverse_rms(x) * gain_ref[...]).astype(bf16)
    normed_ref[...] = normed
    cos_table, sin_table = cos_ref[...], sin_ref[...]
    rows = matmul(normed, w_ref[...]) + bias_ref[...]
    query_width = q_ref.shape[1]
    key_end = query_width + kv_ref.shape[1] // 2
    for start in range(0, rows.shape[1], lanes):
        block = rows[:, start : start + lanes]
        if start < key_end:
            block = turn(block, cos_table, sin_table)
        if start < query_width:
            q_ref[:, start : start + lanes] = block.astype(bf16)
        else:
            kv_ref[:, start - query_width : start - query_width + lanes] = block.astype(bf16)


def qkv_rows(x, p, cos_table, sin_table, kv_width):
    rows, width = x.shape
    total = p["qkv"].shape[1]
    query_width = total - 2 * kv_width
    return call(
        qkv_kernel,
        [shape(rows, width, bf16), shape(rows, query_width, bf16), shape(rows, 2 * kv_width, bf16)],
        [x, p["gain_one"], p["qkv"], p["bias"], cos_table, sin_table],
        flops=2 * rows * width * total,
    )


def variants(block):
    swapped = pltpu.roll(block, HEAD, 1)
    low = lane_of(block) < HEAD
    return jnp.where(low, block, swapped), block, jnp.where(low, swapped, block)


def pair_rows(block):
    low = lane_of(block) < HEAD
    return jnp.concatenate([jnp.where(low, block, 0.0), jnp.where(low, 0.0, block)]).astype(bf16)


def pair_columns(block):
    count = block.shape[1] // 2
    return jnp.concatenate([block[:HEAD, :count], block[HEAD:, count:]]).T


def head_kind(pair, group):
    return lax.div(2 * pair, group) + lax.div(2 * pair + 1, group)


def pair_probs(keys, query_pair, bias):
    scores = matmul_nt(keys, query_pair) + jnp.concatenate([bias, bias], axis=1)
    terms = jnp.exp(scores - jnp.max(scores, axis=0, keepdims=True))
    return terms * (1.0 / jnp.sum(terms, axis=0, keepdims=True))


def attend_kernel(
    group,
    q_ref,
    kva_ref,
    kvb_ref,
    bias_ref,
    x_ref,
    wo_ref,
    gain_ref,
    att_ref,
    res_ref,
    mix_ref,
    keys,
    values,
):
    count = kva_ref.shape[0]
    for i, ref in enumerate((kva_ref, kvb_ref)):
        part = slice(i * count, (i + 1) * count)
        for kind, block in enumerate(variants(ref[:, :lanes].astype(f32))):
            keys[kind, part, :] = block.astype(bf16)
        turned = ref[:, lanes:].astype(f32).T.astype(bf16)
        low, high = turned[:HEAD], turned[HEAD:]
        for kind, (one, two) in enumerate(((low, low), (low, high), (high, high))):
            values[kind, :HEAD, part] = one
            values[kind, HEAD:, part] = two

    @pl.loop(0, q_ref.shape[1] // lanes)
    def _(pair):
        place = pl.ds(pl.multiple_of(pair * lanes, lanes), lanes)
        kind = head_kind(pair, group)
        query_pair = pair_rows(q_ref[:, place].astype(f32) * HEAD**-0.5)
        probs = pair_probs(keys[kind], query_pair, bias_ref[...]).astype(bf16)
        att_ref[:, place] = pair_columns(matmul(values[kind], probs)).astype(bf16)

    residual = x_ref[...].astype(f32) + matmul(att_ref[...], wo_ref[...])
    res_ref[...] = residual
    mix_ref[...] = (residual * inverse_rms(residual) * gain_ref[...]).astype(bf16)


def attend(queries, kva, kvb, bias, x, p):
    rows, width = queries.shape
    total = bias.shape[0]
    kv_width = kva.shape[1] // 2
    group = width // kv_width
    flops = 4 * rows * total * width * 4 + 2 * rows * width * x.shape[1]
    return call(
        functools.partial(attend_kernel, group),
        [shape(rows, width, bf16), shape(*x.shape, f32), shape(*x.shape, bf16)],
        [queries, kva, kvb, bias, x, p["out"], p["gain_two"]],
        scratch=[pltpu.VMEM((3, total, lanes), bf16), pltpu.VMEM((3, lanes, total), bf16)],
        flops=flops,
    )


def norm_back(values, gain, grad):
    inverse = inverse_rms(values)
    unit = values * inverse
    scaled = grad * gain
    back = inverse * (scaled - unit * jnp.mean(scaled * unit, axis=-1, keepdims=True))
    return back, jnp.sum(grad * unit, axis=0, keepdims=True)


def attend_back_kernel(
    group,
    q_ref,
    kva_ref,
    kvb_ref,
    bias_ref,
    mix_low_ref,
    mix_got_ref,
    res_ref,
    gain_ref,
    up_ref,
    wo_ref,
    cos_ref,
    sin_ref,
    dq_ref,
    dkva_ref,
    dkvb_ref,
    gres_ref,
    gatt_ref,
    gain_two_ref,
    keys,
    values,
    keys_turned,
    grad_keys,
    grad_values,
    grad_out,
):
    count = kva_ref.shape[0]
    for i, ref in enumerate((kva_ref, kvb_ref)):
        part = slice(i * count, (i + 1) * count)
        key_block = ref[:, :lanes].astype(f32)
        for kind, block in enumerate(variants(key_block)):
            keys[kind, part, :] = block.astype(bf16)
        for kind, block in enumerate(variants(ref[:, lanes:].astype(f32))):
            values[kind, part, :] = block.astype(bf16)
        turned = key_block.T.astype(bf16)
        low, high = turned[:HEAD], turned[HEAD:]
        for kind, (one, two) in enumerate(((low, low), (low, high), (high, high))):
            keys_turned[kind, :HEAD, part] = one
            keys_turned[kind, HEAD:, part] = two

    grad_mixing = mix_low_ref[...] + mix_got_ref[...].astype(f32)
    back, gain_two = norm_back(res_ref[...], gain_ref[...], grad_mixing)
    gain_two_ref[...] = gain_two
    grad_residual = up_ref[...] + back
    gres_ref[...] = grad_residual
    grad_attended = grad_residual.astype(bf16)
    gatt_ref[...] = grad_attended
    grad_out[...] = matmul_nt(grad_attended, wo_ref[...]).astype(bf16)
    grad_keys[...] = jnp.zeros_like(grad_keys)
    grad_values[...] = jnp.zeros_like(grad_values)

    @pl.loop(0, q_ref.shape[1] // lanes)
    def _(pair):
        place = pl.ds(pl.multiple_of(pair * lanes, lanes), lanes)
        kind = head_kind(pair, group)
        query_pair = pair_rows(q_ref[:, place].astype(f32) * HEAD**-0.5)
        out_pair = pair_rows(grad_out[:, place].astype(f32))
        probs = pair_probs(keys[kind], query_pair, bias_ref[...])
        grad_values[kind] += matmul(probs.astype(bf16), out_pair)
        grad_probs = matmul_nt(values[kind], out_pair)
        delta = jnp.sum(probs * grad_probs, axis=0, keepdims=True)
        grad_scores = (probs * (grad_probs - delta)).astype(bf16)
        grad_keys[kind] += matmul(grad_scores, query_pair)
        grad_query = pair_columns(matmul(keys_turned[kind], grad_scores)) * HEAD**-0.5
        dq_ref[:, place] = turn(grad_query, cos_ref[...], -sin_ref[...]).astype(bf16)

    for i, ref in enumerate((dkva_ref, dkvb_ref)):
        part = slice(i * count, (i + 1) * count)
        for n, sums in enumerate((grad_keys, grad_values)):
            first, mixed, second = sums[0, part, :], sums[1, part, :], sums[2, part, :]
            first = first + pltpu.roll(first, HEAD, 1)
            second = second + pltpu.roll(second, HEAD, 1)
            folded = mixed + jnp.where(lane_of(mixed) < HEAD, first, second)
            ref[:, n * lanes : (n + 1) * lanes] = folded.astype(bf16)


def attend_back(
    queries, kva, kvb, bias, mix_low, mix_got, residual, upstream, p, cos_table, sin_table
):
    rows, width = queries.shape
    total = bias.shape[0]
    kv_width = kva.shape[1] // 2
    group = width // kv_width
    flops = 10 * rows * total * width * 3 + 2 * rows * width * residual.shape[1]
    return call(
        functools.partial(attend_back_kernel, group),
        [
            shape(rows, width, bf16),
            shape(*kva.shape, bf16),
            shape(*kvb.shape, bf16),
            shape(*residual.shape, f32),
            shape(*residual.shape, bf16),
            shape(1, residual.shape[1], f32),
        ],
        [
            queries,
            kva,
            kvb,
            bias,
            mix_low,
            mix_got,
            residual,
            p["gain_two"],
            upstream,
            p["out"],
            cos_table,
            sin_table,
        ],
        scratch=[
            pltpu.VMEM((3, total, lanes), bf16),
            pltpu.VMEM((3, total, lanes), bf16),
            pltpu.VMEM((3, lanes, total), bf16),
            pltpu.VMEM((3, total, lanes), f32),
            pltpu.VMEM((3, total, lanes), f32),
            pltpu.VMEM((rows, width), bf16),
        ],
        flops=flops,
    )


def qkv_back_kernel(
    dq_ref,
    low_ref,
    got_ref,
    cos_ref,
    sin_ref,
    w_ref,
    x_ref,
    gain_ref,
    gres_ref,
    dqkv_ref,
    gin_ref,
    gin_low_ref,
    gain_one_ref,
    bias_ref,
):
    query_width = dq_ref.shape[1]
    grad_kv = low_ref[...] + got_ref[...].astype(f32)
    dqkv_ref[:, :query_width] = dq_ref[...]
    grad_key = turn(grad_kv[:, :lanes], cos_ref[...], -sin_ref[...])
    dqkv_ref[:, query_width : query_width + lanes] = grad_key.astype(bf16)
    dqkv_ref[:, query_width + lanes :] = grad_kv[:, lanes:].astype(bf16)
    dqkv = dqkv_ref[...]
    bias_ref[...] = jnp.sum(dqkv.astype(f32), axis=0, keepdims=True)
    grad_normed = matmul_nt(dqkv, w_ref[...])
    back, gain_one = norm_back(x_ref[...].astype(f32), gain_ref[...], grad_normed)
    gain_one_ref[...] = gain_one
    grad_in = gres_ref[...] + back
    gin_ref[...] = grad_in
    gin_low_ref[...] = grad_in.astype(bf16)


def qkv_back(dq, low, got, x, grad_residual, p, cos_table, sin_table):
    rows, width = x.shape
    total = p["qkv"].shape[1]
    return call(
        qkv_back_kernel,
        [
            shape(rows, total, bf16),
            shape(rows, width, f32),
            shape(rows, width, bf16),
            shape(1, width, f32),
            shape(1, total, f32),
        ],
        [dq, low, got, cos_table, sin_table, p["qkv"], x, p["gain_one"], grad_residual],
        flops=2 * rows * width * total,
    )


def chunk_of(size):
    return 256 if size % 256 == 0 else 128


def ffn_kernel(lower_ref, upper_ref, wg_ref, wu_ref, wd_ref, low_ref, up_ref, hid_ref, g_ref, u_ref, rows, total):
    n = pl.program_id(0)
    half = lower_ref.shape[0]

    @pl.when(n == 0)
    def _():
        rows[:half] = lower_ref[...]
        rows[half:] = upper_ref[...]
        total[...] = jnp.zeros_like(total)

    gate = matmul(rows[...], wg_ref[...])
    up = matmul(rows[...], wu_ref[...])
    hidden = (gate * (1.0 / (1.0 + jnp.exp(-gate))) * up).astype(bf16)
    hid_ref[...] = hidden
    g_ref[...] = gate.astype(bf16)
    u_ref[...] = up.astype(bf16)
    total[...] += matmul(hidden, wd_ref[...])

    @pl.when(n == pl.num_programs(0) - 1)
    def _():
        low_ref[...] = total[:half].astype(bf16)
        up_ref[...] = total[half:].astype(bf16)


def ffn(lower, upper, p):
    half, width = lower.shape
    wide = p["gate"].shape[1]
    chunk = chunk_of(wide)
    rows = half + upper.shape[0]
    whole = pl.BlockSpec((half, width), lambda n: (0, 0))
    columns = pl.BlockSpec((width, chunk), lambda n: (0, n))
    return call(
        ffn_kernel,
        [shape(half, width, bf16), shape(rows - half, width, bf16)] + [shape(rows, wide, bf16)] * 3,
        [lower, upper, p["gate"], p["up"], p["down"]],
        scratch=[pltpu.VMEM((rows, width), bf16), pltpu.VMEM((rows, width), f32)],
        flops=6 * rows * width * wide,
        grid=(wide // chunk,),
        in_specs=[whole, whole, columns, columns, pl.BlockSpec((chunk, width), lambda n: (n, 0))],
        out_specs=[whole, whole] + [pl.BlockSpec((rows, chunk), lambda n: (0, n))] * 3,
    )


def ffn_back_kernel(
    lower_ref, upper_ref, g_ref, u_ref, wg_ref, wu_ref, wd_ref, low_ref, up_ref, gg_ref, gu_ref, rows, total
):
    n = pl.program_id(0)
    half = lower_ref.shape[0]

    @pl.when(n == 0)
    def _():
        rows[:half] = lower_ref[...]
        rows[half:] = upper_ref[...]
        total[...] = jnp.zeros_like(total)

    grad_hidden = matmul_nt(rows[...], wd_ref[...])
    gate = g_ref[...].astype(f32)
    up = u_ref[...].astype(f32)
    sigmoid = 1.0 / (1.0 + jnp.exp(-gate))
    grad_up = (grad_hidden * gate * sigmoid).astype(bf16)
    grad_gate = (grad_hidden * up * sigmoid * (1.0 + gate * (1.0 - sigmoid))).astype(bf16)
    gg_ref[...] = grad_gate
    gu_ref[...] = grad_up
    total[...] += matmul_nt(grad_gate, wg_ref[...]) + matmul_nt(grad_up, wu_ref[...])

    @pl.when(n == pl.num_programs(0) - 1)
    def _():
        low_ref[...] = total[:half].astype(bf16)
        up_ref[...] = total[half:].astype(bf16)


def ffn_back(lower, upper, gate, up, p):
    half, width = lower.shape
    wide = p["gate"].shape[1]
    chunk = chunk_of(wide)
    rows = half + upper.shape[0]
    whole = pl.BlockSpec((half, width), lambda n: (0, 0))
    columns = pl.BlockSpec((width, chunk), lambda n: (0, n))
    inner = pl.BlockSpec((rows, chunk), lambda n: (0, n))
    return call(
        ffn_back_kernel,
        [shape(half, width, bf16), shape(rows - half, width, bf16)] + [shape(rows, wide, bf16)] * 2,
        [lower, upper, gate, up, p["gate"], p["up"], p["down"]],
        scratch=[pltpu.VMEM((rows, width), bf16), pltpu.VMEM((rows, width), f32)],
        flops=6 * rows * width * wide,
        grid=(wide // chunk,),
        in_specs=[
            whole,
            whole,
            inner,
            inner,
            columns,
            columns,
            pl.BlockSpec((chunk, width), lambda n: (n, 0)),
        ],
        out_specs=[whole, whole, inner, inner],
    )


def product_kernel(count, turn_once, *refs):
    lefts, rights = refs[:count], refs[count:-2]
    out_ref, turned = refs[-2:]

    def fill():
        start = 0
        for ref in lefts:
            turned[:, start : start + ref.shape[0]] = ref[...].T
            start += ref.shape[0]

    if turn_once:
        pl.when(pl.program_id(0) == 0)(fill)
    else:
        fill()
    right = jnp.concatenate([ref[...] for ref in rights])
    out_ref[...] = matmul(turned[...], right).astype(out_ref.dtype)


def product_over_rows(lefts, rights):
    depth = sum(left.shape[0] for left in lefts)
    height, width = lefts[0].shape[1], rights[0].shape[1]
    by_columns = width % 256 == 0 or height % 256 != 0
    if by_columns:
        chunk = 256 if width % 256 == 0 else (384 if width % 384 == 0 else width)
        grid = (width // chunk,)
        left_specs = [pl.BlockSpec(left.shape, lambda n: (0, 0)) for left in lefts]
        right_specs = [pl.BlockSpec((r.shape[0], chunk), lambda n: (0, n)) for r in rights]
        out_spec = pl.BlockSpec((height, chunk), lambda n: (0, n))
        turned = pltpu.VMEM((height, depth), bf16)
    else:
        chunk = 256
        grid = (height // chunk,)
        left_specs = [pl.BlockSpec((left.shape[0], chunk), lambda n: (0, n)) for left in lefts]
        right_specs = [pl.BlockSpec(r.shape, lambda n: (0, 0)) for r in rights]
        out_spec = pl.BlockSpec((chunk, width), lambda n: (n, 0))
        turned = pltpu.VMEM((chunk, depth), bf16)
    return call(
        functools.partial(product_kernel, len(lefts), by_columns),
        [shape(height, width, bf16)],
        list(lefts) + list(rights),
        scratch=[turned],
        flops=2 * depth * height * width,
        grid=grid,
        in_specs=left_specs + right_specs,
        out_specs=[out_spec],
    )[0]


def local(
    tokens,
    doc_starts,
    cotangent,
    norm_one,
    w_query,
    b_query,
    w_key,
    b_key,
    w_value,
    b_value,
    w_out,
    norm_two,
    w_gate,
    w_up,
    w_down,
):
    core = lax.axis_index("section")
    cores = lax.axis_size("section")
    spread = lax.axis_size("dp")
    micro_count, _, row_count, width = tokens.shape
    layers = range(2)
    share = row_count // cores
    shard = w_query.shape[1]
    half = shard // 2
    query_width = w_query.shape[2]
    kv_width = w_key.shape[2]
    ff = w_gate.shape[2]
    slice_ff = ff // spread

    def column(vector):
        return jnp.pad(vector, (0, shard - vector.shape[0]))

    vectors = jnp.stack(
        [norm_one[0], norm_two[0], b_query[0], column(b_key[0]), column(b_value[0])], axis=1
    )
    vectors = jnp.pad(vectors, ((0, 0), (0, lanes - vectors.shape[1])))
    attn_own = jnp.concatenate([w_query[0], w_key[0], w_value[0], w_out[0], vectors], axis=1)

    def halves(own):
        middle = own.shape[0] // 2
        low, high = own[:middle], own[middle:]
        got = other(by_section(high, low))
        return by_section(low, got), by_section(got, high)

    def whole(part):
        return both(part, 1).reshape(-1, part.shape[-1])

    def columns_of(part):
        return part.reshape(half, spread, slice_ff).transpose(1, 0, 2)

    wide = -(-slice_ff // lanes) * lanes

    def widen(full, axis):
        pads = [(0, 0), (0, 0)]
        pads[axis] = (0, wide - slice_ff)
        return jnp.pad(full, pads)

    attn_halves = halves(attn_own)
    gate_halves = halves(w_gate[0])
    up_halves = halves(w_up[0])
    attn_full, gate_full, up_full = [], [], []
    for layer in layers:
        part = attn_halves[layer]
        if layer:
            part = after(part, gate_full[layer - 1])
        attn_full.append(whole(reorder(gather_blocks(part, "dp"), "dp")))
        parts = [columns_of(halves_of[layer]) for halves_of in (gate_halves, up_halves)]
        parts = after(jnp.concatenate(parts, axis=1), attn_full[layer])
        parts = exchange(parts, "dp")
        gate_full.append(whole(parts[:, :half]))
        up_full.append(whole(parts[:, half:]))
    down_other = other(w_down[0])
    down_full = [by_section(w_down[0], down_other), by_section(down_other, w_down[0])]

    params = []
    for layer in layers:
        full = attn_full[layer]
        edge = query_width + 2 * kv_width
        small = full[:, edge + width :].astype(f32).reshape(spread, shard, lanes)
        per = kv_width // spread
        bias = jnp.concatenate(
            [
                small[:, :, 2].reshape(-1),
                small[:, :per, 3].reshape(-1),
                small[:, :per, 4].reshape(-1),
            ]
        )
        params.append(
            dict(
                qkv=full[:, :edge],
                out=full[:, edge : edge + width],
                gain_one=small[:, :, 0].reshape(1, -1),
                gain_two=small[:, :, 1].reshape(1, -1),
                bias=bias[None],
                gate=widen(gate_full[layer], 1),
                up=widen(up_full[layer], 1),
                down=widen(down_full[layer], 0),
            )
        )

    first = core * share
    place = lax.axis_index("ctx")
    places = place * row_count + first + jnp.arange(share, dtype=jnp.int32)
    my_tokens = lax.dynamic_slice_in_dim(tokens[:, 0], first, share, 1)
    my_cotangent = lax.dynamic_slice_in_dim(cotangent[:, 0], first, share, 1)
    key_places = jnp.concatenate(
        [
            (place ^ block) * row_count + whose * share + jnp.arange(share, dtype=jnp.int32)
            for whose in (core, 1 - core)
            for block in range(lax.axis_size("ctx"))
        ]
    )

    context = []
    for micro in range(micro_count):
        begins, cos_table, sin_table = tables(doc_starts[micro, 0], places)
        visible = (key_places[:, None] <= places[None, :]) & (
            key_places[:, None] >= begins[None, :]
        )
        context.append((jnp.where(visible, 0.0, masked).astype(f32), cos_table, sin_table))

    kept = [[None] * micro_count for _ in layers]
    rows_in = [my_tokens[micro] for micro in range(micro_count)]
    outputs = []
    for layer in layers:
        p = params[layer]
        results = []
        for micro in range(micro_count):
            bias, cos_table, sin_table = context[micro]
            x = rows_in[micro]
            normed, queries, kv = qkv_rows(x, p, cos_table, sin_table, kv_width)
            kva = jnp.concatenate(gather_parts(kv, "ctx"))
            kvb = other(kva)
            attended, residual, mixing = attend(queries, kva, kvb, bias, x, p)
            lower, upper = gather_parts(mixing, "dp")
            part_low, part_up, hidden, gate, up = ffn(lower, upper, p)
            low, got = scatter_parts(part_low, part_up, "dp")
            results.append((residual + low + got.astype(f32)).astype(bf16))
            kept[layer][micro] = dict(
                x=x,
                normed=normed,
                queries=queries,
                kva=kva,
                kvb=kvb,
                attended=attended,
                residual=residual,
                mixing=(lower, upper),
                hidden=hidden,
                gate=gate,
                up=up,
            )
        outputs.append(jnp.stack(results))
        rows_in = results

    section_out = both_rows(outputs)

    upstream = [(my_cotangent[n].astype(f32), my_cotangent[n]) for n in range(micro_count)]
    grads_in = [None, None]
    final = [None, None]
    for layer in reversed(layers):
        p = params[layer]
        results = []
        for micro in range(micro_count):
            bias, cos_table, sin_table = context[micro]
            k = kept[layer][micro]
            above, above_low = upstream[micro]
            k["grad_ffn"] = gather_parts(above_low, "dp")
            part_low, part_up, k["grad_gate"], k["grad_up"] = ffn_back(
                *k["grad_ffn"], k["gate"], k["up"], p
            )
            low, got = scatter_parts(part_low, part_up, "dp")
            dq, dkva, dkvb, grad_residual, k["grad_attended"], k["gain_two"] = attend_back(
                k["queries"],
                k["kva"],
                k["kvb"],
                bias,
                low,
                got,
                k["residual"],
                above,
                p,
                cos_table,
                sin_table,
            )
            pair = dkva.astype(f32) + other(dkvb).astype(f32)
            middle = pair.shape[0] // 2
            low, got = scatter_parts(pair[:middle], pair[middle:], "ctx")
            k["grad_qkv"], grad_in, grad_low, k["gain_one"], k["bias"] = qkv_back(
                dq, low, got, k["x"], grad_residual, p, cos_table, sin_table
            )
            results.append((grad_in, grad_low))
        upstream = results
        grads_in[layer] = jnp.stack([grad_in for grad_in, _ in results])
        parts = weight_grads(kept[layer], spread, shard, kv_width, query_width, width, slice_ff)
        if final[1] is not None:
            parts = after(parts, final[1])
        final[layer] = lax.psum(parts, "ctx")

    section_grad = both_rows(grads_in)

    from_zero = [lax.ppermute(part, "section", [(0, 1)]) for part in final[1]]
    from_one = [lax.ppermute(part, "section", [(1, 0)]) for part in final[0]]
    attn, gate, up, down = [
        jnp.concatenate([by_section(a0, r1), by_section(r0, a1)], axis=0).astype(f32)
        for a0, a1, r0, r1 in zip(final[0], final[1], from_one, from_zero)
    ]
    edge = query_width + 2 * kv_width
    per = kv_width // spread
    small = attn[:, edge + width :]
    return (
        section_out,
        section_grad,
        small[None, :, 0],
        attn[None, :, :query_width],
        small[None, :, 2],
        attn[None, :, query_width : query_width + kv_width],
        small[None, :per, 3],
        attn[None, :, query_width + kv_width : edge],
        small[None, :per, 4],
        attn[None, :, edge : edge + width],
        small[None, :, 1],
        gate[None],
        up[None],
        down[None],
    )


def both_rows(per_layer):
    first, second = per_layer
    got = other(by_section(second, first))
    return by_section(
        jnp.concatenate([first, got], axis=1), jnp.concatenate([got, second], axis=1)
    )[None, :, None]


def weight_grads(kept, spread, shard, kv_width, query_width, width, slice_ff):
    def column_of(name):
        return [k[name] for k in kept]

    def parts_of(name):
        return [part for k in kept for part in k[name]]

    half = shard // 2

    def split(part):
        mine = by_section(part[:, :half], part[:, half:])
        theirs = by_section(part[:, half:], part[:, :half])
        return (mine.astype(f32) + other(theirs).astype(f32)).astype(bf16)

    down = product_over_rows(column_of("hidden"), parts_of("grad_ffn"))[:slice_ff]
    middle = slice_ff // 2
    mine = by_section(down[:middle], down[middle:])
    theirs = by_section(down[middle:], down[:middle])
    down = (mine.astype(f32) + other(theirs).astype(f32)).astype(bf16)

    def columns(name):
        part = product_over_rows(parts_of("mixing"), column_of(name))[:, :slice_ff]
        return split(part.reshape(spread, shard, slice_ff))

    part = exchange(jnp.concatenate([columns("grad_gate"), columns("grad_up")], axis=1), "dp")
    part = part.reshape(spread, 2, half, slice_ff).transpose(1, 2, 0, 3)
    gate, up = part.reshape(2, half, spread * slice_ff)

    qkv = product_over_rows(column_of("normed"), column_of("grad_qkv"))
    out = product_over_rows(column_of("attended"), column_of("grad_attended"))
    bias = sum(column_of("bias"))[0]
    per = kv_width // spread

    def column(vector):
        return jnp.pad(vector.reshape(spread, -1), ((0, 0), (0, shard - per))).reshape(-1)

    vectors = jnp.stack(
        [
            sum(column_of("gain_one"))[0],
            sum(column_of("gain_two"))[0],
            bias[:query_width],
            column(bias[query_width : query_width + kv_width]),
            column(bias[query_width + kv_width :]),
        ],
        axis=1,
    )
    vectors = jnp.pad(vectors, ((0, 0), (0, lanes - vectors.shape[1])))
    attn = jnp.concatenate([qkv, out, vectors.astype(bf16)], axis=1)
    attn = split(attn.reshape(spread, shard, -1))
    attn = reorder(attn, "dp", back=True).reshape(spread * half, -1)
    low, got = scatter_parts(*jnp.split(attn, 2), "dp")
    attn = (low + got.astype(f32)).astype(bf16)
    return attn, gate, up, down


def solution(mesh):
    return jax.shard_map(
        local,
        mesh=mesh,
        in_specs=(
            P(None, "dp", "ctx", None),
            P(None, "dp", None),
            P(None, "dp", "ctx", None),
            P("section", "dp"),
            P("section", "dp", None),
            P("section", "dp"),
            P("section", "dp", None),
            P("section", "dp"),
            P("section", "dp", None),
            P("section", "dp"),
            P("section", "dp", None),
            P("section", "dp"),
            P("section", "dp", None),
            P("section", "dp", None),
            P("section", "dp", None),
        ),
        out_specs=(
            P("section", None, "dp", "ctx", None),
            P("section", None, "dp", "ctx", None),
            P("section", "dp"),
            P("section", "dp", None),
            P("section", "dp"),
            P("section", "dp", None),
            P("section", "dp"),
            P("section", "dp", None),
            P("section", "dp"),
            P("section", "dp", None),
            P("section", "dp"),
            P("section", "dp", None),
            P("section", "dp", None),
            P("section", "dp", None),
        ),
        check_vma=False,
    )
```

```python
import functools

import jax
import jax.numpy as jnp
from jax import lax
from jax.experimental import pallas as pl
from jax.experimental.pallas import tpu as pltpu
from jax.sharding import PartitionSpec as P

HEAD = 64
rope_base = 1000000.0
norm_eps = 1e-06
masked = -1e30
bf16 = jnp.bfloat16
f32 = jnp.float32


def matmul(left, right):
    return jnp.dot(left, right, preferred_element_type=f32)


def matmul_nt(left, right):
    return lax.dot_general(left, right, (((1,), (1,)), ((), ())), preferred_element_type=f32)


def inverse_rms(values):
    return lax.rsqrt(jnp.mean(values * values, axis=-1, keepdims=True) + norm_eps)


def step_masks(axis):
    size = lax.axis_size(axis)
    assert size & (size - 1) == 0
    ahead = [1 << n for n in range(size.bit_length() - 1)]
    return list(zip(ahead, ahead[::-1] if axis == "dp" else ahead))


def step(block, axis, masks):
    size = lax.axis_size(axis)
    route = [
        (core * size + i, core * size + (i ^ mask))
        for core, mask in enumerate(masks)
        for i in range(size)
    ]
    return lax.ppermute(block, ("section", axis), route)


def gather_steps(rows, axis, give):
    masks = step_masks(axis)
    for pair in masks:
        got = step(rows, axis, pair)
        yield got
        if pair is not masks[-1]:
            rows = jnp.concatenate([rows, got])
    give(rows, got)


def scatter_steps(lower, upper, axis, give):
    masks = step_masks(axis)
    for pair in masks[::-1]:
        got = step(upper.astype(bf16), axis, pair)
        yield got
        if pair is not masks[0]:
            total = lower.astype(f32) + got.astype(f32)
            half = total.shape[0] // 2
            lower, upper = total[:half], total[half:]
    give(lower.astype(f32), got)


def distance(block, axis, core):
    return sum(pair[core] for n, pair in enumerate(step_masks(axis)) if block & (1 << n))


def direct(block, axis, mask):
    size = lax.axis_size(axis)
    return lax.ppermute(block, axis, [(i, i ^ mask) for i in range(size)])


def other(block):
    return lax.ppermute(block, "section", [(0, 1), (1, 0)])


def by_section(first, second):
    return jnp.where(lax.axis_index("section") == 0, first, second)


def after(value, first):
    return lax.optimization_barrier((value, first))[0]


def tables(begins, places):
    lane = jnp.arange(lanes, dtype=jnp.int32) % HEAD
    frequency = rope_base ** (-2.0 * (lane % (HEAD // 2)).astype(f32) / HEAD)
    angles = (places - begins).astype(f32)[:, None] * frequency[None, :]
    signs = jnp.where(lane < HEAD // 2, -1.0, 1.0)
    return jnp.cos(angles), jnp.sin(angles) * signs[None, :]


megabyte = 1024 * 1024
lanes = 128


class Part:
    def __init__(self, array, dim, index):
        self.array, self.dim, self.index = array, dim, index

    def spec(self):
        block = list(self.array.shape)
        block[self.dim] = None
        at = [0] * len(block)
        at[self.dim] = self.index
        return pl.BlockSpec(tuple(block), lambda *_: tuple(at))

    @property
    def shape(self):
        return self.array.shape[: self.dim] + self.array.shape[self.dim + 1 :]

    @property
    def size(self):
        return self.array.size // self.array.shape[self.dim]

    @property
    def dtype(self):
        return self.array.dtype


def call(
    kernel, outs, args, scratch=(), flops=0, grid=None, in_specs=None, out_specs=None, vmem=4
):
    moved = sum(a.size * a.dtype.itemsize for a in args)
    moved += sum(o.size * o.dtype.itemsize for o in outs)
    whole = pl.BlockSpec(memory_space=pltpu.VMEM)
    scalars = pl.BlockSpec(memory_space=pltpu.SMEM)
    specs = []
    for n, arg in enumerate(args):
        if isinstance(arg, Part):
            specs.append(arg.spec())
            grid = grid or (1,)
        elif arg.dtype == jnp.int32:
            specs.append(scalars)
        else:
            specs.append(in_specs[n] if in_specs else whole)
    return pl.pallas_call(
        kernel,
        out_shape=outs,
        grid=grid or (),
        in_specs=specs,
        out_specs=out_specs or [whole] * len(outs),
        scratch_shapes=scratch,
        cost_estimate=pl.CostEstimate(
            flops=int(flops), bytes_accessed=int(moved), transcendentals=0
        ),
        compiler_params=pltpu.CompilerParams(
            vmem_limit_bytes=min(56, vmem * lax.axis_size("dp")) * megabyte
        ),
    )(*[arg.array if isinstance(arg, Part) else arg for arg in args])


def shape(*dims):
    return jax.ShapeDtypeStruct(dims[:-1], dims[-1])


def lane_of(block):
    return lax.broadcasted_iota(jnp.int32, block.shape, 1)


def turn(block, cos_table, sin_table):
    quarter = HEAD // 2
    first = lax.rem(lane_of(block), HEAD) < quarter
    turned = jnp.where(first, pltpu.roll(block, lanes - quarter, 1), pltpu.roll(block, quarter, 1))
    return block * cos_table + turned * sin_table


def qkv_kernel(x_ref, gain_ref, w_ref, bias_ref, cos_ref, sin_ref, normed_ref, q_ref, kv_ref):
    x = x_ref[...].astype(f32)
    normed = (x * inverse_rms(x) * gain_ref[...].astype(f32)).astype(bf16)
    normed_ref[...] = normed
    cos_table, sin_table = cos_ref[...], sin_ref[...]
    rows = matmul(normed, w_ref[...]) + bias_ref[...].astype(f32)
    query_width = q_ref.shape[1]
    key_end = query_width + kv_ref.shape[1] // 2
    for start in range(0, rows.shape[1], lanes):
        block = rows[:, start : start + lanes]
        if start < key_end:
            block = turn(block, cos_table, sin_table)
        if start < query_width:
            q_ref[:, start : start + lanes] = block.astype(bf16)
        else:
            kv_ref[:, start - query_width : start - query_width + lanes] = block.astype(bf16)


def qkv_rows(x, p, cos_table, sin_table, kv_width):
    rows, width = x.shape
    total = p["qkv"].shape[1]
    query_width = total - 2 * kv_width
    return call(
        qkv_kernel,
        [shape(rows, width, bf16), shape(rows, query_width, bf16), shape(rows, 2 * kv_width, bf16)],
        [x, p["gain_one"], p["qkv"], p["bias"], cos_table, sin_table],
        flops=2 * rows * width * total,
    )


def pair_rows(block, pair, group):
    swapped = pltpu.roll(block, HEAD, 1)
    low = lane_of(block) < HEAD
    rows = []
    for side in range(2):
        key_head = (2 * pair + side) // group
        here = block if key_head == side else swapped
        rows.append(jnp.where(low == (key_head == 0), here, 0.0))
    return jnp.concatenate(rows).astype(bf16)


def pair_columns(block, pair, group):
    count = block.shape[1] // 2
    parts = []
    for side in range(2):
        start = (2 * pair + side) // group * HEAD
        parts.append(block[start : start + HEAD, side * count : (side + 1) * count])
    return jnp.concatenate(parts).T


def pair_terms(keys, query_pair, bias):
    scores = matmul_nt(keys, query_pair) + jnp.concatenate([bias, bias], axis=1)
    terms = jnp.exp(scores - jnp.max(scores, axis=0, keepdims=True))
    return terms, 1.0 / jnp.sum(terms, axis=0, keepdims=True)


def lay_keys(refs, keys, values):
    count = refs[0].shape[0] * refs[0].shape[1]
    for i, ref in enumerate(refs):
        rows = ref[...].reshape(count, ref.shape[2])
        keys[i * count : (i + 1) * count] = rows[:, :lanes]
        values[i * count : (i + 1) * count] = rows[:, lanes:]


def attend_kernel(
    group,
    q_ref,
    kva_ref,
    kvb_ref,
    bias_ref,
    x_ref,
    wo_ref,
    gain_ref,
    att_ref,
    res_ref,
    mix_ref,
    keys,
    values,
):
    lay_keys((kva_ref, kvb_ref), keys, values)
    values_turned = values[...].T
    bias = bias_ref[...]
    for pair in range(q_ref.shape[1] // lanes):
        place = slice(pair * lanes, (pair + 1) * lanes)
        query_pair = pair_rows(q_ref[:, place].astype(f32) * HEAD**-0.5, pair, group)
        terms, inverse = pair_terms(keys[...], query_pair, bias)
        output = matmul(values_turned, terms.astype(bf16)) * inverse
        att_ref[:, place] = pair_columns(output, pair, group).astype(bf16)

    residual = x_ref[...].astype(f32) + matmul(att_ref[...], wo_ref[...])
    res_ref[...] = residual
    mix_ref[...] = (residual * inverse_rms(residual) * gain_ref[...].astype(f32)).astype(bf16)


def attend(queries, kva, kvb, bias, x, p, turn_of):
    rows, width = queries.shape
    total = bias.shape[0]
    kv_width = kva.shape[-1] // 2
    group = width // kv_width
    flops = 4 * rows * total * width * 4 + 2 * rows * width * x.shape[1]
    return call(
        functools.partial(attend_kernel, group),
        [shape(rows, width, bf16), shape(*x.shape, f32), shape(*x.shape, bf16)],
        [queries, kva, kvb, bias, x, p["out"], turn_of(p["gain_two"])],
        scratch=[pltpu.VMEM((total, lanes), bf16)] * 2,
        flops=flops,
    )


def norm_back(values, gain, grad):
    inverse = inverse_rms(values)
    unit = values * inverse
    scaled = grad * gain
    back = inverse * (scaled - unit * jnp.mean(scaled * unit, axis=-1, keepdims=True))
    return back, jnp.sum(grad * unit, axis=0, keepdims=True)


def attend_back_kernel(
    group,
    q_ref,
    kva_ref,
    kvb_ref,
    bias_ref,
    mix_low_ref,
    mix_got_ref,
    res_ref,
    gain_ref,
    up_ref,
    wo_ref,
    cos_ref,
    sin_ref,
    dq_ref,
    dkva_ref,
    dkvb_ref,
    gres_ref,
    gatt_ref,
    gain_two_ref,
    keys,
    values,
    queries,
    grads,
    all_probs,
    all_scores,
):
    lay_keys((kva_ref, kvb_ref), keys, values)
    grad_mixing = mix_low_ref[...] + mix_got_ref[...].astype(f32)
    back, gain_two = norm_back(res_ref[...], gain_ref[...].astype(f32), grad_mixing)
    gain_two_ref[...] = gain_two
    grad_residual = up_ref[...].astype(f32) + back
    gres_ref[...] = grad_residual
    grad_attended = grad_residual.astype(bf16)
    gatt_ref[...] = grad_attended
    grad_out = matmul_nt(grad_attended, wo_ref[...]).astype(bf16).astype(f32)
    bias = bias_ref[...]
    pairs = q_ref.shape[1] // lanes
    both = 2 * q_ref.shape[0]
    for pair in range(pairs):
        place = slice(pair * lanes, (pair + 1) * lanes)
        rows = slice(pair * both, (pair + 1) * both)
        query_pair = pair_rows(q_ref[:, place].astype(f32) * HEAD**-0.5, pair, group)
        grad_pair = pair_rows(grad_out[:, place], pair, group)
        queries[rows] = query_pair
        grads[rows] = grad_pair
        terms, inverse = pair_terms(keys[...], query_pair, bias)
        probs = terms * inverse
        all_probs[:, rows] = probs.astype(bf16)
        grad_probs = matmul_nt(values[...], grad_pair)
        delta = jnp.sum(probs * grad_probs, axis=0, keepdims=True)
        all_scores[:, rows] = (probs * (grad_probs - delta)).astype(bf16)

    grad_values = matmul(all_probs[...], grads[...]).astype(bf16)
    grad_keys = matmul(all_scores[...], queries[...]).astype(bf16)
    count = dkva_ref.shape[0]
    for i, ref in enumerate((dkva_ref, dkvb_ref)):
        ref[:, :lanes] = grad_keys[i * count : (i + 1) * count]
        ref[:, lanes:] = grad_values[i * count : (i + 1) * count]
    keys_turned = keys[...].T
    cos_table, sin_table = cos_ref[...], -sin_ref[...]
    for pair in range(pairs):
        place = slice(pair * lanes, (pair + 1) * lanes)
        turned = matmul(keys_turned, all_scores[:, pair * both : (pair + 1) * both])
        grad_query = pair_columns(turned, pair, group) * HEAD**-0.5
        dq_ref[:, place] = turn(grad_query, cos_table, sin_table).astype(bf16)


def attend_back(
    queries, kva, kvb, bias, mix_low, mix_got, residual, upstream, p, cos_table, sin_table
):
    rows, width = queries.shape
    total = bias.shape[0]
    kv_width = kva.shape[-1] // 2
    group = width // kv_width
    flops = 10 * rows * total * width * 3 + 2 * rows * width * residual.shape[1]
    return call(
        functools.partial(attend_back_kernel, group),
        [
            shape(rows, width, bf16),
            shape(total // 2, 2 * kv_width, bf16),
            shape(total // 2, 2 * kv_width, bf16),
            shape(*residual.shape, f32),
            shape(*residual.shape, bf16),
            shape(1, residual.shape[1], f32),
        ],
        [
            queries,
            kva,
            kvb,
            bias,
            mix_low,
            mix_got,
            residual,
            p["gain_two"],
            upstream,
            p["out"],
            cos_table,
            sin_table,
        ],
        scratch=[
            pltpu.VMEM((total, lanes), bf16),
            pltpu.VMEM((total, lanes), bf16),
            pltpu.VMEM((rows * width // HEAD, lanes), bf16),
            pltpu.VMEM((rows * width // HEAD, lanes), bf16),
            pltpu.VMEM((total, rows * width // HEAD), bf16),
            pltpu.VMEM((total, rows * width // HEAD), bf16),
        ],
        flops=flops,
        vmem=6,
    )


def qkv_back_kernel(
    dq_ref,
    low_ref,
    got_ref,
    cos_ref,
    sin_ref,
    w_ref,
    x_ref,
    gain_ref,
    gres_ref,
    dqkv_ref,
    gin_ref,
    gin_low_ref,
    gain_one_ref,
    bias_ref,
):
    query_width = dq_ref.shape[1]
    grad_kv = low_ref[...] + got_ref[...].astype(f32)
    dqkv_ref[:, :query_width] = dq_ref[...]
    grad_key = turn(grad_kv[:, :lanes], cos_ref[...], -sin_ref[...])
    dqkv_ref[:, query_width : query_width + lanes] = grad_key.astype(bf16)
    dqkv_ref[:, query_width + lanes :] = grad_kv[:, lanes:].astype(bf16)
    dqkv = dqkv_ref[...]
    bias_ref[...] = jnp.sum(dqkv.astype(f32), axis=0, keepdims=True)
    grad_normed = matmul_nt(dqkv, w_ref[...])
    back, gain_one = norm_back(x_ref[...].astype(f32), gain_ref[...].astype(f32), grad_normed)
    gain_one_ref[...] = gain_one
    grad_in = gres_ref[...] + back
    gin_ref[...] = grad_in
    gin_low_ref[...] = grad_in.astype(bf16)


def qkv_back(dq, low, got, x, grad_residual, p, cos_table, sin_table):
    rows, width = x.shape
    total = p["qkv"].shape[1]
    return call(
        qkv_back_kernel,
        [
            shape(rows, total, bf16),
            shape(rows, width, f32),
            shape(rows, width, bf16),
            shape(1, width, f32),
            shape(1, total, f32),
        ],
        [dq, low, got, cos_table, sin_table, p["qkv"], x, p["gain_one"], grad_residual],
        flops=2 * rows * width * total,
    )


def chunk_of(size):
    return 256 if size % 256 == 0 else 128


def ffn_kernel(lower_ref, upper_ref, wg_ref, wu_ref, wd_ref, low_ref, up_ref, hid_ref, g_ref, u_ref, rows, total):
    n = pl.program_id(0)
    half = rows.shape[0] // 2

    @pl.when(n == 0)
    def _():
        rows[:half] = lower_ref[...].reshape(half, rows.shape[1])
        rows[half:] = upper_ref[...].reshape(half, rows.shape[1])
        total[...] = jnp.zeros_like(total)

    gate = matmul(rows[...], wg_ref[...])
    up = matmul(rows[...], wu_ref[...])
    hidden = (gate * (1.0 / (1.0 + jnp.exp(-gate))) * up).astype(bf16)
    hid_ref[...] = hidden
    g_ref[...] = gate.astype(bf16)
    u_ref[...] = up.astype(bf16)
    total[...] += matmul(hidden, wd_ref[...])

    @pl.when(n == pl.num_programs(0) - 1)
    def _():
        low_ref[...] = total[:half].astype(bf16)
        up_ref[...] = total[half:].astype(bf16)


def ffn(lower, upper, p):
    half, width = lower.shape
    wide = p["gate"].shape[1]
    chunk = chunk_of(wide)
    rows = half + upper.shape[0]
    whole = pl.BlockSpec((half, width), lambda n: (0, 0))
    columns = pl.BlockSpec((width, chunk), lambda n: (0, n))
    return call(
        ffn_kernel,
        [shape(half, width, bf16), shape(rows - half, width, bf16)] + [shape(rows, wide, bf16)] * 3,
        [lower, upper, p["gate"], p["up"], p["down"]],
        scratch=[pltpu.VMEM((rows, width), bf16), pltpu.VMEM((rows, width), f32)],
        flops=6 * rows * width * wide,
        grid=(wide // chunk,),
        in_specs=[whole, whole, columns, columns, pl.BlockSpec((chunk, width), lambda n: (n, 0))],
        out_specs=[whole, whole] + [pl.BlockSpec((rows, chunk), lambda n: (0, n))] * 3,
    )


def ffn_back_kernel(
    lower_ref, upper_ref, g_ref, u_ref, wg_ref, wu_ref, wd_ref, low_ref, up_ref, gg_ref, gu_ref, rows, total
):
    n = pl.program_id(0)
    half = rows.shape[0] // 2

    @pl.when(n == 0)
    def _():
        rows[:half] = lower_ref[...].reshape(half, rows.shape[1])
        rows[half:] = upper_ref[...].reshape(half, rows.shape[1])
        total[...] = jnp.zeros_like(total)

    grad_hidden = matmul_nt(rows[...], wd_ref[...])
    gate = g_ref[...].astype(f32)
    up = u_ref[...].astype(f32)
    sigmoid = 1.0 / (1.0 + jnp.exp(-gate))
    grad_up = (grad_hidden * gate * sigmoid).astype(bf16)
    grad_gate = (grad_hidden * up * sigmoid * (1.0 + gate * (1.0 - sigmoid))).astype(bf16)
    gg_ref[...] = grad_gate
    gu_ref[...] = grad_up
    total[...] += matmul_nt(grad_gate, wg_ref[...]) + matmul_nt(grad_up, wu_ref[...])

    @pl.when(n == pl.num_programs(0) - 1)
    def _():
        low_ref[...] = total[:half].astype(bf16)
        up_ref[...] = total[half:].astype(bf16)


def ffn_back(lower, upper, gate, up, p):
    half, width = gate.shape[0] // 2, lower.shape[-1]
    wide = p["gate"].shape[1]
    chunk = chunk_of(wide)
    rows = 2 * half
    whole = pl.BlockSpec((half, width), lambda n: (0, 0))
    columns = pl.BlockSpec((width, chunk), lambda n: (0, n))
    inner = pl.BlockSpec((rows, chunk), lambda n: (0, n))
    return call(
        ffn_back_kernel,
        [shape(half, width, bf16), shape(rows - half, width, bf16)] + [shape(rows, wide, bf16)] * 2,
        [lower, upper, gate, up, p["gate"], p["up"], p["down"]],
        scratch=[pltpu.VMEM((rows, width), bf16), pltpu.VMEM((rows, width), f32)],
        flops=6 * rows * width * wide,
        grid=(wide // chunk,),
        in_specs=[
            whole,
            whole,
            inner,
            inner,
            columns,
            columns,
            pl.BlockSpec((chunk, width), lambda n: (n, 0)),
        ],
        out_specs=[whole, whole, inner, inner],
    )


def rows_of(ref):
    return ref[...].reshape(-1, ref.shape[-1])


def turn_rows(refs, turned):
    start = 0
    for ref in refs:
        turned[:, start : start + ref.shape[0]] = ref[...].T
        start += ref.shape[0]


def stack_rows(refs):
    return jnp.concatenate([rows_of(ref) for ref in refs])


def split_halves(info_ref, spread, result, keep_at, send_at):
    half = result.shape[0] // (2 * spread)
    for core in range(2):

        @pl.when(info_ref[0] == core)
        def _(core=core):
            for j in range(spread):
                for ref_at, whose in ((keep_at, core), (send_at, 1 - core)):
                    start = (2 * j + whose) * half
                    ref_at(j, result[start : start + half].astype(bf16))


def gate_up_product_kernel(lefts, spread, info_ref, *refs):
    left_refs, refs = refs[:lefts], refs[lefts:]
    keep_ref, send_ref, turned = refs[-3:]
    rights = refs[:-3]
    turn_rows(left_refs, turned)
    me = info_ref[1]
    count = len(rights) // 2
    for n in range(2):
        right = stack_rows(rights[n * count : (n + 1) * count])
        width = right.shape[1]
        for start in range(0, width, 512):
            place = slice(start, min(start + 512, width))
            result = matmul(turned[...], right[:, place])

            def keep_at(j, block, n=n, place=place):
                keep_ref[j ^ me, n, :, place] = block

            def send_at(j, block, n=n, place=place):
                send_ref[j ^ me, n, :, place] = block

            split_halves(info_ref, spread, result, keep_at, send_at)


def gate_up_product(info, lefts, gates, ups, spread):
    depth = sum(left.size // left.shape[-1] for left in lefts)
    height, width = lefts[0].shape[-1], gates[0].shape[1]
    out = shape(spread, 2, height // (2 * spread), width, bf16)
    return call(
        functools.partial(gate_up_product_kernel, len(lefts), spread),
        [out, out],
        [info] + list(lefts) + list(gates) + list(ups),
        scratch=[pltpu.VMEM((height, depth), bf16)],
        flops=4 * depth * height * width,
        vmem=8,
    )


def down_product_kernel(lefts, info_ref, *refs):
    left_refs, rights = refs[:lefts], refs[lefts:-3]
    keep_ref, send_ref, turned = refs[-3:]
    turn_rows(left_refs, turned)
    middle = keep_ref.shape[0]
    result = matmul(turned[: 2 * middle], stack_rows(rights))
    for core in range(2):

        @pl.when(info_ref[0] == core)
        def _(core=core):
            keep_ref[...] = result[core * middle : (core + 1) * middle].astype(bf16)
            send_ref[...] = result[(1 - core) * middle : (2 - core) * middle].astype(bf16)


def down_product(info, lefts, rights, rows):
    depth = sum(left.size // left.shape[-1] for left in lefts)
    height, width = lefts[0].shape[-1], rights[0].shape[-1]
    return call(
        functools.partial(down_product_kernel, len(lefts)),
        [shape(rows // 2, width, bf16)] * 2,
        [info] + list(lefts) + list(rights),
        scratch=[pltpu.VMEM((height, depth), bf16)],
        flops=2 * depth * height * width,
    )


def attn_product_kernel(count, spread, info_ref, *refs):
    normed, grad_qkv, attended, grad_attended = [
        refs[n * count : (n + 1) * count] for n in range(4)
    ]
    vector_ref, keep_ref, send_ref, turned = refs[4 * count :]
    start = 0
    for lefts, rights in ((normed, grad_qkv), (attended, grad_attended), (None, None)):
        if lefts:
            turn_rows(lefts, turned)
            result = matmul(turned[...], stack_rows(rights))
        else:
            rows = vector_ref[...]
            fill = jnp.zeros((lanes - rows.shape[0], rows.shape[1]), f32)
            result = jnp.concatenate([rows, fill]).T
        place = slice(start, start + result.shape[1])
        start += result.shape[1]

        def keep_at(j, block, place=place):
            keep_ref[info_ref[2 + j], :, place] = block

        def send_at(j, block, place=place):
            send_ref[info_ref[2 + spread + j], :, place] = block

        split_halves(info_ref, spread, result, keep_at, send_at)


def attn_product(info, normed, grad_qkv, attended, grad_attended, vectors, spread):
    depth = sum(part.shape[0] for part in normed)
    width = normed[0].shape[1]
    total = grad_qkv[0].shape[1] + grad_attended[0].shape[1] + lanes
    out = shape(spread, width // (2 * spread), total, bf16)
    return call(
        functools.partial(attn_product_kernel, len(normed), spread),
        [out, out],
        [info] + list(normed) + list(grad_qkv) + list(attended) + list(grad_attended) + [vectors],
        scratch=[pltpu.VMEM((width, depth), bf16)],
        flops=2 * depth * width * total,
    )


def pack_attn_kernel(info_ref, *refs):
    keep_ref, send_ref = refs[-2:]
    half = keep_ref.shape[0]
    for core in range(2):

        @pl.when(info_ref[0] == core)
        def _(core=core):
            start = 0
            for ref in refs[:-2]:
                place = slice(start, start + ref.shape[1])
                start += ref.shape[1]
                keep_ref[:, place] = ref[core * half : (core + 1) * half]
                send_ref[:, place] = ref[(1 - core) * half : (2 - core) * half]


def pack_attn(info, parts):
    out = shape(parts[0].shape[0] // 2, sum(part.shape[1] for part in parts), bf16)
    return call(pack_attn_kernel, [out, out], [info] + parts)


def pack_gate_up_kernel(spread, info_ref, gate_ref, up_ref, keep_ref, send_ref):
    me = info_ref[1]
    half, columns = keep_ref.shape[2:]
    for core in range(2):

        @pl.when(info_ref[0] == core)
        def _(core=core):
            for n, ref in enumerate((gate_ref, up_ref)):
                for j in range(spread):
                    block = ref[:, j * columns : (j + 1) * columns]
                    keep_ref[j ^ me, n] = block[core * half : (core + 1) * half]
                    send_ref[j ^ me, n] = block[(1 - core) * half : (2 - core) * half]


def pack_gate_up(info, gate, up, spread):
    out = shape(spread, 2, gate.shape[0] // 2, gate.shape[1] // spread, bf16)
    return call(
        functools.partial(pack_gate_up_kernel, spread), [out, out], [info, gate, up]
    )


def lay_attn_kernel(edges, at_ref, *refs):
    parts, outs = refs[:4], refs[4:]
    half = outs[0].shape[1]
    n = 0
    for ref in parts:
        for start in range(0, ref.shape[0], half):
            block = ref[start : start + half]
            for out, (low, high) in zip(outs, edges):
                out[at_ref[n]] = block[:, low:high]
            n += 1


def lay_attn(at, parts, half, edges):
    count = at.shape[0]
    outs = [shape(count, half, high - low, bf16) for low, high in edges]
    got = call(functools.partial(lay_attn_kernel, edges), outs, [at] + parts)
    return [part.reshape(count * half, -1) for part in got]


def lay_gate_up_kernel(at_ref, *refs):
    parts, outs = refs[:-2], refs[-2:]
    for i, ref in enumerate(parts):
        for n, out in enumerate(outs):
            columns = ref.shape[2]
            out[at_ref[i], :, :columns] = ref[n]
            if columns < out.shape[2]:
                rest = (out.shape[1], out.shape[2] - columns)
                out[at_ref[i], :, columns:] = jnp.zeros(rest, bf16)


def lay_gate_up(at, parts, wide):
    half = parts[0].shape[1]
    outs = [shape(len(parts), half, wide, bf16)] * 2
    got = call(lay_gate_up_kernel, outs, [at] + parts)
    return [part.reshape(len(parts) * half, wide) for part in got]


def spread_kernel(spread, info_ref, *refs):
    gate_ref, up_ref = refs[-2:]
    count = (len(refs) - 2) // 2
    per = spread // count
    me = info_ref[1]
    half = refs[0].shape[2]
    columns = gate_ref.shape[1] // spread
    for core in range(2):

        @pl.when(info_ref[0] == core)
        def _(core=core):
            for i in range(spread):
                for parts, whose in ((refs[:count], core), (refs[count:-2], 1 - core)):
                    for n, out in enumerate((gate_ref, up_ref)):
                        block = parts[i // per][i % per, n][:, :columns].astype(f32)
                        for j in range(spread):

                            @pl.when((i ^ me) == j)
                            def _(j=j, block=block, whose=whose, out=out):
                                place = slice(j * columns, (j + 1) * columns)
                                out[whose * half : (whose + 1) * half, place] = block


def spread_gate_up(info, mine, theirs, columns, spread):
    half = mine[0].shape[2]
    out = shape(2 * half, spread * columns, f32)
    return call(
        functools.partial(spread_kernel, spread), [out, out], [info] + list(mine) + list(theirs)
    )


def local(
    tokens,
    doc_starts,
    cotangent,
    norm_one,
    w_query,
    b_query,
    w_key,
    b_key,
    w_value,
    b_value,
    w_out,
    norm_two,
    w_gate,
    w_up,
    w_down,
):
    core = lax.axis_index("section")
    cores = lax.axis_size("section")
    spread = lax.axis_size("dp")
    micro_count, _, row_count, width = tokens.shape
    layers = range(2)
    share = row_count // cores
    shard = w_query.shape[1]
    half = shard // 2
    query_width = w_query.shape[2]
    kv_width = w_key.shape[2]
    ff = w_gate.shape[2]
    slice_ff = ff // spread

    me = lax.axis_index("dp")
    wide = -(-slice_ff // lanes) * lanes
    edge = query_width + 2 * kv_width
    per = kv_width // spread

    def order_of(mine):
        masks = step_masks("dp")

        def place(j, core):
            return sum(
                jnp.where(((me ^ j) & pair[core]) != 0, 1 << n, 0) for n, pair in enumerate(masks)
            )

        first, second = (0, 1) if mine else (1, 0)
        return [by_section(place(j, first), place(j, second)) for j in range(spread)]

    def owner(block, mine):
        first, second = (0, 1) if mine else (1, 0)
        masks = [distance(block, "dp", first), distance(block, "dp", second)]
        return me ^ by_section(*masks)

    info = jnp.stack([core, me] + order_of(True) + order_of(False)).astype(jnp.int32)
    attn_at = jnp.stack(
        [
            2 * owner(block, mine) + (core if mine else 1 - core)
            for mine in (True, False)
            for block in range(spread)
        ]
    ).astype(jnp.int32)
    gate_up_at = jnp.stack(
        [2 * (me ^ mask) + whose for whose in (core, 1 - core) for mask in range(spread)]
    ).astype(jnp.int32)

    def column(vector):
        return jnp.pad(vector, (0, shard - vector.shape[0]))

    vectors = jnp.stack(
        [norm_one[0], norm_two[0], b_query[0], column(b_key[0]), column(b_value[0])], axis=1
    )
    vectors = jnp.pad(vectors, ((0, 0), (0, lanes - vectors.shape[1])))

    def per_layer(keep, send):
        got = other(send)
        return by_section(keep, got), by_section(got, keep)

    attn_halves = per_layer(
        *pack_attn(info, [w_query[0], w_key[0], w_value[0], w_out[0], vectors])
    )
    gate_up_halves = per_layer(*pack_gate_up(info, w_gate[0], w_up[0], spread))
    down_other = other(w_down[0])
    downs = by_section(w_down[0], down_other), by_section(down_other, w_down[0])

    params = [{}, {}]
    clock, flows, last, pins = [0], [], [], []

    class Flow:
        def __init__(self, steps, slack):
            self.steps, self.slack = steps, slack
            self.move()
            flows.append(self)

        def move(self):
            self.value = next(self.steps, None)
            self.due = clock[0] + self.slack

        def finish(self):
            while self.value is not None:
                self.move()

    def turn_of(value):
        clock[0] += 1
        for flow in list(flows):
            if flow.value is not None and flow.due <= clock[0]:
                pins.append(flow.value)
                flow.move()
            if flow.value is None:
                flows.remove(flow)
        wait = last + pins
        pins.clear()
        return after(value, wait) if wait else value

    def done(value):
        last[:] = [value]

    def weights_steps(layer, part, blocks):
        p = params[layer]
        parts = []
        yield from gather_steps(part, "dp", lambda *got: parts.extend(got))
        blocks = after(blocks, parts[1])
        qkv, out, small = lay_attn(
            attn_at,
            parts + [other(part) for part in parts],
            half,
            ((0, edge), (edge, edge + width), (edge + width, edge + width + lanes)),
        )
        rows = small.T
        p["qkv"], p["out"] = qkv, out
        p["gain_one"], p["gain_two"] = rows[0:1], rows[1:2]
        key_bias, value_bias = [
            rows[n].reshape(spread, shard)[:, :per].reshape(1, -1) for n in (3, 4)
        ]
        p["bias"] = jnp.concatenate([rows[2:3], key_bias, value_bias], axis=1)
        blocks = [blocks[0]] + [direct(blocks[mask], "dp", mask) for mask in range(1, spread)]
        yield blocks
        p["gate"], p["up"] = lay_gate_up(
            gate_up_at, blocks + [other(block) for block in blocks], wide
        )
        p["down"] = jnp.pad(downs[layer], ((0, wide - slice_ff), (0, 0)))

    first = core * share
    place = lax.axis_index("ctx")
    places = place * row_count + first + jnp.arange(share, dtype=jnp.int32)
    my_tokens = lax.dynamic_slice_in_dim(tokens[:, 0], first, share, 1)
    my_cotangent = lax.dynamic_slice_in_dim(cotangent[:, 0], first, share, 1)
    key_places = jnp.concatenate(
        [
            (place ^ block) * row_count + whose * share + jnp.arange(share, dtype=jnp.int32)
            for whose in (core, 1 - core)
            for block in range(lax.axis_size("ctx"))
        ]
    )
    starts = doc_starts[:, 0, None, :]
    begins = jnp.max(jnp.where(starts <= places[None, :, None], starts, 0), axis=2)
    places_all = jnp.tile(places, micro_count)
    cos_all, sin_all = tables(begins.reshape(-1), places_all)
    visible = (key_places[None, :, None] <= places[None, None, :]) & (
        key_places[None, :, None] >= begins[:, None, :]
    )
    bias_all = jnp.where(visible, 0.0, masked).astype(f32)
    context = [
        (
            Part(bias_all, 0, n),
            Part(cos_all.reshape(micro_count, share, lanes), 0, n),
            Part(sin_all.reshape(micro_count, share, lanes), 0, n),
        )
        for n in range(micro_count)
    ]

    kept = [[{} for _ in range(micro_count)] for _ in layers]
    for n in range(micro_count):
        kept[1][n]["above"] = Part(my_cotangent, 0, n)
    def kv_steps(ks, kv):
        def give(*parts):
            whole = jnp.concatenate(parts)
            theirs = other(whole)
            for n, k in enumerate(ks):
                k["kva"], k["kvb"] = [
                    Part(part.reshape(-1, len(ks), share, 2 * kv_width), 1, n)
                    for part in (whole, theirs)
                ]

        yield from gather_steps(kv[None], "ctx", give)

    def run_q_all():
        flow = Flow(weights_steps(0, attn_halves[0], gate_up_halves[0]), weight_slack)
        while "qkv" not in params[0]:
            flow.move()
        kept[0][0]["weights"] = flow
        tokens_in = turn_of(my_tokens.reshape(-1, width))
        rows = qkv_rows(tokens_in, params[0], cos_all, sin_all, kv_width)
        done(rows[0])
        normed, queries = [part.reshape(micro_count, share, -1) for part in rows[:2]]
        for n in range(micro_count):
            k = kept[0][n]
            k["x"], k["normed"], k["queries"] = [
                Part(part, 0, n) for part in (my_tokens, normed, queries)
            ]
        flow = Flow(kv_steps(kept[0], rows[2]), 1)
        for n in range(micro_count):
            kept[0][n]["kv"] = flow
        part, blocks = after((attn_halves[1], gate_up_halves[1]), kept[0][0]["weights"].value)
        kept[1][0]["weights"] = Flow(weights_steps(1, part, blocks), 2)

    def run_q(n):
        k = kept[1][n]
        kept[0][n]["scatter"].finish()
        while "qkv" not in params[1]:
            kept[1][0]["weights"].move()
        k["x"] = turn_of(kept[0][n]["result"])
        k["normed"], k["queries"], kv = qkv_rows(k["x"], params[1], *context[n][1:], kv_width)
        done(k["normed"])
        k["kv"] = Flow(kv_steps([k], kv), 2)

    def run_a(layer, n):
        k, p = kept[layer][n], params[layer]
        k["kv"].finish()
        k["attended"], k["residual"], mixing = attend(
            k["queries"], k["kva"], k["kvb"], context[n][0], k["x"], p, turn_of
        )
        done(mixing)
        k["gather"] = Flow(gather_steps(mixing, "dp", lambda *got: k.update(mixing=got)), 2)

    def run_f(layer, n):
        k, p = kept[layer][n], params[layer]
        k["gather"].finish()
        kept[layer][0]["weights"].finish()
        lower, upper = k["mixing"]
        part_low, part_up, k["hidden"], k["gate"], k["up"] = ffn(lower, turn_of(upper), p)
        done(k["gate"])

        def give(low, got):
            k["result"] = (k["residual"] + low + got.astype(f32)).astype(bf16)

        k["scatter"] = Flow(scatter_steps(part_low, part_up, "dp", give), 2 if layer == 0 else 6)
        if layer:
            k["after"] = k["scatter"]

    def run_c():
        def give(*parts):
            for n in range(micro_count):
                kept[1][n]["grad_ffn"] = [
                    Part(part.reshape(-1, micro_count, share, width), 1, n) for part in parts
                ]

        rows = after(my_cotangent[None], last)
        kept[1][0]["cotangent"] = Flow(gather_steps(rows, "dp", give), 4)

    def run_d(layer, n):
        k, p = kept[layer][n], params[layer]
        if layer:
            kept[1][0]["cotangent"].finish()
        else:
            k["gather"].finish()
        lower, upper = k["grad_ffn"]
        part_low, part_up, k["grad_gate"], k["grad_up"] = ffn_back(
            lower, upper, turn_of(k["gate"]), k["up"], p
        )
        done(k["grad_gate"])
        k["scatter"] = Flow(
            scatter_steps(part_low, part_up, "dp", lambda *got: k.update(scattered=got)), 2
        )

    def run_b(layer, n):
        k, p = kept[layer][n], params[layer]
        k["scatter"].finish()
        bias, cos_table, sin_table = context[n]
        low, got = k["scattered"]
        k["dq"], dkva, dkvb, k["grad_residual"], k["grad_attended"], k["gain_two"] = attend_back(
            k["queries"],
            k["kva"],
            k["kvb"],
            bias,
            low,
            turn_of(got),
            k["residual"],
            k["above"],
            p,
            cos_table,
            sin_table,
        )
        done(k["dq"])
        pair = dkva.astype(f32) + other(dkvb).astype(f32)
        middle = pair.shape[0] // 2
        k["scatter"] = Flow(
            scatter_steps(
                pair[:middle], pair[middle:], "ctx", lambda *got: k.update(grad_kv=got)
            ),
            2,
        )

    def run_k(layer, n):
        k, p = kept[layer][n], params[layer]
        k["scatter"].finish()
        low, got = k["grad_kv"]
        k["grad_qkv"], k["grad_in"], grad_low, k["gain_one"], k["bias"] = qkv_back(
            k["dq"], low, turn_of(got), k["x"], k["grad_residual"], p, *context[n][1:]
        )
        done(k["grad_qkv"])
        if layer:
            below = kept[0][n]
            below["above"] = k["grad_in"]
            below["gather"] = Flow(
                gather_steps(grad_low, "dp", lambda *got: below.update(grad_ffn=got)), 2
            )

    ends = (place == 0) | (place == 3)
    hops = [[(0, 1), (3, 2)], [(1, 2), (2, 1)], [(1, 0), (2, 3)]]
    sums = {}

    def ctx_steps(name, value):
        for hop, route in enumerate(hops):
            got = lax.ppermute(value, "ctx", route)
            yield got
            if hop == 2:
                sums[name] = jnp.where(ends, got, value)
            else:
                value = (value.astype(f32) + got.astype(f32)).astype(bf16)

    waiting, moving, exchanges = {}, [], {}

    def tick(*names):
        for flow in list(moving):
            pins.append(flow.value)
            flow.move()
            if flow.value is None:
                moving.remove(flow)
        for name in names:
            if name not in waiting:
                exchanges.pop(name).finish()
            moving.append(Flow(ctx_steps(name, waiting.pop(name)), 1000))

    def column_of(layer, name):
        return [k[name] for k in kept[layer]]

    def parts_of(layer, name):
        return [part for k in kept[layer] for part in k[name]]

    def over_cores(keep, send):
        return keep.astype(f32) + other(send).astype(f32)

    def run_pd(layer):
        hidden = column_of(layer, "hidden")
        hidden[0] = turn_of(hidden[0])
        keep, send = down_product(info, hidden, parts_of(layer, "grad_ffn"), slice_ff)
        done(keep)
        waiting["down", layer] = over_cores(keep, send).astype(bf16)

    def run_pg(layer):
        grads = column_of(layer, "grad_gate")
        grads[0] = turn_of(grads[0])
        keep, send = gate_up_product(
            info, parts_of(layer, "mixing"), grads, column_of(layer, "grad_up"), spread
        )
        done(keep)
        blocks = over_cores(keep, send).astype(bf16)
        before = kept[layer][micro_count - 1]["scatter"].value

        def steps():
            sent = after(blocks, before) if before is not None else blocks
            parts = [sent[0]] + [direct(sent[mask], "dp", mask) for mask in range(1, spread)]
            yield parts[1:]
            middle = spread // 2
            waiting["low", layer] = jnp.stack(parts[:middle])
            waiting["high", layer] = jnp.stack(parts[middle:])

        exchanges["low", layer] = Flow(steps(), 3)

    def run_pa(layer):
        bias = sum(column_of(layer, "bias"))[0]

        def column_sum(vector):
            return jnp.pad(vector.reshape(spread, -1), ((0, 0), (0, shard - per))).reshape(-1)

        vectors = jnp.stack(
            [
                sum(column_of(layer, "gain_one"))[0],
                sum(column_of(layer, "gain_two"))[0],
                bias[:query_width],
                column_sum(bias[query_width : query_width + kv_width]),
                column_sum(bias[query_width + kv_width :]),
            ]
            + [jnp.zeros((width,), f32)] * 3
        )
        keep, send = attn_product(
            info,
            column_of(layer, "normed"),
            column_of(layer, "grad_qkv"),
            column_of(layer, "attended"),
            column_of(layer, "grad_attended"),
            turn_of(vectors),
            spread,
        )
        done(keep)
        attn = over_cores(keep, send).reshape(spread * half, -1)


        def give(low, got):
            waiting["attn", layer] = (low + got.astype(f32)).astype(bf16)

        exchanges["attn", layer] = Flow(scatter_steps(*jnp.split(attn, 2), "dp", give), 2)

    steps = dict(
        q=run_q,
        a=run_a,
        f=run_f,
        c=run_c,
        d=run_d,
        b=run_b,
        k=run_k,
        D=run_pd,
        G=run_pg,
        P=run_pa,
    )
    run_q_all()
    names = dict(d="down", l="low", h="high", a="attn")
    for word in order.split():
        if word[0] == "z":
            tick(*[(names[word[n]], int(word[n + 1])) for n in range(1, len(word), 2)])
        else:
            steps[word[0]](*[int(digit) for digit in word[1:]])
    while moving:
        tick()
    for k in kept[1]:
        if "result" not in k:
            k["after"].finish()

    section_out = both_rows([jnp.stack(column_of(layer, "result")) for layer in layers])
    section_grad = both_rows([jnp.stack(column_of(layer, "grad_in")) for layer in layers])

    final = [[sums[name, layer] for name in ("attn", "low", "high", "down")] for layer in layers]
    mine = [by_section(*pair) for pair in zip(*final)]
    theirs = [other(by_section(*pair[::-1])) for pair in zip(*final)]
    gate, up = spread_gate_up(info, mine[1:3], theirs[1:3], slice_ff, spread)

    def in_order(mine, theirs):
        return by_section(
            jnp.concatenate([mine, theirs]), jnp.concatenate([theirs, mine])
        ).astype(f32)

    attn = in_order(mine[0], theirs[0])
    down = in_order(mine[3], theirs[3])
    small = attn[:, edge + width :]
    return (
        section_out,
        section_grad,
        small[None, :, 0],
        attn[None, :, :query_width],
        small[None, :, 2],
        attn[None, :, query_width : query_width + kv_width],
        small[None, :per, 3],
        attn[None, :, query_width + kv_width : edge],
        small[None, :per, 4],
        attn[None, :, edge : edge + width],
        small[None, :, 1],
        gate[None],
        up[None],
        down[None],
    )


weight_slack = 3
order = (
    "a00 a01 f00 a02 f01 q0 f02 q1 a10 q2 a11 c f10 a12 f11 "
    "d10 f12 d11 b10 d12 D1 G1 b11 zd1 k10 b12 zl1 k11 d00 zh1 k12 d01 z P1 d02 za1 G0 z D0 b00 zl0 b01 zh0 k00 b02 zd0 k01 k02 "
    "P0 za0"
)


def both_rows(per_layer):
    first, second = per_layer
    got = other(by_section(second, first))
    return by_section(
        jnp.concatenate([first, got], axis=1), jnp.concatenate([got, second], axis=1)
    )[None, :, None]


def solution(mesh):
    return jax.shard_map(
        local,
        mesh=mesh,
        in_specs=(
            P(None, "dp", "ctx", None),
            P(None, "dp", None),
            P(None, "dp", "ctx", None),
            P("section", "dp"),
            P("section", "dp", None),
            P("section", "dp"),
            P("section", "dp", None),
            P("section", "dp"),
            P("section", "dp", None),
            P("section", "dp"),
            P("section", "dp", None),
            P("section", "dp"),
            P("section", "dp", None),
            P("section", "dp", None),
            P("section", "dp", None),
        ),
        out_specs=(
            P("section", None, "dp", "ctx", None),
            P("section", None, "dp", "ctx", None),
            P("section", "dp"),
            P("section", "dp", None),
            P("section", "dp"),
            P("section", "dp", None),
            P("section", "dp"),
            P("section", "dp", None),
            P("section", "dp"),
            P("section", "dp", None),
            P("section", "dp"),
            P("section", "dp", None),
            P("section", "dp", None),
            P("section", "dp", None),
        ),
        check_vma=False,
    )
```

```python
import functools

import jax
import jax.numpy as jnp
from jax import lax
from jax.experimental import pallas as pl
from jax.experimental.pallas import tpu as pltpu
from jax.sharding import PartitionSpec as P

HEAD = 64
rope_base = 1000000.0
norm_eps = 1e-06
masked = -1e30
bf16 = jnp.bfloat16
f32 = jnp.float32


def matmul(left, right):
    return jnp.dot(left, right, preferred_element_type=f32)


def matmul_nt(left, right):
    return lax.dot_general(left, right, (((1,), (1,)), ((), ())), preferred_element_type=f32)


def inverse_rms(values):
    return lax.rsqrt(jnp.mean(values * values, axis=-1, keepdims=True) + norm_eps)


def step_masks(axis):
    size = lax.axis_size(axis)
    assert size & (size - 1) == 0
    ahead = [1 << n for n in range(size.bit_length() - 1)]
    return list(zip(ahead, ahead[::-1] if axis == "dp" else ahead))


def step(block, axis, masks):
    size = lax.axis_size(axis)
    route = [
        (core * size + i, core * size + (i ^ mask))
        for core, mask in enumerate(masks)
        for i in range(size)
    ]
    return lax.ppermute(block, ("section", axis), route)


def gather_steps(rows, axis, give):
    masks = step_masks(axis)
    for pair in masks:
        got = step(rows, axis, pair)
        yield got
        if pair is not masks[-1]:
            rows = jnp.concatenate([rows, got])
    give(rows, got)


def scatter_steps(lower, upper, axis, give):
    masks = step_masks(axis)
    for pair in masks[::-1]:
        got = step(upper.astype(bf16), axis, pair)
        yield got
        if pair is not masks[0]:
            total = lower.astype(f32) + got.astype(f32)
            half = total.shape[0] // 2
            lower, upper = total[:half], total[half:]
    give(lower.astype(f32), got)


def distance(block, axis, core):
    return sum(pair[core] for n, pair in enumerate(step_masks(axis)) if block & (1 << n))


def direct(block, axis, mask):
    size = lax.axis_size(axis)
    return lax.ppermute(block, axis, [(i, i ^ mask) for i in range(size)])


def other(block):
    return lax.ppermute(block, "section", [(0, 1), (1, 0)])


def by_section(first, second):
    return jnp.where(lax.axis_index("section") == 0, first, second)


def after(value, first):
    return lax.optimization_barrier((value, first))[0]


def tables(begins, places):
    lane = jnp.arange(lanes, dtype=jnp.int32) % HEAD
    frequency = rope_base ** (-2.0 * (lane % (HEAD // 2)).astype(f32) / HEAD)
    angles = (places - begins).astype(f32)[:, None] * frequency[None, :]
    signs = jnp.where(lane < HEAD // 2, -1.0, 1.0)
    return jnp.cos(angles), jnp.sin(angles) * signs[None, :]


megabyte = 1024 * 1024
lanes = 128


class Part:
    def __init__(self, array, dim, index):
        self.array, self.dim, self.index = array, dim, index

    def spec(self):
        block = list(self.array.shape)
        block[self.dim] = None
        at = [0] * len(block)
        at[self.dim] = self.index
        return pl.BlockSpec(tuple(block), lambda *_: tuple(at))

    @property
    def shape(self):
        return self.array.shape[: self.dim] + self.array.shape[self.dim + 1 :]

    @property
    def size(self):
        return self.array.size // self.array.shape[self.dim]

    @property
    def dtype(self):
        return self.array.dtype


def call(
    kernel, outs, args, scratch=(), flops=0, grid=None, in_specs=None, out_specs=None, vmem=4
):
    moved = sum(a.size * a.dtype.itemsize for a in args)
    moved += sum(o.size * o.dtype.itemsize for o in outs)
    whole = pl.BlockSpec(memory_space=pltpu.VMEM)
    scalars = pl.BlockSpec(memory_space=pltpu.SMEM)
    specs = []
    for n, arg in enumerate(args):
        if isinstance(arg, Part):
            specs.append(arg.spec())
            grid = grid or (1,)
        elif arg.dtype == jnp.int32:
            specs.append(scalars)
        else:
            specs.append(in_specs[n] if in_specs else whole)
    return pl.pallas_call(
        kernel,
        out_shape=outs,
        grid=grid or (),
        in_specs=specs,
        out_specs=out_specs or [whole] * len(outs),
        scratch_shapes=scratch,
        cost_estimate=pl.CostEstimate(
            flops=int(flops), bytes_accessed=int(moved), transcendentals=0
        ),
        compiler_params=pltpu.CompilerParams(
            vmem_limit_bytes=min(56, vmem * lax.axis_size("dp")) * megabyte
        ),
    )(*[arg.array if isinstance(arg, Part) else arg for arg in args])


def shape(*dims):
    return jax.ShapeDtypeStruct(dims[:-1], dims[-1])


def lane_of(block):
    return lax.broadcasted_iota(jnp.int32, block.shape, 1)


def turn(block, cos_table, sin_table):
    quarter = HEAD // 2
    first = lax.rem(lane_of(block), HEAD) < quarter
    turned = jnp.where(first, pltpu.roll(block, lanes - quarter, 1), pltpu.roll(block, quarter, 1))
    return block * cos_table + turned * sin_table


def qkv_kernel(x_ref, gain_ref, w_ref, bias_ref, cos_ref, sin_ref, normed_ref, q_ref, kv_ref):
    x = x_ref[...].astype(f32)
    normed = (x * inverse_rms(x) * gain_ref[...].astype(f32)).astype(bf16)
    normed_ref[...] = normed
    cos_table, sin_table = cos_ref[...], sin_ref[...]
    rows = matmul(normed, w_ref[...]) + bias_ref[...].astype(f32)
    query_width = q_ref.shape[1]
    key_end = query_width + kv_ref.shape[1] // 2
    for start in range(0, rows.shape[1], lanes):
        block = rows[:, start : start + lanes]
        if start < key_end:
            block = turn(block, cos_table, sin_table)
        if start < query_width:
            q_ref[:, start : start + lanes] = block.astype(bf16)
        else:
            kv_ref[:, start - query_width : start - query_width + lanes] = block.astype(bf16)


def qkv_rows(x, p, cos_table, sin_table, kv_width):
    rows, width = x.shape
    total = p["qkv"].shape[1]
    query_width = total - 2 * kv_width
    return call(
        qkv_kernel,
        [shape(rows, width, bf16), shape(rows, query_width, bf16), shape(rows, 2 * kv_width, bf16)],
        [x, p["gain_one"], p["qkv"], p["bias"], cos_table, sin_table],
        flops=2 * rows * width * total,
    )


def pair_rows(block, pair, group):
    swapped = pltpu.roll(block, HEAD, 1)
    low = lane_of(block) < HEAD
    rows = []
    for side in range(2):
        key_head = (2 * pair + side) // group
        here = block if key_head == side else swapped
        rows.append(jnp.where(low == (key_head == 0), here, 0.0))
    return jnp.concatenate(rows).astype(bf16)


def pair_columns(block, pair, group):
    count = block.shape[1] // 2
    parts = []
    for side in range(2):
        start = (2 * pair + side) // group * HEAD
        parts.append(block[start : start + HEAD, side * count : (side + 1) * count])
    return jnp.concatenate(parts).T


def pair_terms(keys, query_pair, bias):
    scores = matmul_nt(keys, query_pair) + jnp.concatenate([bias, bias], axis=1)
    terms = jnp.exp(scores - jnp.max(scores, axis=0, keepdims=True))
    return terms, 1.0 / jnp.sum(terms, axis=0, keepdims=True)


def lay_keys(refs, keys, values):
    count = refs[0].shape[0] * refs[0].shape[1]
    for i, ref in enumerate(refs):
        rows = ref[...].reshape(count, ref.shape[2])
        keys[i * count : (i + 1) * count] = rows[:, :lanes]
        values[i * count : (i + 1) * count] = rows[:, lanes:]


def attend_kernel(
    group,
    q_ref,
    kva_ref,
    kvb_ref,
    bias_ref,
    x_ref,
    wo_ref,
    gain_ref,
    att_ref,
    res_ref,
    mix_ref,
    keys,
    values,
):
    lay_keys((kva_ref, kvb_ref), keys, values)
    values_turned = values[...].T
    bias = bias_ref[...]
    for pair in range(q_ref.shape[1] // lanes):
        place = slice(pair * lanes, (pair + 1) * lanes)
        query_pair = pair_rows(q_ref[:, place].astype(f32) * HEAD**-0.5, pair, group)
        terms, inverse = pair_terms(keys[...], query_pair, bias)
        output = matmul(values_turned, terms.astype(bf16)) * inverse
        att_ref[:, place] = pair_columns(output, pair, group).astype(bf16)

    residual = x_ref[...].astype(f32) + matmul(att_ref[...], wo_ref[...])
    res_ref[...] = residual
    mix_ref[...] = (residual * inverse_rms(residual) * gain_ref[...].astype(f32)).astype(bf16)


def attend(queries, kva, kvb, bias, x, p, turn_of):
    rows, width = queries.shape
    total = bias.shape[0]
    kv_width = kva.shape[-1] // 2
    group = width // kv_width
    flops = 4 * rows * total * width * 4 + 2 * rows * width * x.shape[1]
    return call(
        functools.partial(attend_kernel, group),
        [shape(rows, width, bf16), shape(*x.shape, f32), shape(*x.shape, bf16)],
        [queries, kva, kvb, bias, x, p["out"], turn_of(p["gain_two"])],
        scratch=[pltpu.VMEM((total, lanes), bf16)] * 2,
        flops=flops,
    )


def norm_back(values, gain, grad):
    inverse = inverse_rms(values)
    unit = values * inverse
    scaled = grad * gain
    back = inverse * (scaled - unit * jnp.mean(scaled * unit, axis=-1, keepdims=True))
    return back, jnp.sum(grad * unit, axis=0, keepdims=True)


def attend_back_kernel(
    group,
    q_ref,
    kva_ref,
    kvb_ref,
    bias_ref,
    mix_low_ref,
    mix_got_ref,
    res_ref,
    gain_ref,
    up_ref,
    wo_ref,
    cos_ref,
    sin_ref,
    dq_ref,
    dkva_ref,
    dkvb_ref,
    gres_ref,
    gatt_ref,
    gain_two_ref,
    keys,
    values,
    queries,
    grads,
    all_probs,
    all_scores,
):
    lay_keys((kva_ref, kvb_ref), keys, values)
    grad_mixing = mix_low_ref[...] + mix_got_ref[...].astype(f32)
    back, gain_two = norm_back(res_ref[...], gain_ref[...].astype(f32), grad_mixing)
    gain_two_ref[...] = gain_two
    grad_residual = up_ref[...].astype(f32) + back
    gres_ref[...] = grad_residual
    grad_attended = grad_residual.astype(bf16)
    gatt_ref[...] = grad_attended
    grad_out = matmul_nt(grad_attended, wo_ref[...]).astype(bf16).astype(f32)
    bias = bias_ref[...]
    pairs = q_ref.shape[1] // lanes
    both = 2 * q_ref.shape[0]
    for pair in range(pairs):
        place = slice(pair * lanes, (pair + 1) * lanes)
        rows = slice(pair * both, (pair + 1) * both)
        query_pair = pair_rows(q_ref[:, place].astype(f32) * HEAD**-0.5, pair, group)
        grad_pair = pair_rows(grad_out[:, place], pair, group)
        queries[rows] = query_pair
        grads[rows] = grad_pair
        terms, inverse = pair_terms(keys[...], query_pair, bias)
        probs = terms * inverse
        all_probs[:, rows] = probs.astype(bf16)
        grad_probs = matmul_nt(values[...], grad_pair)
        delta = jnp.sum(probs * grad_probs, axis=0, keepdims=True)
        all_scores[:, rows] = (probs * (grad_probs - delta)).astype(bf16)

    grad_values = matmul(all_probs[...], grads[...]).astype(bf16)
    grad_keys = matmul(all_scores[...], queries[...]).astype(bf16)
    count = dkva_ref.shape[0]
    for i, ref in enumerate((dkva_ref, dkvb_ref)):
        ref[:, :lanes] = grad_keys[i * count : (i + 1) * count]
        ref[:, lanes:] = grad_values[i * count : (i + 1) * count]
    keys_turned = keys[...].T
    cos_table, sin_table = cos_ref[...], -sin_ref[...]
    for pair in range(pairs):
        place = slice(pair * lanes, (pair + 1) * lanes)
        turned = matmul(keys_turned, all_scores[:, pair * both : (pair + 1) * both])
        grad_query = pair_columns(turned, pair, group) * HEAD**-0.5
        dq_ref[:, place] = turn(grad_query, cos_table, sin_table).astype(bf16)


def attend_back(
    queries, kva, kvb, bias, mix_low, mix_got, residual, upstream, p, cos_table, sin_table
):
    rows, width = queries.shape
    total = bias.shape[0]
    kv_width = kva.shape[-1] // 2
    group = width // kv_width
    flops = 10 * rows * total * width * 3 + 2 * rows * width * residual.shape[1]
    return call(
        functools.partial(attend_back_kernel, group),
        [
            shape(rows, width, bf16),
            shape(total // 2, 2 * kv_width, bf16),
            shape(total // 2, 2 * kv_width, bf16),
            shape(*residual.shape, f32),
            shape(*residual.shape, bf16),
            shape(1, residual.shape[1], f32),
        ],
        [
            queries,
            kva,
            kvb,
            bias,
            mix_low,
            mix_got,
            residual,
            p["gain_two"],
            upstream,
            p["out"],
            cos_table,
            sin_table,
        ],
        scratch=[
            pltpu.VMEM((total, lanes), bf16),
            pltpu.VMEM((total, lanes), bf16),
            pltpu.VMEM((rows * width // HEAD, lanes), bf16),
            pltpu.VMEM((rows * width // HEAD, lanes), bf16),
            pltpu.VMEM((total, rows * width // HEAD), bf16),
            pltpu.VMEM((total, rows * width // HEAD), bf16),
        ],
        flops=flops,
        vmem=6,
    )


def qkv_back_kernel(
    dq_ref,
    low_ref,
    got_ref,
    cos_ref,
    sin_ref,
    w_ref,
    x_ref,
    gain_ref,
    gres_ref,
    dqkv_ref,
    gin_ref,
    gin_low_ref,
    gain_one_ref,
    bias_ref,
):
    query_width = dq_ref.shape[1]
    grad_kv = low_ref[...] + got_ref[...].astype(f32)
    dqkv_ref[:, :query_width] = dq_ref[...]
    grad_key = turn(grad_kv[:, :lanes], cos_ref[...], -sin_ref[...])
    dqkv_ref[:, query_width : query_width + lanes] = grad_key.astype(bf16)
    dqkv_ref[:, query_width + lanes :] = grad_kv[:, lanes:].astype(bf16)
    dqkv = dqkv_ref[...]
    bias_ref[...] = jnp.sum(dqkv.astype(f32), axis=0, keepdims=True)
    grad_normed = matmul_nt(dqkv, w_ref[...])
    back, gain_one = norm_back(x_ref[...].astype(f32), gain_ref[...].astype(f32), grad_normed)
    gain_one_ref[...] = gain_one
    grad_in = gres_ref[...] + back
    gin_ref[...] = grad_in
    gin_low_ref[...] = grad_in.astype(bf16)


def qkv_back(dq, low, got, x, grad_residual, p, cos_table, sin_table):
    rows, width = x.shape
    total = p["qkv"].shape[1]
    return call(
        qkv_back_kernel,
        [
            shape(rows, total, bf16),
            shape(rows, width, f32),
            shape(rows, width, bf16),
            shape(1, width, f32),
            shape(1, total, f32),
        ],
        [dq, low, got, cos_table, sin_table, p["qkv"], x, p["gain_one"], grad_residual],
        flops=2 * rows * width * total,
    )


def chunk_of(size):
    return 256 if size % 256 == 0 else 128


def ffn_kernel(lower_ref, upper_ref, wg_ref, wu_ref, wd_ref, low_ref, up_ref, hid_ref, g_ref, u_ref, rows, total):
    n = pl.program_id(0)
    half = rows.shape[0] // 2

    @pl.when(n == 0)
    def _():
        rows[:half] = lower_ref[...].reshape(half, rows.shape[1])
        rows[half:] = upper_ref[...].reshape(half, rows.shape[1])
        total[...] = jnp.zeros_like(total)

    gate = matmul(rows[...], wg_ref[...])
    up = matmul(rows[...], wu_ref[...])
    hidden = (gate * (1.0 / (1.0 + jnp.exp(-gate))) * up).astype(bf16)
    hid_ref[...] = hidden
    g_ref[...] = gate.astype(bf16)
    u_ref[...] = up.astype(bf16)
    total[...] += matmul(hidden, wd_ref[...])

    @pl.when(n == pl.num_programs(0) - 1)
    def _():
        low_ref[...] = total[:half].astype(bf16)
        up_ref[...] = total[half:].astype(bf16)


def ffn(lower, upper, p):
    half, width = lower.shape
    wide = p["gate"].shape[1]
    chunk = chunk_of(wide)
    rows = half + upper.shape[0]
    whole = pl.BlockSpec((half, width), lambda n: (0, 0))
    columns = pl.BlockSpec((width, chunk), lambda n: (0, n))
    return call(
        ffn_kernel,
        [shape(half, width, bf16), shape(rows - half, width, bf16)] + [shape(rows, wide, bf16)] * 3,
        [lower, upper, p["gate"], p["up"], p["down"]],
        scratch=[pltpu.VMEM((rows, width), bf16), pltpu.VMEM((rows, width), f32)],
        flops=6 * rows * width * wide,
        grid=(wide // chunk,),
        in_specs=[whole, whole, columns, columns, pl.BlockSpec((chunk, width), lambda n: (n, 0))],
        out_specs=[whole, whole] + [pl.BlockSpec((rows, chunk), lambda n: (0, n))] * 3,
    )


def ffn_back_kernel(
    lower_ref, upper_ref, g_ref, u_ref, wg_ref, wu_ref, wd_ref, low_ref, up_ref, gg_ref, gu_ref, rows, total
):
    n = pl.program_id(0)
    half = rows.shape[0] // 2

    @pl.when(n == 0)
    def _():
        rows[:half] = lower_ref[...].reshape(half, rows.shape[1])
        rows[half:] = upper_ref[...].reshape(half, rows.shape[1])
        total[...] = jnp.zeros_like(total)

    grad_hidden = matmul_nt(rows[...], wd_ref[...])
    gate = g_ref[...].astype(f32)
    up = u_ref[...].astype(f32)
    sigmoid = 1.0 / (1.0 + jnp.exp(-gate))
    grad_up = (grad_hidden * gate * sigmoid).astype(bf16)
    grad_gate = (grad_hidden * up * sigmoid * (1.0 + gate * (1.0 - sigmoid))).astype(bf16)
    gg_ref[...] = grad_gate
    gu_ref[...] = grad_up
    total[...] += matmul_nt(grad_gate, wg_ref[...]) + matmul_nt(grad_up, wu_ref[...])

    @pl.when(n == pl.num_programs(0) - 1)
    def _():
        low_ref[...] = total[:half].astype(bf16)
        up_ref[...] = total[half:].astype(bf16)


def ffn_back(lower, upper, gate, up, p):
    half, width = gate.shape[0] // 2, lower.shape[-1]
    wide = p["gate"].shape[1]
    chunk = chunk_of(wide)
    rows = 2 * half
    whole = pl.BlockSpec((half, width), lambda n: (0, 0))
    columns = pl.BlockSpec((width, chunk), lambda n: (0, n))
    inner = pl.BlockSpec((rows, chunk), lambda n: (0, n))
    return call(
        ffn_back_kernel,
        [shape(half, width, bf16), shape(rows - half, width, bf16)] + [shape(rows, wide, bf16)] * 2,
        [lower, upper, gate, up, p["gate"], p["up"], p["down"]],
        scratch=[pltpu.VMEM((rows, width), bf16), pltpu.VMEM((rows, width), f32)],
        flops=6 * rows * width * wide,
        grid=(wide // chunk,),
        in_specs=[
            whole,
            whole,
            inner,
            inner,
            columns,
            columns,
            pl.BlockSpec((chunk, width), lambda n: (n, 0)),
        ],
        out_specs=[whole, whole, inner, inner],
    )


def rows_of(ref):
    return ref[...].reshape(-1, ref.shape[-1])


def turn_rows(refs, turned):
    start = 0
    for ref in refs:
        turned[:, start : start + ref.shape[0]] = ref[...].T
        start += ref.shape[0]


def stack_rows(refs):
    return jnp.concatenate([rows_of(ref) for ref in refs])


def split_halves(info_ref, spread, result, keep_at, send_at):
    half = result.shape[0] // (2 * spread)
    for core in range(2):

        @pl.when(info_ref[0] == core)
        def _(core=core):
            for j in range(spread):
                for ref_at, whose in ((keep_at, core), (send_at, 1 - core)):
                    start = (2 * j + whose) * half
                    ref_at(j, result[start : start + half].astype(bf16))


def gate_up_product_kernel(lefts, spread, info_ref, *refs):
    left_refs, refs = refs[:lefts], refs[lefts:]
    keep_ref, send_ref, turned = refs[-3:]
    rights = refs[:-3]
    turn_rows(left_refs, turned)
    me = info_ref[1]
    count = len(rights) // 2
    for n in range(2):
        right = stack_rows(rights[n * count : (n + 1) * count])
        width = right.shape[1]
        for start in range(0, width, 512):
            place = slice(start, min(start + 512, width))
            result = matmul(turned[...], right[:, place])

            def keep_at(j, block, n=n, place=place):
                keep_ref[j ^ me, n, :, place] = block

            def send_at(j, block, n=n, place=place):
                send_ref[j ^ me, n, :, place] = block

            split_halves(info_ref, spread, result, keep_at, send_at)


def gate_up_product(info, lefts, gates, ups, spread):
    depth = sum(left.size // left.shape[-1] for left in lefts)
    height, width = lefts[0].shape[-1], gates[0].shape[1]
    out = shape(spread, 2, height // (2 * spread), width, bf16)
    return call(
        functools.partial(gate_up_product_kernel, len(lefts), spread),
        [out, out],
        [info] + list(lefts) + list(gates) + list(ups),
        scratch=[pltpu.VMEM((height, depth), bf16)],
        flops=4 * depth * height * width,
        vmem=8,
    )


def down_product_kernel(lefts, info_ref, *refs):
    left_refs, rights = refs[:lefts], refs[lefts:-3]
    keep_ref, send_ref, turned = refs[-3:]
    turn_rows(left_refs, turned)
    middle = keep_ref.shape[0]
    result = matmul(turned[: 2 * middle], stack_rows(rights))
    for core in range(2):

        @pl.when(info_ref[0] == core)
        def _(core=core):
            keep_ref[...] = result[core * middle : (core + 1) * middle].astype(bf16)
            send_ref[...] = result[(1 - core) * middle : (2 - core) * middle].astype(bf16)


def down_product(info, lefts, rights, rows):
    depth = sum(left.size // left.shape[-1] for left in lefts)
    height, width = lefts[0].shape[-1], rights[0].shape[-1]
    return call(
        functools.partial(down_product_kernel, len(lefts)),
        [shape(rows // 2, width, bf16)] * 2,
        [info] + list(lefts) + list(rights),
        scratch=[pltpu.VMEM((height, depth), bf16)],
        flops=2 * depth * height * width,
    )


def attn_product_kernel(count, spread, info_ref, *refs):
    normed, grad_qkv, attended, grad_attended = [
        refs[n * count : (n + 1) * count] for n in range(4)
    ]
    vector_ref, keep_ref, send_ref, turned = refs[4 * count :]
    start = 0
    for lefts, rights in ((normed, grad_qkv), (attended, grad_attended), (None, None)):
        if lefts:
            turn_rows(lefts, turned)
            result = matmul(turned[...], stack_rows(rights))
        else:
            rows = vector_ref[...]
            fill = jnp.zeros((lanes - rows.shape[0], rows.shape[1]), f32)
            result = jnp.concatenate([rows, fill]).T
        place = slice(start, start + result.shape[1])
        start += result.shape[1]

        def keep_at(j, block, place=place):
            keep_ref[info_ref[2 + j], :, place] = block

        def send_at(j, block, place=place):
            send_ref[info_ref[2 + spread + j], :, place] = block

        split_halves(info_ref, spread, result, keep_at, send_at)


def attn_product(info, normed, grad_qkv, attended, grad_attended, vectors, spread):
    depth = sum(part.shape[0] for part in normed)
    width = normed[0].shape[1]
    total = grad_qkv[0].shape[1] + grad_attended[0].shape[1] + lanes
    out = shape(spread, width // (2 * spread), total, bf16)
    return call(
        functools.partial(attn_product_kernel, len(normed), spread),
        [out, out],
        [info] + list(normed) + list(grad_qkv) + list(attended) + list(grad_attended) + [vectors],
        scratch=[pltpu.VMEM((width, depth), bf16)],
        flops=2 * depth * width * total,
    )


def pack_attn_kernel(info_ref, *refs):
    keep_ref, send_ref = refs[-2:]
    half = keep_ref.shape[0]
    for core in range(2):

        @pl.when(info_ref[0] == core)
        def _(core=core):
            start = 0
            for ref in refs[:-2]:
                place = slice(start, start + ref.shape[1])
                start += ref.shape[1]
                keep_ref[:, place] = ref[core * half : (core + 1) * half]
                send_ref[:, place] = ref[(1 - core) * half : (2 - core) * half]


def pack_attn(info, parts):
    out = shape(parts[0].shape[0] // 2, sum(part.shape[1] for part in parts), bf16)
    return call(pack_attn_kernel, [out, out], [info] + parts)


def pack_gate_up_kernel(spread, info_ref, gate_ref, up_ref, keep_ref, send_ref):
    me = info_ref[1]
    half, columns = keep_ref.shape[2:]
    for core in range(2):

        @pl.when(info_ref[0] == core)
        def _(core=core):
            for n, ref in enumerate((gate_ref, up_ref)):
                for j in range(spread):
                    block = ref[:, j * columns : (j + 1) * columns]
                    keep_ref[j ^ me, n] = block[core * half : (core + 1) * half]
                    send_ref[j ^ me, n] = block[(1 - core) * half : (2 - core) * half]


def pack_gate_up(info, gate, up, spread):
    out = shape(spread, 2, gate.shape[0] // 2, gate.shape[1] // spread, bf16)
    return call(
        functools.partial(pack_gate_up_kernel, spread), [out, out], [info, gate, up]
    )


def lay_attn_kernel(edges, at_ref, *refs):
    parts, outs = refs[:4], refs[4:]
    half = outs[0].shape[1]
    n = 0
    for ref in parts:
        for start in range(0, ref.shape[0], half):
            block = ref[start : start + half]
            for out, (low, high) in zip(outs, edges):
                out[at_ref[n]] = block[:, low:high]
            n += 1


def lay_attn(at, parts, half, edges):
    count = at.shape[0]
    outs = [shape(count, half, high - low, bf16) for low, high in edges]
    got = call(functools.partial(lay_attn_kernel, edges), outs, [at] + parts)
    return [part.reshape(count * half, -1) for part in got]


def lay_gate_up_kernel(at_ref, *refs):
    parts, outs = refs[:-2], refs[-2:]
    for i, ref in enumerate(parts):
        for n, out in enumerate(outs):
            columns = ref.shape[2]
            out[at_ref[i], :, :columns] = ref[n]
            if columns < out.shape[2]:
                rest = (out.shape[1], out.shape[2] - columns)
                out[at_ref[i], :, columns:] = jnp.zeros(rest, bf16)


def lay_gate_up(at, parts, wide):
    half = parts[0].shape[1]
    outs = [shape(len(parts), half, wide, bf16)] * 2
    got = call(lay_gate_up_kernel, outs, [at] + parts)
    return [part.reshape(len(parts) * half, wide) for part in got]


def spread_kernel(spread, info_ref, *refs):
    gate_ref, up_ref = refs[-2:]
    count = (len(refs) - 2) // 2
    per = spread // count
    me = info_ref[1]
    half = refs[0].shape[2]
    columns = gate_ref.shape[1] // spread
    for core in range(2):

        @pl.when(info_ref[0] == core)
        def _(core=core):
            for i in range(spread):
                for parts, whose in ((refs[:count], core), (refs[count:-2], 1 - core)):
                    for n, out in enumerate((gate_ref, up_ref)):
                        block = parts[i // per][i % per, n][:, :columns].astype(f32)
                        for j in range(spread):

                            @pl.when((i ^ me) == j)
                            def _(j=j, block=block, whose=whose, out=out):
                                place = slice(j * columns, (j + 1) * columns)
                                out[whose * half : (whose + 1) * half, place] = block


def spread_gate_up(info, mine, theirs, columns, spread):
    half = mine[0].shape[2]
    out = shape(2 * half, spread * columns, f32)
    return call(
        functools.partial(spread_kernel, spread), [out, out], [info] + list(mine) + list(theirs)
    )


def local(
    tokens,
    doc_starts,
    cotangent,
    norm_one,
    w_query,
    b_query,
    w_key,
    b_key,
    w_value,
    b_value,
    w_out,
    norm_two,
    w_gate,
    w_up,
    w_down,
):
    core = lax.axis_index("section")
    cores = lax.axis_size("section")
    spread = lax.axis_size("dp")
    micro_count, _, row_count, width = tokens.shape
    layers = range(2)
    share = row_count // cores
    shard = w_query.shape[1]
    half = shard // 2
    query_width = w_query.shape[2]
    kv_width = w_key.shape[2]
    ff = w_gate.shape[2]
    slice_ff = ff // spread

    me = lax.axis_index("dp")
    wide = -(-slice_ff // lanes) * lanes
    edge = query_width + 2 * kv_width
    per = kv_width // spread

    def order_of(mine):
        masks = step_masks("dp")

        def place(j, core):
            return sum(
                jnp.where(((me ^ j) & pair[core]) != 0, 1 << n, 0) for n, pair in enumerate(masks)
            )

        first, second = (0, 1) if mine else (1, 0)
        return [by_section(place(j, first), place(j, second)) for j in range(spread)]

    def owner(block, mine):
        first, second = (0, 1) if mine else (1, 0)
        masks = [distance(block, "dp", first), distance(block, "dp", second)]
        return me ^ by_section(*masks)

    info = jnp.stack([core, me] + order_of(True) + order_of(False)).astype(jnp.int32)
    attn_at = jnp.stack(
        [
            2 * owner(block, mine) + (core if mine else 1 - core)
            for mine in (True, False)
            for block in range(spread)
        ]
    ).astype(jnp.int32)
    gate_up_at = jnp.stack(
        [2 * (me ^ mask) + whose for whose in (core, 1 - core) for mask in range(spread)]
    ).astype(jnp.int32)

    def column(vector):
        return jnp.pad(vector, (0, shard - vector.shape[0]))

    vectors = jnp.stack(
        [norm_one[0], norm_two[0], b_query[0], column(b_key[0]), column(b_value[0])], axis=1
    )
    vectors = jnp.pad(vectors, ((0, 0), (0, lanes - vectors.shape[1])))

    def per_layer(keep, send):
        got = other(send)
        return by_section(keep, got), by_section(got, keep)

    attn_halves = per_layer(
        *pack_attn(info, [w_query[0], w_key[0], w_value[0], w_out[0], vectors])
    )
    gate_up_halves = per_layer(*pack_gate_up(info, w_gate[0], w_up[0], spread))
    down_other = other(w_down[0])
    downs = by_section(w_down[0], down_other), by_section(down_other, w_down[0])

    params = [{}, {}]
    clock, flows, last, pins = [0], [], [], []

    class Flow:
        def __init__(self, steps, slack):
            self.steps, self.slack = steps, slack
            self.move()
            flows.append(self)

        def move(self):
            self.value = next(self.steps, None)
            self.due = clock[0] + self.slack

        def finish(self):
            while self.value is not None:
                self.move()

    def turn_of(value):
        clock[0] += 1
        for flow in list(flows):
            if flow.value is not None and flow.due <= clock[0]:
                pins.append(flow.value)
                flow.move()
            if flow.value is None:
                flows.remove(flow)
        wait = last + pins
        pins.clear()
        return after(value, wait) if wait else value

    def done(value):
        last[:] = [value]

    def weights_steps(layer, part, blocks):
        p = params[layer]
        parts = []
        yield from gather_steps(part, "dp", lambda *got: parts.extend(got))
        blocks = after(blocks, parts[1])
        qkv, out, small = lay_attn(
            attn_at,
            parts + [other(part) for part in parts],
            half,
            ((0, edge), (edge, edge + width), (edge + width, edge + width + lanes)),
        )
        rows = small.T
        p["qkv"], p["out"] = qkv, out
        p["gain_one"], p["gain_two"] = rows[0:1], rows[1:2]
        key_bias, value_bias = [
            rows[n].reshape(spread, shard)[:, :per].reshape(1, -1) for n in (3, 4)
        ]
        p["bias"] = jnp.concatenate([rows[2:3], key_bias, value_bias], axis=1)
        blocks = [blocks[0]] + [direct(blocks[mask], "dp", mask) for mask in range(1, spread)]
        yield blocks
        yield blocks
        blocks = blocks + [other(block) for block in blocks]
        blocks, down = after((blocks, downs[layer]), list(last))
        p["gate"], p["up"] = lay_gate_up(gate_up_at, blocks, wide)
        p["down"] = jnp.pad(down, ((0, wide - slice_ff), (0, 0)))

    first = core * share
    place = lax.axis_index("ctx")
    places = place * row_count + first + jnp.arange(share, dtype=jnp.int32)
    my_tokens = lax.dynamic_slice_in_dim(tokens[:, 0], first, share, 1)
    my_cotangent = lax.dynamic_slice_in_dim(cotangent[:, 0], first, share, 1)
    key_places = jnp.concatenate(
        [
            (place ^ block) * row_count + whose * share + jnp.arange(share, dtype=jnp.int32)
            for whose in (core, 1 - core)
            for block in range(lax.axis_size("ctx"))
        ]
    )
    starts = doc_starts[:, 0, None, :]
    begins = jnp.max(jnp.where(starts <= places[None, :, None], starts, 0), axis=2)
    places_all = jnp.tile(places, micro_count)
    cos_all, sin_all = tables(begins.reshape(-1), places_all)
    visible = (key_places[None, :, None] <= places[None, None, :]) & (
        key_places[None, :, None] >= begins[:, None, :]
    )
    bias_all = jnp.where(visible, 0.0, masked).astype(f32)
    context = [
        (
            Part(bias_all, 0, n),
            Part(cos_all.reshape(micro_count, share, lanes), 0, n),
            Part(sin_all.reshape(micro_count, share, lanes), 0, n),
        )
        for n in range(micro_count)
    ]

    kept = [[{} for _ in range(micro_count)] for _ in layers]
    for n in range(micro_count):
        kept[1][n]["above"] = Part(my_cotangent, 0, n)
    def kv_steps(ks, kv):
        def give(*parts):
            whole = jnp.concatenate(parts)
            theirs = other(whole)
            for n, k in enumerate(ks):
                k["kva"], k["kvb"] = [
                    Part(part.reshape(-1, len(ks), share, 2 * kv_width), 1, n)
                    for part in (whole, theirs)
                ]

        yield from gather_steps(kv[None], "ctx", give)

    def run_q_all():
        flow = Flow(weights_steps(0, attn_halves[0], gate_up_halves[0]), weight_slack)
        while "qkv" not in params[0]:
            flow.move()
        kept[0][0]["weights"] = flow
        tokens_in = turn_of(my_tokens.reshape(-1, width))
        rows = qkv_rows(tokens_in, params[0], cos_all, sin_all, kv_width)
        done(rows[0])
        normed, queries = [part.reshape(micro_count, share, -1) for part in rows[:2]]
        for n in range(micro_count):
            k = kept[0][n]
            k["x"], k["normed"], k["queries"] = [
                Part(part, 0, n) for part in (my_tokens, normed, queries)
            ]
        flow = Flow(kv_steps(kept[0], rows[2]), 1)
        for n in range(micro_count):
            kept[0][n]["kv"] = flow
        halves = after((attn_halves[1], gate_up_halves[1]), list(last))
        kept[1][0]["weights"] = Flow(weights_steps(1, *halves), 1)

    def run_q(n):
        k = kept[1][n]
        kept[0][n]["scatter"].finish()
        while "qkv" not in params[1]:
            kept[1][0]["weights"].move()
        k["x"] = turn_of(kept[0][n]["result"])
        k["normed"], k["queries"], kv = qkv_rows(k["x"], params[1], *context[n][1:], kv_width)
        done(k["normed"])
        k["kv"] = Flow(kv_steps([k], kv), 2)

    def run_a(layer, n):
        k, p = kept[layer][n], params[layer]
        k["kv"].finish()
        k["attended"], k["residual"], mixing = attend(
            k["queries"], k["kva"], k["kvb"], context[n][0], k["x"], p, turn_of
        )
        done(mixing)
        k["gather"] = Flow(gather_steps(mixing, "dp", lambda *got: k.update(mixing=got)), 2)

    def run_f(layer, n):
        k, p = kept[layer][n], params[layer]
        k["gather"].finish()
        kept[layer][0]["weights"].finish()
        lower, upper = k["mixing"]
        part_low, part_up, k["hidden"], k["gate"], k["up"] = ffn(lower, turn_of(upper), p)
        done(k["gate"])

        def give(low, got):
            k["result"] = (k["residual"] + low + got.astype(f32)).astype(bf16)

        k["scatter"] = Flow(scatter_steps(part_low, part_up, "dp", give), 2 if layer == 0 else 6)
        if layer:
            k["after"] = k["scatter"]

    def run_c():
        def give(*parts):
            for n in range(micro_count):
                kept[1][n]["grad_ffn"] = [
                    Part(part.reshape(-1, micro_count, share, width), 1, n) for part in parts
                ]

        rows = after(my_cotangent[None], last)
        kept[1][0]["cotangent"] = Flow(gather_steps(rows, "dp", give), 4)

    def run_d(layer, n):
        k, p = kept[layer][n], params[layer]
        if layer:
            kept[1][0]["cotangent"].finish()
        else:
            k["gather"].finish()
        lower, upper = k["grad_ffn"]
        part_low, part_up, k["grad_gate"], k["grad_up"] = ffn_back(
            lower, upper, turn_of(k["gate"]), k["up"], p
        )
        done(k["grad_gate"])
        k["scatter"] = Flow(
            scatter_steps(part_low, part_up, "dp", lambda *got: k.update(scattered=got)), 2
        )

    def run_b(layer, n):
        k, p = kept[layer][n], params[layer]
        k["scatter"].finish()
        bias, cos_table, sin_table = context[n]
        low, got = k["scattered"]
        k["dq"], dkva, dkvb, k["grad_residual"], k["grad_attended"], k["gain_two"] = attend_back(
            k["queries"],
            k["kva"],
            k["kvb"],
            bias,
            low,
            turn_of(got),
            k["residual"],
            k["above"],
            p,
            cos_table,
            sin_table,
        )
        done(k["dq"])
        pair = dkva.astype(f32) + other(dkvb).astype(f32)
        middle = pair.shape[0] // 2
        k["scatter"] = Flow(
            scatter_steps(
                pair[:middle], pair[middle:], "ctx", lambda *got: k.update(grad_kv=got)
            ),
            2,
        )

    def run_k(layer, n):
        k, p = kept[layer][n], params[layer]
        k["scatter"].finish()
        low, got = k["grad_kv"]
        k["grad_qkv"], k["grad_in"], grad_low, k["gain_one"], k["bias"] = qkv_back(
            k["dq"], low, turn_of(got), k["x"], k["grad_residual"], p, *context[n][1:]
        )
        done(k["grad_qkv"])
        if layer:
            below = kept[0][n]
            below["above"] = k["grad_in"]
            below["gather"] = Flow(
                gather_steps(grad_low, "dp", lambda *got: below.update(grad_ffn=got)), 2
            )

    ends = (place == 0) | (place == 3)
    hops = [[(0, 1), (3, 2)], [(1, 2), (2, 1)], [(1, 0), (2, 3)]]
    sums = {}

    def ctx_steps(name, value):
        for hop, route in enumerate(hops):
            got = lax.ppermute(value, "ctx", route)
            yield got
            if hop == 2:
                sums[name] = jnp.where(ends, got, value)
            else:
                value = (value.astype(f32) + got.astype(f32)).astype(bf16)

    waiting, moving, exchanges = {}, [], {}

    def tick(*names):
        for flow in list(moving):
            pins.append(flow.value)
            flow.move()
            if flow.value is None:
                moving.remove(flow)
        for name in names:
            if name not in waiting:
                exchanges.pop(name).finish()
            moving.append(Flow(ctx_steps(name, waiting.pop(name)), 1000))

    def column_of(layer, name):
        return [k[name] for k in kept[layer]]

    def parts_of(layer, name):
        return [part for k in kept[layer] for part in k[name]]

    def over_cores(keep, send):
        return keep.astype(f32) + other(send).astype(f32)

    def run_pd(layer):
        hidden = column_of(layer, "hidden")
        hidden[0] = turn_of(hidden[0])
        keep, send = down_product(info, hidden, parts_of(layer, "grad_ffn"), slice_ff)
        done(keep)
        waiting["down", layer] = over_cores(keep, send).astype(bf16)

    def run_pg(layer):
        grads = column_of(layer, "grad_gate")
        grads[0] = turn_of(grads[0])
        keep, send = gate_up_product(
            info, parts_of(layer, "mixing"), grads, column_of(layer, "grad_up"), spread
        )
        done(keep)
        blocks = over_cores(keep, send).astype(bf16)
        before = kept[layer][micro_count - 1]["scatter"].value

        def steps():
            sent = after(blocks, before) if before is not None else blocks
            parts = [sent[0]] + [direct(sent[mask], "dp", mask) for mask in range(1, spread)]
            yield parts[1:]
            middle = spread // 2
            waiting["low", layer] = jnp.stack(parts[:middle])
            waiting["high", layer] = jnp.stack(parts[middle:])

        exchanges["low", layer] = Flow(steps(), 3)

    def run_pa(layer):
        bias = sum(column_of(layer, "bias"))[0]

        def column_sum(vector):
            return jnp.pad(vector.reshape(spread, -1), ((0, 0), (0, shard - per))).reshape(-1)

        vectors = jnp.stack(
            [
                sum(column_of(layer, "gain_one"))[0],
                sum(column_of(layer, "gain_two"))[0],
                bias[:query_width],
                column_sum(bias[query_width : query_width + kv_width]),
                column_sum(bias[query_width + kv_width :]),
            ]
            + [jnp.zeros((width,), f32)] * 3
        )
        keep, send = attn_product(
            info,
            column_of(layer, "normed"),
            column_of(layer, "grad_qkv"),
            column_of(layer, "attended"),
            column_of(layer, "grad_attended"),
            turn_of(vectors),
            spread,
        )
        done(keep)
        attn = over_cores(keep, send).reshape(spread * half, -1)


        def give(low, got):
            waiting["attn", layer] = (low + got.astype(f32)).astype(bf16)

        exchanges["attn", layer] = Flow(scatter_steps(*jnp.split(attn, 2), "dp", give), 2)

    steps = dict(
        q=run_q,
        a=run_a,
        f=run_f,
        c=run_c,
        d=run_d,
        b=run_b,
        k=run_k,
        D=run_pd,
        G=run_pg,
        P=run_pa,
    )
    run_q_all()
    names = dict(d="down", l="low", h="high", a="attn")
    for word in order:
        if word[0] == "z":
            tick(*[(names[word[n]], int(word[n + 1])) for n in range(1, len(word), 2)])
        else:
            steps[word[0]](*[int(digit) for digit in word[1:]])
    while moving:
        tick()
    for k in kept[1]:
        if "result" not in k:
            k["after"].finish()

    section_out = both_rows([jnp.stack(column_of(layer, "result")) for layer in layers])
    section_grad = both_rows([jnp.stack(column_of(layer, "grad_in")) for layer in layers])

    final = [[sums[name, layer] for name in ("attn", "low", "high", "down")] for layer in layers]
    mine = [by_section(*pair) for pair in zip(*final)]
    theirs = [other(by_section(*pair[::-1])) for pair in zip(*final)]
    gate, up = spread_gate_up(info, mine[1:3], theirs[1:3], slice_ff, spread)

    def in_order(mine, theirs):
        return by_section(
            jnp.concatenate([mine, theirs]), jnp.concatenate([theirs, mine])
        ).astype(f32)

    attn = in_order(*after((mine[0], theirs[0]), gate))
    down = in_order(mine[3], theirs[3])
    small = attn[:, edge + width :]
    return (
        section_out,
        section_grad,
        small[None, :, 0],
        attn[None, :, :query_width],
        small[None, :, 2],
        attn[None, :, query_width : query_width + kv_width],
        small[None, :per, 3],
        attn[None, :, query_width + kv_width : edge],
        small[None, :per, 4],
        attn[None, :, edge : edge + width],
        small[None, :, 1],
        gate[None],
        up[None],
        down[None],
    )


weight_slack = 2
order = (
    "a00", "a01", "f00", "a02", "f01", "q0", "f02", "q1", "a10", "q2", "a11", "c", "f10", "a12", "f11", "d10",
    "f12", "d11", "b10", "d12", "D1", "zd1", "G1", "b11", "z", "k10", "b12", "zl1", "k11", "d00", "zh1",
    "k12", "d01", "z", "P1", "d02", "za1", "D0", "zd0", "G0", "b00", "zl0", "b01", "zh0", "k00", "b02", "z",
    "k01", "k02", "z", "P0", "za0",
)


def both_rows(per_layer):
    first, second = per_layer
    got = other(by_section(second, first))
    return by_section(
        jnp.concatenate([first, got], axis=1), jnp.concatenate([got, second], axis=1)
    )[None, :, None]


def solution(mesh):
    return jax.shard_map(
        local,
        mesh=mesh,
        in_specs=(
            P(None, "dp", "ctx", None),
            P(None, "dp", None),
            P(None, "dp", "ctx", None),
            P("section", "dp"),
            P("section", "dp", None),
            P("section", "dp"),
            P("section", "dp", None),
            P("section", "dp"),
            P("section", "dp", None),
            P("section", "dp"),
            P("section", "dp", None),
            P("section", "dp"),
            P("section", "dp", None),
            P("section", "dp", None),
            P("section", "dp", None),
        ),
        out_specs=(
            P("section", None, "dp", "ctx", None),
            P("section", None, "dp", "ctx", None),
            P("section", "dp"),
            P("section", "dp", None),
            P("section", "dp"),
            P("section", "dp", None),
            P("section", "dp"),
            P("section", "dp", None),
            P("section", "dp"),
            P("section", "dp", None),
            P("section", "dp"),
            P("section", "dp", None),
            P("section", "dp", None),
            P("section", "dp", None),
        ),
        check_vma=False,
    )
```

```python
import functools
from types import SimpleNamespace

import jax
import jax.numpy as jnp
from jax import lax
from jax.experimental import pallas as pl
from jax.experimental.pallas import tpu as pltpu
from jax.sharding import PartitionSpec as P

HEAD = 64
rope_base = 1000000.0
norm_eps = 1e-06
masked = -1e30
bf16 = jnp.bfloat16
f32 = jnp.float32


def matmul(left, right):
    return jnp.dot(left, right, preferred_element_type=f32)


def matmul_nt(left, right):
    return lax.dot_general(left, right, (((1,), (1,)), ((), ())), preferred_element_type=f32)


def inverse_rms(values):
    return lax.rsqrt(jnp.mean(values * values, axis=-1, keepdims=True) + norm_eps)


def step_masks(axis):
    size = lax.axis_size(axis)
    assert size & (size - 1) == 0
    ahead = [1 << n for n in range(size.bit_length() - 1)]
    return list(zip(ahead, ahead[::-1] if axis == "dp" else ahead))


def step(block, axis, masks):
    size = lax.axis_size(axis)
    route = [
        (core * size + i, core * size + (i ^ mask))
        for core, mask in enumerate(masks)
        for i in range(size)
    ]
    return lax.ppermute(block, ("section", axis), route)


def gather_steps(rows, axis, give):
    masks = step_masks(axis)
    for pair in masks:
        got = step(rows, axis, pair)
        yield got
        if pair is not masks[-1]:
            rows = jnp.concatenate([rows, got])
    give(rows, got)


def scatter_steps(lower, upper, axis, give):
    masks = step_masks(axis)
    for pair in masks[::-1]:
        got = step(upper.astype(bf16), axis, pair)
        yield got
        if pair is not masks[0]:
            total = lower.astype(f32) + got.astype(f32)
            half = total.shape[0] // 2
            lower, upper = total[:half], total[half:]
    give(lower.astype(f32), got)


def distance(block, axis, core):
    return sum(pair[core] for n, pair in enumerate(step_masks(axis)) if block & (1 << n))


def direct(block, axis, mask):
    size = lax.axis_size(axis)
    return lax.ppermute(block, axis, [(i, i ^ mask) for i in range(size)])


def other(block):
    return lax.ppermute(block, "section", [(0, 1), (1, 0)])


def by_section(first, second):
    return jnp.where(lax.axis_index("section") == 0, first, second)


def after(value, first):
    return lax.optimization_barrier((value, first))[0]


def tables(begins, places):
    lane = jnp.arange(lanes, dtype=jnp.int32) % HEAD
    frequency = rope_base ** (-2.0 * (lane % (HEAD // 2)).astype(f32) / HEAD)
    angles = (places - begins).astype(f32)[:, None] * frequency[None, :]
    signs = jnp.where(lane < HEAD // 2, -1.0, 1.0)
    return jnp.cos(angles), jnp.sin(angles) * signs[None, :]


megabyte = 1024 * 1024
lanes = 128


class Part:
    def __init__(self, array, dim, index):
        self.array, self.dim, self.index = array, dim, index

    def spec(self):
        block = list(self.array.shape)
        block[self.dim] = None
        at = [0] * len(block)
        at[self.dim] = self.index
        return pl.BlockSpec(tuple(block), lambda *_: tuple(at))

    @property
    def shape(self):
        return self.array.shape[: self.dim] + self.array.shape[self.dim + 1 :]

    @property
    def size(self):
        return self.array.size // self.array.shape[self.dim]

    @property
    def dtype(self):
        return self.array.dtype


def call(
    kernel, outs, args, scratch=(), flops=0, grid=None, in_specs=None, out_specs=None, vmem=4
):
    moved = sum(a.size * a.dtype.itemsize for a in args)
    moved += sum(o.size * o.dtype.itemsize for o in outs)
    whole = pl.BlockSpec(memory_space=pltpu.VMEM)
    scalars = pl.BlockSpec(memory_space=pltpu.SMEM)
    specs = []
    for n, arg in enumerate(args):
        if isinstance(arg, Part):
            specs.append(arg.spec())
            grid = grid or (1,)
        elif arg.dtype == jnp.int32:
            specs.append(scalars)
        else:
            specs.append(in_specs[n] if in_specs else whole)
    return pl.pallas_call(
        kernel,
        out_shape=outs,
        grid=grid or (),
        in_specs=specs,
        out_specs=out_specs or [whole] * len(outs),
        scratch_shapes=scratch,
        cost_estimate=pl.CostEstimate(
            flops=int(flops), bytes_accessed=int(moved), transcendentals=0
        ),
        compiler_params=pltpu.CompilerParams(
            vmem_limit_bytes=min(56, vmem * lax.axis_size("dp")) * megabyte
        ),
    )(*[arg.array if isinstance(arg, Part) else arg for arg in args])


def shape(*dims):
    return jax.ShapeDtypeStruct(dims[:-1], dims[-1])


def lane_of(block):
    return lax.broadcasted_iota(jnp.int32, block.shape, 1)


def turn(block, cos_table, sin_table):
    quarter = HEAD // 2
    first = lax.rem(lane_of(block), HEAD) < quarter
    turned = jnp.where(first, pltpu.roll(block, lanes - quarter, 1), pltpu.roll(block, quarter, 1))
    return block * cos_table + turned * sin_table


def qkv_kernel(x_ref, gain_ref, w_ref, bias_ref, cos_ref, sin_ref, normed_ref, q_ref, kv_ref):
    x = x_ref[...].astype(f32)
    normed = (x * inverse_rms(x) * gain_ref[...].astype(f32)).astype(bf16)
    normed_ref[...] = normed
    cos_table, sin_table = cos_ref[...], sin_ref[...]
    rows = matmul(normed, w_ref[...]) + bias_ref[...].astype(f32)
    query_width = q_ref.shape[1]
    key_end = query_width + kv_ref.shape[1] // 2
    for start in range(0, rows.shape[1], lanes):
        block = rows[:, start : start + lanes]
        if start < key_end:
            block = turn(block, cos_table, sin_table)
        if start < query_width:
            q_ref[:, start : start + lanes] = block.astype(bf16)
        else:
            kv_ref[:, start - query_width : start - query_width + lanes] = block.astype(bf16)


def qkv_rows(x, p, cos_table, sin_table, kv_width):
    rows, width = x.shape
    total = p.qkv.shape[1]
    query_width = total - 2 * kv_width
    return call(
        qkv_kernel,
        [shape(rows, width, bf16), shape(rows, query_width, bf16), shape(rows, 2 * kv_width, bf16)],
        [x, p.gain_one, p.qkv, p.bias, cos_table, sin_table],
        flops=2 * rows * width * total,
    )


def pair_rows(block, pair, group):
    swapped = pltpu.roll(block, HEAD, 1)
    low = lane_of(block) < HEAD
    rows = []
    for side in range(2):
        key_head = (2 * pair + side) // group
        here = block if key_head == side else swapped
        rows.append(jnp.where(low == (key_head == 0), here, 0.0))
    return jnp.concatenate(rows).astype(bf16)


def pair_columns(block, pair, group):
    count = block.shape[1] // 2
    parts = []
    for side in range(2):
        start = (2 * pair + side) // group * HEAD
        parts.append(block[start : start + HEAD, side * count : (side + 1) * count])
    return jnp.concatenate(parts).T


def pair_terms(keys, query_pair, bias):
    scores = matmul_nt(keys, query_pair) + jnp.concatenate([bias, bias], axis=1)
    terms = jnp.exp(scores - jnp.max(scores, axis=0, keepdims=True))
    return terms, 1.0 / jnp.sum(terms, axis=0, keepdims=True)


def lay_keys(refs, keys, values):
    count = refs[0].shape[0] * refs[0].shape[1]
    for i, ref in enumerate(refs):
        rows = ref[...].reshape(count, ref.shape[2])
        keys[i * count : (i + 1) * count] = rows[:, :lanes]
        values[i * count : (i + 1) * count] = rows[:, lanes:]


def attend_kernel(
    group,
    q_ref,
    kva_ref,
    kvb_ref,
    bias_ref,
    x_ref,
    wo_ref,
    gain_ref,
    att_ref,
    res_ref,
    mix_ref,
    keys,
    values,
):
    lay_keys((kva_ref, kvb_ref), keys, values)
    values_turned = values[...].T
    bias = bias_ref[...]
    for pair in range(q_ref.shape[1] // lanes):
        place = slice(pair * lanes, (pair + 1) * lanes)
        query_pair = pair_rows(q_ref[:, place].astype(f32) * HEAD**-0.5, pair, group)
        terms, inverse = pair_terms(keys[...], query_pair, bias)
        output = matmul(values_turned, terms.astype(bf16)) * inverse
        att_ref[:, place] = pair_columns(output, pair, group).astype(bf16)

    residual = x_ref[...].astype(f32) + matmul(att_ref[...], wo_ref[...])
    res_ref[...] = residual
    mix_ref[...] = (residual * inverse_rms(residual) * gain_ref[...].astype(f32)).astype(bf16)


def attend(queries, kva, kvb, bias, x, p, turn_of):
    rows, width = queries.shape
    total = bias.shape[0]
    kv_width = kva.shape[-1] // 2
    group = width // kv_width
    flops = 4 * rows * total * width * 4 + 2 * rows * width * x.shape[1]
    return call(
        functools.partial(attend_kernel, group),
        [shape(rows, width, bf16), shape(*x.shape, f32), shape(*x.shape, bf16)],
        [queries, kva, kvb, bias, x, p.out, turn_of(p.gain_two)],
        scratch=[pltpu.VMEM((total, lanes), bf16)] * 2,
        flops=flops,
    )


def norm_back(values, gain, grad):
    inverse = inverse_rms(values)
    unit = values * inverse
    scaled = grad * gain
    back = inverse * (scaled - unit * jnp.mean(scaled * unit, axis=-1, keepdims=True))
    return back, jnp.sum(grad * unit, axis=0, keepdims=True)


def attend_back_kernel(
    group,
    q_ref,
    kva_ref,
    kvb_ref,
    bias_ref,
    mix_low_ref,
    mix_got_ref,
    res_ref,
    gain_ref,
    up_ref,
    wo_ref,
    cos_ref,
    sin_ref,
    dq_ref,
    dkva_ref,
    dkvb_ref,
    gres_ref,
    gatt_ref,
    gain_two_ref,
    keys,
    values,
    queries,
    grads,
    all_probs,
    all_scores,
):
    lay_keys((kva_ref, kvb_ref), keys, values)
    grad_mixing = mix_low_ref[...] + mix_got_ref[...].astype(f32)
    back, gain_two = norm_back(res_ref[...], gain_ref[...].astype(f32), grad_mixing)
    gain_two_ref[...] = gain_two
    grad_residual = up_ref[...].astype(f32) + back
    gres_ref[...] = grad_residual
    grad_attended = grad_residual.astype(bf16)
    gatt_ref[...] = grad_attended
    grad_out = matmul_nt(grad_attended, wo_ref[...]).astype(bf16).astype(f32)
    bias = bias_ref[...]
    pairs = q_ref.shape[1] // lanes
    both = 2 * q_ref.shape[0]
    for pair in range(pairs):
        place = slice(pair * lanes, (pair + 1) * lanes)
        rows = slice(pair * both, (pair + 1) * both)
        query_pair = pair_rows(q_ref[:, place].astype(f32) * HEAD**-0.5, pair, group)
        grad_pair = pair_rows(grad_out[:, place], pair, group)
        queries[rows] = query_pair
        grads[rows] = grad_pair
        terms, inverse = pair_terms(keys[...], query_pair, bias)
        probs = terms * inverse
        all_probs[:, rows] = probs.astype(bf16)
        grad_probs = matmul_nt(values[...], grad_pair)
        delta = jnp.sum(probs * grad_probs, axis=0, keepdims=True)
        all_scores[:, rows] = (probs * (grad_probs - delta)).astype(bf16)

    grad_values = matmul(all_probs[...], grads[...]).astype(bf16)
    grad_keys = matmul(all_scores[...], queries[...]).astype(bf16)
    count = dkva_ref.shape[0]
    for i, ref in enumerate((dkva_ref, dkvb_ref)):
        ref[:, :lanes] = grad_keys[i * count : (i + 1) * count]
        ref[:, lanes:] = grad_values[i * count : (i + 1) * count]
    keys_turned = keys[...].T
    cos_table, sin_table = cos_ref[...], -sin_ref[...]
    for pair in range(pairs):
        place = slice(pair * lanes, (pair + 1) * lanes)
        turned = matmul(keys_turned, all_scores[:, pair * both : (pair + 1) * both])
        grad_query = pair_columns(turned, pair, group) * HEAD**-0.5
        dq_ref[:, place] = turn(grad_query, cos_table, sin_table).astype(bf16)


def attend_back(
    queries, kva, kvb, bias, mix_low, mix_got, residual, upstream, p, cos_table, sin_table
):
    rows, width = queries.shape
    total = bias.shape[0]
    kv_width = kva.shape[-1] // 2
    group = width // kv_width
    flops = 10 * rows * total * width * 3 + 2 * rows * width * residual.shape[1]
    return call(
        functools.partial(attend_back_kernel, group),
        [
            shape(rows, width, bf16),
            shape(total // 2, 2 * kv_width, bf16),
            shape(total // 2, 2 * kv_width, bf16),
            shape(*residual.shape, f32),
            shape(*residual.shape, bf16),
            shape(1, residual.shape[1], f32),
        ],
        [
            queries,
            kva,
            kvb,
            bias,
            mix_low,
            mix_got,
            residual,
            p.gain_two,
            upstream,
            p.out,
            cos_table,
            sin_table,
        ],
        scratch=[
            pltpu.VMEM((total, lanes), bf16),
            pltpu.VMEM((total, lanes), bf16),
            pltpu.VMEM((rows * width // HEAD, lanes), bf16),
            pltpu.VMEM((rows * width // HEAD, lanes), bf16),
            pltpu.VMEM((total, rows * width // HEAD), bf16),
            pltpu.VMEM((total, rows * width // HEAD), bf16),
        ],
        flops=flops,
        vmem=6,
    )


def qkv_back_kernel(
    dq_ref,
    low_ref,
    got_ref,
    cos_ref,
    sin_ref,
    w_ref,
    x_ref,
    gain_ref,
    gres_ref,
    dqkv_ref,
    gin_ref,
    gin_low_ref,
    gain_one_ref,
    bias_ref,
):
    query_width = dq_ref.shape[1]
    grad_kv = low_ref[...] + got_ref[...].astype(f32)
    dqkv_ref[:, :query_width] = dq_ref[...]
    grad_key = turn(grad_kv[:, :lanes], cos_ref[...], -sin_ref[...])
    dqkv_ref[:, query_width : query_width + lanes] = grad_key.astype(bf16)
    dqkv_ref[:, query_width + lanes :] = grad_kv[:, lanes:].astype(bf16)
    dqkv = dqkv_ref[...]
    bias_ref[...] = jnp.sum(dqkv.astype(f32), axis=0, keepdims=True)
    grad_normed = matmul_nt(dqkv, w_ref[...])
    back, gain_one = norm_back(x_ref[...].astype(f32), gain_ref[...].astype(f32), grad_normed)
    gain_one_ref[...] = gain_one
    grad_in = gres_ref[...] + back
    gin_ref[...] = grad_in
    gin_low_ref[...] = grad_in.astype(bf16)


def qkv_back(dq, low, got, x, grad_residual, p, cos_table, sin_table):
    rows, width = x.shape
    total = p.qkv.shape[1]
    return call(
        qkv_back_kernel,
        [
            shape(rows, total, bf16),
            shape(rows, width, f32),
            shape(rows, width, bf16),
            shape(1, width, f32),
            shape(1, total, f32),
        ],
        [dq, low, got, cos_table, sin_table, p.qkv, x, p.gain_one, grad_residual],
        flops=2 * rows * width * total,
    )


def chunk_of(size):
    return 256 if size % 256 == 0 else 128


def ffn_kernel(lower_ref, upper_ref, wg_ref, wu_ref, wd_ref, low_ref, up_ref, hid_ref, g_ref, u_ref, rows, total):
    n = pl.program_id(0)
    half = rows.shape[0] // 2

    @pl.when(n == 0)
    def _():
        rows[:half] = lower_ref[...].reshape(half, rows.shape[1])
        rows[half:] = upper_ref[...].reshape(half, rows.shape[1])
        total[...] = jnp.zeros_like(total)

    gate = matmul(rows[...], wg_ref[...])
    up = matmul(rows[...], wu_ref[...])
    hidden = (gate * (1.0 / (1.0 + jnp.exp(-gate))) * up).astype(bf16)
    hid_ref[...] = hidden
    g_ref[...] = gate.astype(bf16)
    u_ref[...] = up.astype(bf16)
    total[...] += matmul(hidden, wd_ref[...])

    @pl.when(n == pl.num_programs(0) - 1)
    def _():
        low_ref[...] = total[:half].astype(bf16)
        up_ref[...] = total[half:].astype(bf16)


def ffn(lower, upper, p):
    half, width = lower.shape
    wide = p.gate.shape[1]
    chunk = wide
    rows = half + upper.shape[0]
    whole = pl.BlockSpec((half, width), lambda n: (0, 0))
    columns = pl.BlockSpec((width, chunk), lambda n: (0, n))
    return call(
        ffn_kernel,
        [shape(half, width, bf16), shape(rows - half, width, bf16)] + [shape(rows, wide, bf16)] * 3,
        [lower, upper, p.gate, p.up, p.down],
        scratch=[pltpu.VMEM((rows, width), bf16), pltpu.VMEM((rows, width), f32)],
        flops=6 * rows * width * wide,
        vmem=6,
        grid=(wide // chunk,),
        in_specs=[whole, whole, columns, columns, pl.BlockSpec((chunk, width), lambda n: (n, 0))],
        out_specs=[whole, whole] + [pl.BlockSpec((rows, chunk), lambda n: (0, n))] * 3,
    )


def ffn_back_kernel(
    lower_ref, upper_ref, g_ref, u_ref, wg_ref, wu_ref, wd_ref, low_ref, up_ref, gg_ref, gu_ref, rows, total
):
    n = pl.program_id(0)
    half = rows.shape[0] // 2

    @pl.when(n == 0)
    def _():
        rows[:half] = lower_ref[...].reshape(half, rows.shape[1])
        rows[half:] = upper_ref[...].reshape(half, rows.shape[1])
        total[...] = jnp.zeros_like(total)

    grad_hidden = matmul_nt(rows[...], wd_ref[...])
    gate = g_ref[...].astype(f32)
    up = u_ref[...].astype(f32)
    sigmoid = 1.0 / (1.0 + jnp.exp(-gate))
    grad_up = (grad_hidden * gate * sigmoid).astype(bf16)
    grad_gate = (grad_hidden * up * sigmoid * (1.0 + gate * (1.0 - sigmoid))).astype(bf16)
    gg_ref[...] = grad_gate
    gu_ref[...] = grad_up
    total[...] += matmul_nt(grad_gate, wg_ref[...]) + matmul_nt(grad_up, wu_ref[...])

    @pl.when(n == pl.num_programs(0) - 1)
    def _():
        low_ref[...] = total[:half].astype(bf16)
        up_ref[...] = total[half:].astype(bf16)


def ffn_back(lower, upper, gate, up, p):
    half, width = gate.shape[0] // 2, lower.shape[-1]
    wide = p.gate.shape[1]
    chunk = wide
    rows = 2 * half
    whole = pl.BlockSpec((half, width), lambda n: (0, 0))
    columns = pl.BlockSpec((width, chunk), lambda n: (0, n))
    inner = pl.BlockSpec((rows, chunk), lambda n: (0, n))
    return call(
        ffn_back_kernel,
        [shape(half, width, bf16), shape(rows - half, width, bf16)] + [shape(rows, wide, bf16)] * 2,
        [lower, upper, gate, up, p.gate, p.up, p.down],
        scratch=[pltpu.VMEM((rows, width), bf16), pltpu.VMEM((rows, width), f32)],
        flops=6 * rows * width * wide,
        vmem=6,
        grid=(wide // chunk,),
        in_specs=[
            whole,
            whole,
            inner,
            inner,
            columns,
            columns,
            pl.BlockSpec((chunk, width), lambda n: (n, 0)),
        ],
        out_specs=[whole, whole, inner, inner],
    )


def rows_of(ref):
    return ref[...].reshape(-1, ref.shape[-1])


def turn_rows(refs, turned):
    start = 0
    for ref in refs:
        turned[:, start : start + ref.shape[0]] = ref[...].T
        start += ref.shape[0]


def stack_rows(refs):
    return jnp.concatenate([rows_of(ref) for ref in refs])


def split_halves(info_ref, spread, result, keep_at, send_at):
    half = result.shape[0] // (2 * spread)
    for core in range(2):

        @pl.when(info_ref[0] == core)
        def _(core=core):
            for j in range(spread):
                for ref_at, whose in ((keep_at, core), (send_at, 1 - core)):
                    start = (2 * j + whose) * half
                    ref_at(j, result[start : start + half].astype(bf16))


def gate_up_product_kernel(lefts, spread, info_ref, *refs):
    left_refs, refs = refs[:lefts], refs[lefts:]
    keep_ref, send_ref, turned = refs[-3:]
    rights = refs[:-3]
    turn_rows(left_refs, turned)
    me = info_ref[1]
    count = len(rights) // 2
    for n in range(2):
        right = stack_rows(rights[n * count : (n + 1) * count])
        width = right.shape[1]
        for start in range(0, width, 512):
            place = slice(start, min(start + 512, width))
            result = matmul(turned[...], right[:, place])

            def keep_at(j, block, n=n, place=place):
                keep_ref[j ^ me, n, :, place] = block

            def send_at(j, block, n=n, place=place):
                send_ref[j ^ me, n, :, place] = block

            split_halves(info_ref, spread, result, keep_at, send_at)


def gate_up_product(info, lefts, gates, ups, spread):
    depth = sum(left.size // left.shape[-1] for left in lefts)
    height, width = lefts[0].shape[-1], gates[0].shape[1]
    out = shape(spread, 2, height // (2 * spread), width, bf16)
    return call(
        functools.partial(gate_up_product_kernel, len(lefts), spread),
        [out, out],
        [info] + list(lefts) + list(gates) + list(ups),
        scratch=[pltpu.VMEM((height, depth), bf16)],
        flops=4 * depth * height * width,
        vmem=8,
    )


def down_product_kernel(lefts, info_ref, *refs):
    left_refs, rights = refs[:lefts], refs[lefts:-3]
    keep_ref, send_ref, turned = refs[-3:]
    turn_rows(left_refs, turned)
    middle = keep_ref.shape[0]
    result = matmul(turned[: 2 * middle], stack_rows(rights))
    for core in range(2):

        @pl.when(info_ref[0] == core)
        def _(core=core):
            keep_ref[...] = result[core * middle : (core + 1) * middle].astype(bf16)
            send_ref[...] = result[(1 - core) * middle : (2 - core) * middle].astype(bf16)


def down_product(info, lefts, rights, rows):
    depth = sum(left.size // left.shape[-1] for left in lefts)
    height, width = lefts[0].shape[-1], rights[0].shape[-1]
    return call(
        functools.partial(down_product_kernel, len(lefts)),
        [shape(rows // 2, width, bf16)] * 2,
        [info] + list(lefts) + list(rights),
        scratch=[pltpu.VMEM((height, depth), bf16)],
        flops=2 * depth * height * width,
    )


def attn_product_kernel(count, spread, info_ref, *refs):
    normed, grad_qkv, attended, grad_attended = [
        refs[n * count : (n + 1) * count] for n in range(4)
    ]
    vector_ref, keep_ref, send_ref, turned = refs[4 * count :]
    start = 0
    for lefts, rights in ((normed, grad_qkv), (attended, grad_attended), (None, None)):
        if lefts:
            turn_rows(lefts, turned)
            result = matmul(turned[...], stack_rows(rights))
        else:
            rows = vector_ref[...]
            fill = jnp.zeros((lanes - rows.shape[0], rows.shape[1]), f32)
            result = jnp.concatenate([rows, fill]).T
        place = slice(start, start + result.shape[1])
        start += result.shape[1]

        def keep_at(j, block, place=place):
            keep_ref[info_ref[2 + j], :, place] = block

        def send_at(j, block, place=place):
            send_ref[info_ref[2 + spread + j], :, place] = block

        split_halves(info_ref, spread, result, keep_at, send_at)


def attn_product(info, normed, grad_qkv, attended, grad_attended, vectors, spread):
    depth = sum(part.shape[0] for part in normed)
    width = normed[0].shape[1]
    total = grad_qkv[0].shape[1] + grad_attended[0].shape[1] + lanes
    out = shape(spread, width // (2 * spread), total, bf16)
    return call(
        functools.partial(attn_product_kernel, len(normed), spread),
        [out, out],
        [info] + list(normed) + list(grad_qkv) + list(attended) + list(grad_attended) + [vectors],
        scratch=[pltpu.VMEM((width, depth), bf16)],
        flops=2 * depth * width * total,
    )


def pack_attn_kernel(info_ref, *refs):
    keep_ref, send_ref = refs[-2:]
    half = keep_ref.shape[0]
    for core in range(2):

        @pl.when(info_ref[0] == core)
        def _(core=core):
            start = 0
            for ref in refs[:-2]:
                place = slice(start, start + ref.shape[1])
                start += ref.shape[1]
                keep_ref[:, place] = ref[core * half : (core + 1) * half]
                send_ref[:, place] = ref[(1 - core) * half : (2 - core) * half]


def pack_attn(info, parts):
    out = shape(parts[0].shape[0] // 2, sum(part.shape[1] for part in parts), bf16)
    return call(pack_attn_kernel, [out, out], [info] + parts)


def pack_gate_up_kernel(spread, info_ref, gate_ref, up_ref, keep_ref, send_ref):
    me = info_ref[1]
    half, columns = keep_ref.shape[2:]
    for core in range(2):

        @pl.when(info_ref[0] == core)
        def _(core=core):
            for n, ref in enumerate((gate_ref, up_ref)):
                for j in range(spread):
                    block = ref[:, j * columns : (j + 1) * columns]
                    keep_ref[j ^ me, n] = block[core * half : (core + 1) * half]
                    send_ref[j ^ me, n] = block[(1 - core) * half : (2 - core) * half]


def pack_gate_up(info, gate, up, spread):
    out = shape(spread, 2, gate.shape[0] // 2, gate.shape[1] // spread, bf16)
    return call(
        functools.partial(pack_gate_up_kernel, spread), [out, out], [info, gate, up]
    )


def lay_attn_kernel(edges, at_ref, *refs):
    parts, outs = refs[:4], refs[4:]
    half = outs[0].shape[1]
    n = 0
    for ref in parts:
        for start in range(0, ref.shape[0], half):
            block = ref[start : start + half]
            for out, (low, high) in zip(outs, edges):
                out[at_ref[n]] = block[:, low:high]
            n += 1


def lay_attn(at, parts, half, edges):
    count = at.shape[0]
    outs = [shape(count, half, high - low, bf16) for low, high in edges]
    got = call(functools.partial(lay_attn_kernel, edges), outs, [at] + parts)
    return [part.reshape(count * half, -1) for part in got]


def lay_gate_up_kernel(at_ref, *refs):
    parts, outs = refs[:-2], refs[-2:]
    for i, ref in enumerate(parts):
        for n, out in enumerate(outs):
            columns = ref.shape[2]
            out[at_ref[i], :, :columns] = ref[n]
            if columns < out.shape[2]:
                rest = (out.shape[1], out.shape[2] - columns)
                out[at_ref[i], :, columns:] = jnp.zeros(rest, bf16)


def lay_gate_up(at, parts, wide):
    half = parts[0].shape[1]
    outs = [shape(len(parts), half, wide, bf16)] * 2
    got = call(lay_gate_up_kernel, outs, [at] + parts)
    return [part.reshape(len(parts) * half, wide) for part in got]


def spread_kernel(spread, info_ref, *refs):
    gate_ref, up_ref = refs[-2:]
    count = (len(refs) - 2) // 2
    per = spread // count
    me = info_ref[1]
    half = refs[0].shape[2]
    columns = gate_ref.shape[1] // spread
    for core in range(2):

        @pl.when(info_ref[0] == core)
        def _(core=core):
            for i in range(spread):
                for parts, whose in ((refs[:count], core), (refs[count:-2], 1 - core)):
                    for n, out in enumerate((gate_ref, up_ref)):
                        block = parts[i // per][i % per, n][:, :columns].astype(f32)
                        for j in range(spread):

                            @pl.when((i ^ me) == j)
                            def _(j=j, block=block, whose=whose, out=out):
                                place = slice(j * columns, (j + 1) * columns)
                                out[whose * half : (whose + 1) * half, place] = block


def spread_gate_up(info, mine, theirs, columns, spread):
    half = mine[0].shape[2]
    out = shape(2 * half, spread * columns, f32)
    return call(
        functools.partial(spread_kernel, spread), [out, out], [info] + list(mine) + list(theirs)
    )


def local(
    tokens,
    doc_starts,
    cotangent,
    norm_one,
    w_query,
    b_query,
    w_key,
    b_key,
    w_value,
    b_value,
    w_out,
    norm_two,
    w_gate,
    w_up,
    w_down,
):
    core = lax.axis_index("section")
    cores = lax.axis_size("section")
    spread = lax.axis_size("dp")
    micro_count, _, row_count, width = tokens.shape
    layers = range(2)
    share = row_count // cores
    shard = w_query.shape[1]
    half = shard // 2
    query_width = w_query.shape[2]
    kv_width = w_key.shape[2]
    ff = w_gate.shape[2]
    slice_ff = ff // spread

    me = lax.axis_index("dp")
    wide = -(-slice_ff // lanes) * lanes
    edge = query_width + 2 * kv_width
    per = kv_width // spread

    def order_of(mine):
        masks = step_masks("dp")

        def place(j, core):
            return sum(
                jnp.where(((me ^ j) & pair[core]) != 0, 1 << n, 0) for n, pair in enumerate(masks)
            )

        first, second = (0, 1) if mine else (1, 0)
        return [by_section(place(j, first), place(j, second)) for j in range(spread)]

    def owner(block, mine):
        first, second = (0, 1) if mine else (1, 0)
        masks = [distance(block, "dp", first), distance(block, "dp", second)]
        return me ^ by_section(*masks)

    info = jnp.stack([core, me] + order_of(True) + order_of(False)).astype(jnp.int32)
    attn_at = jnp.stack(
        [
            2 * owner(block, mine) + (core if mine else 1 - core)
            for mine in (True, False)
            for block in range(spread)
        ]
    ).astype(jnp.int32)
    gate_up_at = jnp.stack(
        [2 * (me ^ mask) + whose for whose in (core, 1 - core) for mask in range(spread)]
    ).astype(jnp.int32)

    def column(vector):
        return jnp.pad(vector, (0, shard - vector.shape[0]))

    vectors = jnp.stack(
        [norm_one[0], norm_two[0], b_query[0], column(b_key[0]), column(b_value[0])], axis=1
    )
    vectors = jnp.pad(vectors, ((0, 0), (0, lanes - vectors.shape[1])))

    def per_layer(keep, send):
        got = other(send)
        return by_section(keep, got), by_section(got, keep)

    attn_halves = per_layer(
        *pack_attn(info, [w_query[0], w_key[0], w_value[0], w_out[0], vectors])
    )
    gate_up_halves = per_layer(*pack_gate_up(info, w_gate[0], w_up[0], spread))
    down_other = other(w_down[0])
    downs = by_section(w_down[0], down_other), by_section(down_other, w_down[0])

    params = [SimpleNamespace(), SimpleNamespace()]
    clock, flows, last, pins = [0], [], [], []

    class Flow:
        def __init__(self, steps, slack):
            self.steps, self.slack = steps, slack
            self.move()
            flows.append(self)

        def move(self):
            self.value = next(self.steps, None)
            self.due = clock[0] + self.slack

        def finish(self):
            while self.value is not None:
                self.move()

    def turn_of(value):
        clock[0] += 1
        for flow in list(flows):
            if flow.value is not None and flow.due <= clock[0]:
                pins.append(flow.value)
                flow.move()
            if flow.value is None:
                flows.remove(flow)
        wait = last + pins
        pins.clear()
        return after(value, wait) if wait else value

    def done(value):
        last[:] = [value]

    def weights_steps(layer, part, blocks):
        p = params[layer]
        parts = []
        yield from gather_steps(part, "dp", lambda *got: parts.extend(got))
        blocks = after(blocks, parts[1])
        qkv, out, small = lay_attn(
            attn_at,
            parts + [other(part) for part in parts],
            half,
            ((0, edge), (edge, edge + width), (edge + width, edge + width + lanes)),
        )
        rows = small.T
        p.qkv, p.out = qkv, out
        p.gain_one, p.gain_two = rows[0:1], rows[1:2]
        key_bias, value_bias = [
            rows[n].reshape(spread, shard)[:, :per].reshape(1, -1) for n in (3, 4)
        ]
        p.bias = jnp.concatenate([rows[2:3], key_bias, value_bias], axis=1)
        blocks = [blocks[0]] + [direct(blocks[mask], "dp", mask) for mask in range(1, spread)]
        yield blocks
        yield blocks
        blocks = blocks + [other(block) for block in blocks]
        blocks, down = after((blocks, downs[layer]), list(last))
        p.gate, p.up = lay_gate_up(gate_up_at, blocks, wide)
        p.down = jnp.pad(down, ((0, wide - slice_ff), (0, 0)))

    first = core * share
    place = lax.axis_index("ctx")
    places = place * row_count + first + jnp.arange(share, dtype=jnp.int32)
    my_tokens = lax.dynamic_slice_in_dim(tokens[:, 0], first, share, 1)
    my_cotangent = lax.dynamic_slice_in_dim(cotangent[:, 0], first, share, 1)
    key_places = jnp.concatenate(
        [
            (place ^ block) * row_count + whose * share + jnp.arange(share, dtype=jnp.int32)
            for whose in (core, 1 - core)
            for block in range(lax.axis_size("ctx"))
        ]
    )
    starts = doc_starts[:, 0, None, :]
    begins = jnp.max(jnp.where(starts <= places[None, :, None], starts, 0), axis=2)
    places_all = jnp.tile(places, micro_count)
    cos_all, sin_all = tables(begins.reshape(-1), places_all)
    visible = (key_places[None, :, None] <= places[None, None, :]) & (
        key_places[None, :, None] >= begins[:, None, :]
    )
    bias_all = jnp.where(visible, 0.0, masked).astype(f32)
    context = [
        (
            Part(bias_all, 0, n),
            Part(cos_all.reshape(micro_count, share, lanes), 0, n),
            Part(sin_all.reshape(micro_count, share, lanes), 0, n),
        )
        for n in range(micro_count)
    ]

    kept = [[SimpleNamespace() for _ in range(micro_count)] for _ in layers]
    for n in range(micro_count):
        kept[1][n].above = Part(my_cotangent, 0, n)
    def kv_steps(ks, kv):
        def give(*parts):
            whole = jnp.concatenate(parts)
            theirs = other(whole)
            for n, k in enumerate(ks):
                k.kva, k.kvb = [
                    Part(part.reshape(-1, len(ks), share, 2 * kv_width), 1, n)
                    for part in (whole, theirs)
                ]

        yield from gather_steps(kv[None], "ctx", give)

    def run_q_all():
        flow = Flow(weights_steps(0, attn_halves[0], gate_up_halves[0]), weight_slack)
        while not hasattr(params[0], "qkv"):
            flow.move()
        kept[0][0].weights = flow
        tokens_in = turn_of(my_tokens.reshape(-1, width))
        rows = qkv_rows(tokens_in, params[0], cos_all, sin_all, kv_width)
        done(rows[0])
        normed, queries = [part.reshape(micro_count, share, -1) for part in rows[:2]]
        for n in range(micro_count):
            k = kept[0][n]
            k.x, k.normed, k.queries = [
                Part(part, 0, n) for part in (my_tokens, normed, queries)
            ]
        flow = Flow(kv_steps(kept[0], rows[2]), 1)
        for n in range(micro_count):
            kept[0][n].kv = flow
        halves = after((attn_halves[1], gate_up_halves[1]), list(last))
        kept[1][0].weights = Flow(weights_steps(1, *halves), 1)

    def run_q(n):
        k = kept[1][n]
        kept[0][n].scatter.finish()
        while not hasattr(params[1], "qkv"):
            kept[1][0].weights.move()
        k.x = turn_of(kept[0][n].result)
        k.normed, k.queries, kv = qkv_rows(k.x, params[1], *context[n][1:], kv_width)
        done(k.normed)
        k.kv = Flow(kv_steps([k], kv), 2)

    def run_a(layer, n):
        k, p = kept[layer][n], params[layer]
        k.kv.finish()
        k.attended, k.residual, mixing = attend(
            k.queries, k.kva, k.kvb, context[n][0], k.x, p, turn_of
        )
        done(mixing)
        k.gather = Flow(gather_steps(mixing, "dp", lambda *got: k.__dict__.update(mixing=got)), 2)

    def run_f(layer, n):
        k, p = kept[layer][n], params[layer]
        k.gather.finish()
        kept[layer][0].weights.finish()
        lower, upper = k.mixing
        part_low, part_up, k.hidden, k.gate, k.up = ffn(lower, turn_of(upper), p)
        done(k.gate)

        def give(low, got):
            k.result = (k.residual + low + got.astype(f32)).astype(bf16)

        k.scatter = Flow(scatter_steps(part_low, part_up, "dp", give), 2 if layer == 0 else 6)
        if layer:
            k.after = k.scatter

    def run_c():
        def give(*parts):
            for n in range(micro_count):
                kept[1][n].grad_ffn = [
                    Part(part.reshape(-1, micro_count, share, width), 1, n) for part in parts
                ]

        rows = after(my_cotangent[None], last)
        kept[1][0].cotangent = Flow(gather_steps(rows, "dp", give), 4)

    def run_d(layer, n):
        k, p = kept[layer][n], params[layer]
        if layer:
            kept[1][0].cotangent.finish()
        else:
            k.gather.finish()
        lower, upper = k.grad_ffn
        part_low, part_up, k.grad_gate, k.grad_up = ffn_back(
            lower, upper, turn_of(k.gate), k.up, p
        )
        done(k.grad_gate)
        k.scatter = Flow(
            scatter_steps(part_low, part_up, "dp", lambda *got: k.__dict__.update(scattered=got)), 2
        )

    def run_b(layer, n):
        k, p = kept[layer][n], params[layer]
        k.scatter.finish()
        bias, cos_table, sin_table = context[n]
        low, got = k.scattered
        k.dq, dkva, dkvb, k.grad_residual, k.grad_attended, k.gain_two = attend_back(
            k.queries,
            k.kva,
            k.kvb,
            bias,
            low,
            turn_of(got),
            k.residual,
            k.above,
            p,
            cos_table,
            sin_table,
        )
        done(k.dq)
        pair = dkva.astype(f32) + other(dkvb).astype(f32)
        middle = pair.shape[0] // 2
        k.scatter = Flow(
            scatter_steps(
                pair[:middle], pair[middle:], "ctx", lambda *got: k.__dict__.update(grad_kv=got)
            ),
            2,
        )

    def run_k(layer, n):
        k, p = kept[layer][n], params[layer]
        k.scatter.finish()
        low, got = k.grad_kv
        k.grad_qkv, k.grad_in, grad_low, k.gain_one, k.bias = qkv_back(
            k.dq, low, turn_of(got), k.x, k.grad_residual, p, *context[n][1:]
        )
        done(k.grad_qkv)
        if layer:
            below = kept[0][n]
            below.above = k.grad_in
            below.gather = Flow(
                gather_steps(grad_low, "dp", lambda *got: below.__dict__.update(grad_ffn=got)), 2
            )

    ends = (place == 0) | (place == 3)
    hops = [[(0, 1), (3, 2)], [(1, 2), (2, 1)], [(1, 0), (2, 3)]]
    sums = {}

    def ctx_steps(name, value):
        for hop, route in enumerate(hops):
            got = lax.ppermute(value, "ctx", route)
            yield got
            if hop == 2:
                sums[name] = jnp.where(ends, got, value)
            else:
                value = (value.astype(f32) + got.astype(f32)).astype(bf16)

    waiting, moving, exchanges = {}, [], {}

    def tick(*names):
        for flow in list(moving):
            pins.append(flow.value)
            flow.move()
            if flow.value is None:
                moving.remove(flow)
        for name in names:
            if name not in waiting:
                exchanges.pop(name).finish()
            moving.append(Flow(ctx_steps(name, waiting.pop(name)), 1000))

    def column_of(layer, name):
        return [getattr(k, name) for k in kept[layer]]

    def parts_of(layer, name):
        return [part for k in kept[layer] for part in getattr(k, name)]

    def over_cores(keep, send):
        return keep.astype(f32) + other(send).astype(f32)

    def run_pd(layer):
        hidden = column_of(layer, "hidden")
        hidden[0] = turn_of(hidden[0])
        keep, send = down_product(info, hidden, parts_of(layer, "grad_ffn"), slice_ff)
        done(keep)
        waiting["down", layer] = over_cores(keep, send).astype(bf16)

    def run_pg(layer):
        grads = column_of(layer, "grad_gate")
        grads[0] = turn_of(grads[0])
        keep, send = gate_up_product(
            info, parts_of(layer, "mixing"), grads, column_of(layer, "grad_up"), spread
        )
        done(keep)
        blocks = over_cores(keep, send).astype(bf16)
        before = kept[layer][micro_count - 1].scatter.value

        def steps():
            sent = after(blocks, before) if before is not None else blocks
            parts = [sent[0]] + [direct(sent[mask], "dp", mask) for mask in range(1, spread)]
            yield parts[1:]
            middle = spread // 2
            waiting["low", layer] = jnp.stack(parts[:middle])
            waiting["high", layer] = jnp.stack(parts[middle:])

        exchanges["low", layer] = Flow(steps(), 3)

    def run_pa(layer):
        bias = sum(column_of(layer, "bias"))[0]

        def column_sum(vector):
            return jnp.pad(vector.reshape(spread, -1), ((0, 0), (0, shard - per))).reshape(-1)

        vectors = jnp.stack(
            [
                sum(column_of(layer, "gain_one"))[0],
                sum(column_of(layer, "gain_two"))[0],
                bias[:query_width],
                column_sum(bias[query_width : query_width + kv_width]),
                column_sum(bias[query_width + kv_width :]),
            ]
            + [jnp.zeros((width,), f32)] * 3
        )
        keep, send = attn_product(
            info,
            column_of(layer, "normed"),
            column_of(layer, "grad_qkv"),
            column_of(layer, "attended"),
            column_of(layer, "grad_attended"),
            turn_of(vectors),
            spread,
        )
        done(keep)
        attn = over_cores(keep, send).reshape(spread * half, -1)


        def give(low, got):
            waiting["attn", layer] = (low + got.astype(f32)).astype(bf16)

        exchanges["attn", layer] = Flow(scatter_steps(*jnp.split(attn, 2), "dp", give), 2)

    steps = dict(
        q=run_q,
        a=run_a,
        f=run_f,
        c=run_c,
        d=run_d,
        b=run_b,
        k=run_k,
        D=run_pd,
        G=run_pg,
        P=run_pa,
    )
    run_q_all()
    names = dict(d="down", l="low", h="high", a="attn")
    for word in order:
        if word[0] == "z":
            tick(*[(names[word[n]], int(word[n + 1])) for n in range(1, len(word), 2)])
        else:
            steps[word[0]](*[int(digit) for digit in word[1:]])
    while moving:
        tick()
    for k in kept[1]:
        if not hasattr(k, "result"):
            k.after.finish()

    section_out = both_rows([jnp.stack(column_of(layer, "result")) for layer in layers])
    section_grad = both_rows([jnp.stack(column_of(layer, "grad_in")) for layer in layers])

    final = [[sums[name, layer] for name in ("attn", "low", "high", "down")] for layer in layers]
    mine = [by_section(*pair) for pair in zip(*final)]
    theirs = [other(by_section(*pair[::-1])) for pair in zip(*final)]
    gate, up = spread_gate_up(info, mine[1:3], theirs[1:3], slice_ff, spread)

    def in_order(mine, theirs):
        return by_section(
            jnp.concatenate([mine, theirs]), jnp.concatenate([theirs, mine])
        ).astype(f32)

    attn = in_order(*after((mine[0], theirs[0]), gate))
    down = in_order(mine[3], theirs[3])
    small = attn[:, edge + width :]
    return (
        section_out,
        section_grad,
        small[None, :, 0],
        attn[None, :, :query_width],
        small[None, :, 2],
        attn[None, :, query_width : query_width + kv_width],
        small[None, :per, 3],
        attn[None, :, query_width + kv_width : edge],
        small[None, :per, 4],
        attn[None, :, edge : edge + width],
        small[None, :, 1],
        gate[None],
        up[None],
        down[None],
    )


weight_slack = 2
order = (
    "a00", "a01", "f00", "a02", "f01", "q0", "f02", "q1", "a10", "q2", "a11", "c", "f10", "a12", "f11", "d10",
    "f12", "d11", "b10", "d12", "D1", "zd1", "G1", "b11", "z", "k10", "b12", "zl1", "k11", "d00", "zh1",
    "k12", "d01", "z", "P1", "d02", "za1", "D0", "zd0", "G0", "b00", "zl0", "b01", "zh0", "k00", "b02", "z",
    "k01", "k02", "z", "P0", "za0",
)


def both_rows(per_layer):
    first, second = per_layer
    got = other(by_section(second, first))
    return by_section(
        jnp.concatenate([first, got], axis=1), jnp.concatenate([got, second], axis=1)
    )[None, :, None]


def solution(mesh):
    return jax.shard_map(
        local,
        mesh=mesh,
        in_specs=(
            P(None, "dp", "ctx", None),
            P(None, "dp", None),
            P(None, "dp", "ctx", None),
            P("section", "dp"),
            P("section", "dp", None),
            P("section", "dp"),
            P("section", "dp", None),
            P("section", "dp"),
            P("section", "dp", None),
            P("section", "dp"),
            P("section", "dp", None),
            P("section", "dp"),
            P("section", "dp", None),
            P("section", "dp", None),
            P("section", "dp", None),
        ),
        out_specs=(
            P("section", None, "dp", "ctx", None),
            P("section", None, "dp", "ctx", None),
            P("section", "dp"),
            P("section", "dp", None),
            P("section", "dp"),
            P("section", "dp", None),
            P("section", "dp"),
            P("section", "dp", None),
            P("section", "dp"),
            P("section", "dp", None),
            P("section", "dp"),
            P("section", "dp", None),
            P("section", "dp", None),
            P("section", "dp", None),
        ),
        check_vma=False,
    )
```

```python
import functools
from types import SimpleNamespace

import jax
import jax.numpy as jnp
from jax import lax
from jax.experimental import pallas as pl
from jax.experimental.pallas import tpu as pltpu
from jax.sharding import PartitionSpec as P

HEAD = 64
rope_base = 1000000.0
norm_eps = 1e-06
masked = -1e30
bf16 = jnp.bfloat16
f32 = jnp.float32


def matmul(left, right):
    return jnp.dot(left, right, preferred_element_type=f32)


def matmul_nt(left, right):
    return lax.dot_general(left, right, (((1,), (1,)), ((), ())), preferred_element_type=f32)


def inverse_rms(values):
    return lax.rsqrt(jnp.mean(values * values, axis=-1, keepdims=True) + norm_eps)


def step_masks(axis):
    size = lax.axis_size(axis)
    assert size & (size - 1) == 0
    ahead = [1 << n for n in range(size.bit_length() - 1)]
    return list(zip(ahead, ahead[::-1] if axis == "dp" else ahead))


def step(block, axis, masks):
    size = lax.axis_size(axis)
    route = [
        (core * size + i, core * size + (i ^ mask))
        for core, mask in enumerate(masks)
        for i in range(size)
    ]
    return lax.ppermute(block, ("section", axis), route)


def gather_steps(rows, axis, give):
    masks = step_masks(axis)
    for pair in masks:
        got = step(rows, axis, pair)
        yield got
        if pair is not masks[-1]:
            rows = jnp.concatenate([rows, got])
    give(rows, got)


def scatter_steps(lower, upper, axis, give):
    masks = step_masks(axis)
    for pair in masks[::-1]:
        got = step(upper.astype(bf16), axis, pair)
        yield got
        if pair is not masks[0]:
            total = lower.astype(f32) + got.astype(f32)
            half = total.shape[0] // 2
            lower, upper = total[:half], total[half:]
    give(lower.astype(f32), got)


def distance(block, axis, core):
    return sum(pair[core] for n, pair in enumerate(step_masks(axis)) if block & (1 << n))


def direct(block, axis, mask):
    size = lax.axis_size(axis)
    return lax.ppermute(block, axis, [(i, i ^ mask) for i in range(size)])


def other(block):
    return lax.ppermute(block, "section", [(0, 1), (1, 0)])


def by_section(first, second):
    return jnp.where(lax.axis_index("section") == 0, first, second)


def after(value, first):
    return lax.optimization_barrier((value, first))[0]


def tables(begins, places):
    lane = jnp.arange(lanes, dtype=jnp.int32) % HEAD
    frequency = rope_base ** (-2.0 * (lane % (HEAD // 2)).astype(f32) / HEAD)
    angles = (places - begins).astype(f32)[:, None] * frequency[None, :]
    signs = jnp.where(lane < HEAD // 2, -1.0, 1.0)
    return jnp.cos(angles), jnp.sin(angles) * signs[None, :]


megabyte = 1024 * 1024
lanes = 128


class Part:
    def __init__(self, array, dim, index):
        self.array, self.dim, self.index = array, dim, index

    def spec(self):
        block = list(self.array.shape)
        block[self.dim] = None
        at = [0] * len(block)
        at[self.dim] = self.index
        return pl.BlockSpec(tuple(block), lambda *_: tuple(at))

    @property
    def shape(self):
        return self.array.shape[: self.dim] + self.array.shape[self.dim + 1 :]

    @property
    def size(self):
        return self.array.size // self.array.shape[self.dim]

    @property
    def dtype(self):
        return self.array.dtype


def call(
    kernel, outs, args, scratch=(), flops=0, grid=None, in_specs=None, out_specs=None, vmem=4
):
    moved = sum(a.size * a.dtype.itemsize for a in args)
    moved += sum(o.size * o.dtype.itemsize for o in outs)
    whole = pl.BlockSpec(memory_space=pltpu.VMEM)
    scalars = pl.BlockSpec(memory_space=pltpu.SMEM)
    specs = []
    for n, arg in enumerate(args):
        if isinstance(arg, Part):
            specs.append(arg.spec())
            grid = grid or (1,)
        elif arg.dtype == jnp.int32:
            specs.append(scalars)
        else:
            specs.append(in_specs[n] if in_specs else whole)
    return pl.pallas_call(
        kernel,
        out_shape=outs,
        grid=grid or (),
        in_specs=specs,
        out_specs=out_specs or [whole] * len(outs),
        scratch_shapes=scratch,
        cost_estimate=pl.CostEstimate(
            flops=int(flops), bytes_accessed=int(moved), transcendentals=0
        ),
        compiler_params=pltpu.CompilerParams(
            vmem_limit_bytes=min(56, vmem * lax.axis_size("dp")) * megabyte
        ),
    )(*[arg.array if isinstance(arg, Part) else arg for arg in args])


def shape(*dims):
    return jax.ShapeDtypeStruct(dims[:-1], dims[-1])


def lane_of(block):
    return lax.broadcasted_iota(jnp.int32, block.shape, 1)


def turn(block, cos_table, sin_table):
    quarter = HEAD // 2
    first = lax.rem(lane_of(block), HEAD) < quarter
    turned = jnp.where(first, pltpu.roll(block, lanes - quarter, 1), pltpu.roll(block, quarter, 1))
    return block * cos_table + turned * sin_table


def qkv_kernel(x_ref, gain_ref, w_ref, bias_ref, cos_ref, sin_ref, normed_ref, q_ref, kv_ref):
    x = x_ref[...].astype(f32)
    normed = (x * inverse_rms(x) * gain_ref[...].astype(f32)).astype(bf16)
    normed_ref[...] = normed
    cos_table, sin_table = cos_ref[...], sin_ref[...]
    rows = matmul(normed, w_ref[...]) + bias_ref[...].astype(f32)
    query_width = q_ref.shape[1]
    key_end = query_width + kv_ref.shape[1] // 2
    for start in range(0, rows.shape[1], lanes):
        block = rows[:, start : start + lanes]
        if start < key_end:
            block = turn(block, cos_table, sin_table)
        if start < query_width:
            q_ref[:, start : start + lanes] = block.astype(bf16)
        else:
            kv_ref[:, start - query_width : start - query_width + lanes] = block.astype(bf16)


def qkv_rows(x, p, cos_table, sin_table, kv_width):
    rows, width = x.shape
    total = p.qkv.shape[1]
    query_width = total - 2 * kv_width
    return call(
        qkv_kernel,
        [shape(rows, width, bf16), shape(rows, query_width, bf16), shape(rows, 2 * kv_width, bf16)],
        [x, p.gain_one, p.qkv, p.bias, cos_table, sin_table],
        flops=2 * rows * width * total,
    )


def pair_rows(block, pair, group):
    swapped = pltpu.roll(block, HEAD, 1)
    low = lane_of(block) < HEAD
    rows = []
    for side in range(2):
        key_head = (2 * pair + side) // group
        here = block if key_head == side else swapped
        rows.append(jnp.where(low == (key_head == 0), here, 0.0))
    return jnp.concatenate(rows).astype(bf16)


def pair_columns(block, pair, group):
    count = block.shape[1] // 2
    parts = []
    for side in range(2):
        start = (2 * pair + side) // group * HEAD
        parts.append(block[start : start + HEAD, side * count : (side + 1) * count])
    return jnp.concatenate(parts).T


def pair_terms(keys, query_pair, bias):
    scores = matmul_nt(keys, query_pair) + jnp.concatenate([bias, bias], axis=1)
    terms = jnp.exp(scores - jnp.max(scores, axis=0, keepdims=True))
    return terms, 1.0 / jnp.sum(terms, axis=0, keepdims=True)


def lay_keys(refs, keys, values):
    count = refs[0].shape[0] * refs[0].shape[1]
    for i, ref in enumerate(refs):
        rows = ref[...].reshape(count, ref.shape[2])
        keys[i * count : (i + 1) * count] = rows[:, :lanes]
        values[i * count : (i + 1) * count] = rows[:, lanes:]


def attend_kernel(
    group,
    q_ref,
    kva_ref,
    kvb_ref,
    bias_ref,
    x_ref,
    wo_ref,
    gain_ref,
    att_ref,
    res_ref,
    mix_ref,
    keys,
    values,
):
    lay_keys((kva_ref, kvb_ref), keys, values)
    values_turned = values[...].T
    bias = bias_ref[...]
    for pair in range(q_ref.shape[1] // lanes):
        place = slice(pair * lanes, (pair + 1) * lanes)
        query_pair = pair_rows(q_ref[:, place].astype(f32) * HEAD**-0.5, pair, group)
        terms, inverse = pair_terms(keys[...], query_pair, bias)
        output = matmul(values_turned, terms.astype(bf16)) * inverse
        att_ref[:, place] = pair_columns(output, pair, group).astype(bf16)

    residual = x_ref[...].astype(f32) + matmul(att_ref[...], wo_ref[...])
    res_ref[...] = residual
    mix_ref[...] = (residual * inverse_rms(residual) * gain_ref[...].astype(f32)).astype(bf16)


def attend(queries, kva, kvb, bias, x, p, turn_of):
    rows, width = queries.shape
    total = bias.shape[0]
    kv_width = kva.shape[-1] // 2
    group = width // kv_width
    flops = 4 * rows * total * width * 4 + 2 * rows * width * x.shape[1]
    return call(
        functools.partial(attend_kernel, group),
        [shape(rows, width, bf16), shape(*x.shape, f32), shape(*x.shape, bf16)],
        [queries, kva, kvb, bias, x, p.out, turn_of(p.gain_two)],
        scratch=[pltpu.VMEM((total, lanes), bf16)] * 2,
        flops=flops,
    )


def norm_back(values, gain, grad):
    inverse = inverse_rms(values)
    unit = values * inverse
    scaled = grad * gain
    back = inverse * (scaled - unit * jnp.mean(scaled * unit, axis=-1, keepdims=True))
    return back, jnp.sum(grad * unit, axis=0, keepdims=True)


def attend_back_kernel(
    group,
    q_ref,
    kva_ref,
    kvb_ref,
    bias_ref,
    mix_low_ref,
    mix_got_ref,
    res_ref,
    gain_ref,
    up_ref,
    wo_ref,
    cos_ref,
    sin_ref,
    dq_ref,
    dkva_ref,
    dkvb_ref,
    gres_ref,
    gatt_ref,
    gain_two_ref,
    keys,
    values,
    queries,
    grads,
    all_probs,
    all_scores,
):
    lay_keys((kva_ref, kvb_ref), keys, values)
    grad_mixing = mix_low_ref[...] + mix_got_ref[...].astype(f32)
    back, gain_two = norm_back(res_ref[...], gain_ref[...].astype(f32), grad_mixing)
    gain_two_ref[...] = gain_two
    grad_residual = up_ref[...].astype(f32) + back
    gres_ref[...] = grad_residual
    grad_attended = grad_residual.astype(bf16)
    gatt_ref[...] = grad_attended
    grad_out = matmul_nt(grad_attended, wo_ref[...]).astype(bf16).astype(f32)
    bias = bias_ref[...]
    pairs = q_ref.shape[1] // lanes
    both = 2 * q_ref.shape[0]
    for pair in range(pairs):
        place = slice(pair * lanes, (pair + 1) * lanes)
        rows = slice(pair * both, (pair + 1) * both)
        query_pair = pair_rows(q_ref[:, place].astype(f32) * HEAD**-0.5, pair, group)
        grad_pair = pair_rows(grad_out[:, place], pair, group)
        queries[rows] = query_pair
        grads[rows] = grad_pair
        terms, inverse = pair_terms(keys[...], query_pair, bias)
        probs = terms * inverse
        all_probs[:, rows] = probs.astype(bf16)
        grad_probs = matmul_nt(values[...], grad_pair)
        delta = jnp.sum(probs * grad_probs, axis=0, keepdims=True)
        all_scores[:, rows] = (probs * (grad_probs - delta)).astype(bf16)

    grad_values = matmul(all_probs[...], grads[...]).astype(bf16)
    grad_keys = matmul(all_scores[...], queries[...]).astype(bf16)
    count = dkva_ref.shape[0]
    for i, ref in enumerate((dkva_ref, dkvb_ref)):
        ref[:, :lanes] = grad_keys[i * count : (i + 1) * count]
        ref[:, lanes:] = grad_values[i * count : (i + 1) * count]
    keys_turned = keys[...].T
    cos_table, sin_table = cos_ref[...], -sin_ref[...]
    for pair in range(pairs):
        place = slice(pair * lanes, (pair + 1) * lanes)
        turned = matmul(keys_turned, all_scores[:, pair * both : (pair + 1) * both])
        grad_query = pair_columns(turned, pair, group) * HEAD**-0.5
        dq_ref[:, place] = turn(grad_query, cos_table, sin_table).astype(bf16)


def attend_back(
    queries, kva, kvb, bias, mix_low, mix_got, residual, upstream, p, cos_table, sin_table
):
    rows, width = queries.shape
    total = bias.shape[0]
    kv_width = kva.shape[-1] // 2
    group = width // kv_width
    flops = 10 * rows * total * width * 3 + 2 * rows * width * residual.shape[1]
    return call(
        functools.partial(attend_back_kernel, group),
        [
            shape(rows, width, bf16),
            shape(total // 2, 2 * kv_width, bf16),
            shape(total // 2, 2 * kv_width, bf16),
            shape(*residual.shape, f32),
            shape(*residual.shape, bf16),
            shape(1, residual.shape[1], f32),
        ],
        [
            queries,
            kva,
            kvb,
            bias,
            mix_low,
            mix_got,
            residual,
            p.gain_two,
            upstream,
            p.out,
            cos_table,
            sin_table,
        ],
        scratch=[
            pltpu.VMEM((total, lanes), bf16),
            pltpu.VMEM((total, lanes), bf16),
            pltpu.VMEM((rows * width // HEAD, lanes), bf16),
            pltpu.VMEM((rows * width // HEAD, lanes), bf16),
            pltpu.VMEM((total, rows * width // HEAD), bf16),
            pltpu.VMEM((total, rows * width // HEAD), bf16),
        ],
        flops=flops,
        vmem=6,
    )


def qkv_back_kernel(
    dq_ref,
    low_ref,
    got_ref,
    cos_ref,
    sin_ref,
    w_ref,
    x_ref,
    gain_ref,
    gres_ref,
    dqkv_ref,
    gin_ref,
    gin_low_ref,
    gain_one_ref,
    bias_ref,
):
    query_width = dq_ref.shape[1]
    grad_kv = low_ref[...] + got_ref[...].astype(f32)
    dqkv_ref[:, :query_width] = dq_ref[...]
    grad_key = turn(grad_kv[:, :lanes], cos_ref[...], -sin_ref[...])
    dqkv_ref[:, query_width : query_width + lanes] = grad_key.astype(bf16)
    dqkv_ref[:, query_width + lanes :] = grad_kv[:, lanes:].astype(bf16)
    dqkv = dqkv_ref[...]
    bias_ref[...] = jnp.sum(dqkv.astype(f32), axis=0, keepdims=True)
    grad_normed = matmul_nt(dqkv, w_ref[...])
    back, gain_one = norm_back(x_ref[...].astype(f32), gain_ref[...].astype(f32), grad_normed)
    gain_one_ref[...] = gain_one
    grad_in = gres_ref[...] + back
    gin_ref[...] = grad_in
    gin_low_ref[...] = grad_in.astype(bf16)


def qkv_back(dq, low, got, x, grad_residual, p, cos_table, sin_table):
    rows, width = x.shape
    total = p.qkv.shape[1]
    return call(
        qkv_back_kernel,
        [
            shape(rows, total, bf16),
            shape(rows, width, f32),
            shape(rows, width, bf16),
            shape(1, width, f32),
            shape(1, total, f32),
        ],
        [dq, low, got, cos_table, sin_table, p.qkv, x, p.gain_one, grad_residual],
        flops=2 * rows * width * total,
    )


def chunk_of(size):
    return 256 if size % 256 == 0 else 128


def ffn_kernel(lower_ref, upper_ref, wg_ref, wu_ref, wd_ref, low_ref, up_ref, hid_ref, g_ref, u_ref, rows, total):
    n = pl.program_id(0)
    half = rows.shape[0] // 2

    @pl.when(n == 0)
    def _():
        rows[:half] = lower_ref[...].reshape(half, rows.shape[1])
        rows[half:] = upper_ref[...].reshape(half, rows.shape[1])
        total[...] = jnp.zeros_like(total)

    gate = matmul(rows[...], wg_ref[...])
    up = matmul(rows[...], wu_ref[...])
    hidden = (gate * (1.0 / (1.0 + jnp.exp(-gate))) * up).astype(bf16)
    hid_ref[...] = hidden
    g_ref[...] = gate.astype(bf16)
    u_ref[...] = up.astype(bf16)
    total[...] += matmul(hidden, wd_ref[...])

    @pl.when(n == pl.num_programs(0) - 1)
    def _():
        low_ref[...] = total[:half].astype(bf16)
        up_ref[...] = total[half:].astype(bf16)


def ffn(lower, upper, p):
    half, width = lower.shape
    wide = p.gate.shape[1]
    chunk = wide
    rows = half + upper.shape[0]
    whole = pl.BlockSpec((half, width), lambda n: (0, 0))
    columns = pl.BlockSpec((width, chunk), lambda n: (0, n))
    return call(
        ffn_kernel,
        [shape(half, width, bf16), shape(rows - half, width, bf16)] + [shape(rows, wide, bf16)] * 3,
        [lower, upper, p.gate, p.up, p.down],
        scratch=[pltpu.VMEM((rows, width), bf16), pltpu.VMEM((rows, width), f32)],
        flops=6 * rows * width * wide,
        vmem=6,
        grid=(wide // chunk,),
        in_specs=[whole, whole, columns, columns, pl.BlockSpec((chunk, width), lambda n: (n, 0))],
        out_specs=[whole, whole] + [pl.BlockSpec((rows, chunk), lambda n: (0, n))] * 3,
    )


def ffn_back_kernel(
    lower_ref, upper_ref, g_ref, u_ref, wg_ref, wu_ref, wd_ref, low_ref, up_ref, gg_ref, gu_ref, rows, total
):
    n = pl.program_id(0)
    half = rows.shape[0] // 2

    @pl.when(n == 0)
    def _():
        rows[:half] = lower_ref[...].reshape(half, rows.shape[1])
        rows[half:] = upper_ref[...].reshape(half, rows.shape[1])
        total[...] = jnp.zeros_like(total)

    grad_hidden = matmul_nt(rows[...], wd_ref[...])
    gate = g_ref[...].astype(f32)
    up = u_ref[...].astype(f32)
    sigmoid = 1.0 / (1.0 + jnp.exp(-gate))
    grad_up = (grad_hidden * gate * sigmoid).astype(bf16)
    grad_gate = (grad_hidden * up * sigmoid * (1.0 + gate * (1.0 - sigmoid))).astype(bf16)
    gg_ref[...] = grad_gate
    gu_ref[...] = grad_up
    total[...] += matmul_nt(grad_gate, wg_ref[...]) + matmul_nt(grad_up, wu_ref[...])

    @pl.when(n == pl.num_programs(0) - 1)
    def _():
        low_ref[...] = total[:half].astype(bf16)
        up_ref[...] = total[half:].astype(bf16)


def ffn_back(lower, upper, gate, up, p):
    half, width = gate.shape[0] // 2, lower.shape[-1]
    wide = p.gate.shape[1]
    chunk = wide
    rows = 2 * half
    whole = pl.BlockSpec((half, width), lambda n: (0, 0))
    columns = pl.BlockSpec((width, chunk), lambda n: (0, n))
    inner = pl.BlockSpec((rows, chunk), lambda n: (0, n))
    return call(
        ffn_back_kernel,
        [shape(half, width, bf16), shape(rows - half, width, bf16)] + [shape(rows, wide, bf16)] * 2,
        [lower, upper, gate, up, p.gate, p.up, p.down],
        scratch=[pltpu.VMEM((rows, width), bf16), pltpu.VMEM((rows, width), f32)],
        flops=6 * rows * width * wide,
        vmem=6,
        grid=(wide // chunk,),
        in_specs=[
            whole,
            whole,
            inner,
            inner,
            columns,
            columns,
            pl.BlockSpec((chunk, width), lambda n: (n, 0)),
        ],
        out_specs=[whole, whole, inner, inner],
    )


def rows_of(ref):
    return ref[...].reshape(-1, ref.shape[-1])


def turn_rows(refs, turned):
    start = 0
    for ref in refs:
        turned[:, start : start + ref.shape[0]] = ref[...].T
        start += ref.shape[0]


def stack_rows(refs):
    return jnp.concatenate([rows_of(ref) for ref in refs])


def split_halves(info_ref, spread, result, keep_at, send_at):
    half = result.shape[0] // (2 * spread)
    for core in range(2):

        @pl.when(info_ref[0] == core)
        def _(core=core):
            for j in range(spread):
                for ref_at, whose in ((keep_at, core), (send_at, 1 - core)):
                    start = (2 * j + whose) * half
                    ref_at(j, result[start : start + half].astype(bf16))


def gate_up_product_kernel(lefts, spread, info_ref, *refs):
    left_refs, refs = refs[:lefts], refs[lefts:]
    keep_ref, send_ref, turned = refs[-3:]
    rights = refs[:-3]
    turn_rows(left_refs, turned)
    me = info_ref[1]
    count = len(rights) // 2
    for n in range(2):
        right = stack_rows(rights[n * count : (n + 1) * count])
        width = right.shape[1]
        for start in range(0, width, 512):
            place = slice(start, min(start + 512, width))
            result = matmul(turned[...], right[:, place])

            def keep_at(j, block, n=n, place=place):
                keep_ref[j ^ me, n, :, place] = block

            def send_at(j, block, n=n, place=place):
                send_ref[j ^ me, n, :, place] = block

            split_halves(info_ref, spread, result, keep_at, send_at)


def gate_up_product(info, lefts, gates, ups, spread):
    depth = sum(left.size // left.shape[-1] for left in lefts)
    height, width = lefts[0].shape[-1], gates[0].shape[1]
    out = shape(spread, 2, height // (2 * spread), width, bf16)
    return call(
        functools.partial(gate_up_product_kernel, len(lefts), spread),
        [out, out],
        [info] + list(lefts) + list(gates) + list(ups),
        scratch=[pltpu.VMEM((height, depth), bf16)],
        flops=4 * depth * height * width,
        vmem=8,
    )


def down_product_kernel(lefts, info_ref, *refs):
    left_refs, rights = refs[:lefts], refs[lefts:-3]
    keep_ref, send_ref, turned = refs[-3:]
    turn_rows(left_refs, turned)
    middle = keep_ref.shape[0]
    result = matmul(turned[: 2 * middle], stack_rows(rights))
    for core in range(2):

        @pl.when(info_ref[0] == core)
        def _(core=core):
            keep_ref[...] = result[core * middle : (core + 1) * middle].astype(bf16)
            send_ref[...] = result[(1 - core) * middle : (2 - core) * middle].astype(bf16)


def down_product(info, lefts, rights, rows):
    depth = sum(left.size // left.shape[-1] for left in lefts)
    height, width = lefts[0].shape[-1], rights[0].shape[-1]
    return call(
        functools.partial(down_product_kernel, len(lefts)),
        [shape(rows // 2, width, bf16)] * 2,
        [info] + list(lefts) + list(rights),
        scratch=[pltpu.VMEM((height, depth), bf16)],
        flops=2 * depth * height * width,
    )


def attn_product_kernel(count, spread, info_ref, *refs):
    normed, grad_qkv, attended, grad_attended = [
        refs[n * count : (n + 1) * count] for n in range(4)
    ]
    vector_ref, keep_ref, send_ref, turned = refs[4 * count :]
    start = 0
    for lefts, rights in ((normed, grad_qkv), (attended, grad_attended), (None, None)):
        if lefts:
            turn_rows(lefts, turned)
            result = matmul(turned[...], stack_rows(rights))
        else:
            rows = vector_ref[...]
            fill = jnp.zeros((lanes - rows.shape[0], rows.shape[1]), f32)
            result = jnp.concatenate([rows, fill]).T
        place = slice(start, start + result.shape[1])
        start += result.shape[1]

        def keep_at(j, block, place=place):
            keep_ref[info_ref[2 + j], :, place] = block

        def send_at(j, block, place=place):
            send_ref[info_ref[2 + spread + j], :, place] = block

        split_halves(info_ref, spread, result, keep_at, send_at)


def attn_product(info, normed, grad_qkv, attended, grad_attended, vectors, spread):
    depth = sum(part.shape[0] for part in normed)
    width = normed[0].shape[1]
    total = grad_qkv[0].shape[1] + grad_attended[0].shape[1] + lanes
    out = shape(spread, width // (2 * spread), total, bf16)
    return call(
        functools.partial(attn_product_kernel, len(normed), spread),
        [out, out],
        [info] + list(normed) + list(grad_qkv) + list(attended) + list(grad_attended) + [vectors],
        scratch=[pltpu.VMEM((width, depth), bf16)],
        flops=2 * depth * width * total,
    )


def pack_attn_kernel(info_ref, *refs):
    keep_ref, send_ref = refs[-2:]
    half = keep_ref.shape[0]
    for core in range(2):

        @pl.when(info_ref[0] == core)
        def _(core=core):
            start = 0
            for ref in refs[:-2]:
                place = slice(start, start + ref.shape[1])
                start += ref.shape[1]
                keep_ref[:, place] = ref[core * half : (core + 1) * half]
                send_ref[:, place] = ref[(1 - core) * half : (2 - core) * half]


def pack_attn(info, parts):
    out = shape(parts[0].shape[0] // 2, sum(part.shape[1] for part in parts), bf16)
    return call(pack_attn_kernel, [out, out], [info] + parts)


def pack_gate_up_kernel(spread, info_ref, gate_ref, up_ref, keep_ref, send_ref):
    me = info_ref[1]
    half, columns = keep_ref.shape[2:]
    for core in range(2):

        @pl.when(info_ref[0] == core)
        def _(core=core):
            for n, ref in enumerate((gate_ref, up_ref)):
                for j in range(spread):
                    block = ref[:, j * columns : (j + 1) * columns]
                    keep_ref[j ^ me, n] = block[core * half : (core + 1) * half]
                    send_ref[j ^ me, n] = block[(1 - core) * half : (2 - core) * half]


def pack_gate_up(info, gate, up, spread):
    out = shape(spread, 2, gate.shape[0] // 2, gate.shape[1] // spread, bf16)
    return call(
        functools.partial(pack_gate_up_kernel, spread), [out, out], [info, gate, up]
    )


def lay_attn_kernel(edges, at_ref, *refs):
    parts, outs = refs[:4], refs[4:]
    half = outs[0].shape[1]
    n = 0
    for ref in parts:
        for start in range(0, ref.shape[0], half):
            block = ref[start : start + half]
            for out, (low, high) in zip(outs, edges):
                out[at_ref[n]] = block[:, low:high]
            n += 1


def lay_attn(at, parts, half, edges):
    count = at.shape[0]
    outs = [shape(count, half, high - low, bf16) for low, high in edges]
    got = call(functools.partial(lay_attn_kernel, edges), outs, [at] + parts)
    return [part.reshape(count * half, -1) for part in got]


def lay_gate_up_kernel(at_ref, *refs):
    parts, outs = refs[:-2], refs[-2:]
    for i, ref in enumerate(parts):
        for n, out in enumerate(outs):
            columns = ref.shape[2]
            out[at_ref[i], :, :columns] = ref[n]
            if columns < out.shape[2]:
                rest = (out.shape[1], out.shape[2] - columns)
                out[at_ref[i], :, columns:] = jnp.zeros(rest, bf16)


def lay_gate_up(at, parts, wide):
    half = parts[0].shape[1]
    outs = [shape(len(parts), half, wide, bf16)] * 2
    got = call(lay_gate_up_kernel, outs, [at] + parts)
    return [part.reshape(len(parts) * half, wide) for part in got]


def spread_kernel(spread, info_ref, *refs):
    gate_ref, up_ref = refs[-2:]
    count = (len(refs) - 2) // 2
    per = spread // count
    me = info_ref[1]
    half = refs[0].shape[2]
    columns = gate_ref.shape[1] // spread
    for core in range(2):

        @pl.when(info_ref[0] == core)
        def _(core=core):
            for i in range(spread):
                for parts, whose in ((refs[:count], core), (refs[count:-2], 1 - core)):
                    for n, out in enumerate((gate_ref, up_ref)):
                        block = parts[i // per][i % per, n][:, :columns].astype(f32)
                        for j in range(spread):

                            @pl.when((i ^ me) == j)
                            def _(j=j, block=block, whose=whose, out=out):
                                place = slice(j * columns, (j + 1) * columns)
                                out[whose * half : (whose + 1) * half, place] = block


def spread_gate_up(info, mine, theirs, columns, spread):
    half = mine[0].shape[2]
    out = shape(2 * half, spread * columns, f32)
    return call(
        functools.partial(spread_kernel, spread), [out, out], [info] + list(mine) + list(theirs)
    )


def local(
    tokens,
    doc_starts,
    cotangent,
    norm_one,
    w_query,
    b_query,
    w_key,
    b_key,
    w_value,
    b_value,
    w_out,
    norm_two,
    w_gate,
    w_up,
    w_down,
):
    core = lax.axis_index("section")
    cores = lax.axis_size("section")
    spread = lax.axis_size("dp")
    micro_count, _, row_count, width = tokens.shape
    layers = range(2)
    share = row_count // cores
    shard = w_query.shape[1]
    half = shard // 2
    query_width = w_query.shape[2]
    kv_width = w_key.shape[2]
    ff = w_gate.shape[2]
    slice_ff = ff // spread

    me = lax.axis_index("dp")
    wide = -(-slice_ff // lanes) * lanes
    edge = query_width + 2 * kv_width
    per = kv_width // spread

    def order_of(mine):
        masks = step_masks("dp")

        def place(j, core):
            return sum(
                jnp.where(((me ^ j) & pair[core]) != 0, 1 << n, 0) for n, pair in enumerate(masks)
            )

        first, second = (0, 1) if mine else (1, 0)
        return [by_section(place(j, first), place(j, second)) for j in range(spread)]

    def owner(block, mine):
        first, second = (0, 1) if mine else (1, 0)
        masks = [distance(block, "dp", first), distance(block, "dp", second)]
        return me ^ by_section(*masks)

    info = jnp.stack([core, me] + order_of(True) + order_of(False)).astype(jnp.int32)
    attn_at = jnp.stack(
        [
            2 * owner(block, mine) + (core if mine else 1 - core)
            for mine in (True, False)
            for block in range(spread)
        ]
    ).astype(jnp.int32)
    gate_up_at = jnp.stack(
        [2 * (me ^ mask) + whose for whose in (core, 1 - core) for mask in range(spread)]
    ).astype(jnp.int32)

    def column(vector):
        return jnp.pad(vector, (0, shard - vector.shape[0]))

    vectors = jnp.stack(
        [norm_one[0], norm_two[0], b_query[0], column(b_key[0]), column(b_value[0])], axis=1
    )
    vectors = jnp.pad(vectors, ((0, 0), (0, lanes - vectors.shape[1])))

    def per_layer(keep, send):
        got = other(send)
        return by_section(keep, got), by_section(got, keep)

    attn_halves = per_layer(
        *pack_attn(info, [w_query[0], w_key[0], w_value[0], w_out[0], vectors])
    )
    gate_up_halves = per_layer(*pack_gate_up(info, w_gate[0], w_up[0], spread))
    down_other = other(w_down[0])
    downs = by_section(w_down[0], down_other), by_section(down_other, w_down[0])

    params = [SimpleNamespace(), SimpleNamespace()]
    clock, flows, last, pins = [0], [], [], []

    class Flow:
        def __init__(self, steps, slack):
            self.steps, self.slack = steps, slack
            self.move()
            flows.append(self)

        def move(self):
            self.value = next(self.steps, None)
            self.due = clock[0] + self.slack

        def finish(self):
            while self.value is not None:
                self.move()

    def turn_of(value):
        clock[0] += 1
        for flow in list(flows):
            if flow.value is not None and flow.due <= clock[0]:
                pins.append(flow.value)
                flow.move()
            if flow.value is None:
                flows.remove(flow)
        wait = last + pins
        pins.clear()
        return after(value, wait) if wait else value

    def done(value):
        last[:] = [value]

    def weights_steps(layer, part, blocks):
        p = params[layer]
        parts = []
        yield from gather_steps(part, "dp", lambda *got: parts.extend(got))
        blocks = after(blocks, parts[1])
        qkv, out, small = lay_attn(
            attn_at,
            parts + [other(part) for part in parts],
            half,
            ((0, edge), (edge, edge + width), (edge + width, edge + width + lanes)),
        )
        rows = small.T
        p.qkv, p.out = qkv, out
        p.gain_one, p.gain_two = rows[0:1], rows[1:2]
        key_bias, value_bias = [
            rows[n].reshape(spread, shard)[:, :per].reshape(1, -1) for n in (3, 4)
        ]
        p.bias = jnp.concatenate([rows[2:3], key_bias, value_bias], axis=1)
        blocks = [blocks[0]] + [direct(blocks[mask], "dp", mask) for mask in range(1, spread)]
        yield blocks
        yield blocks
        blocks = blocks + [other(block) for block in blocks]
        blocks, down = after((blocks, downs[layer]), list(last))
        p.gate, p.up = lay_gate_up(gate_up_at, blocks, wide)
        p.down = jnp.pad(down, ((0, wide - slice_ff), (0, 0)))

    first = core * share
    place = lax.axis_index("ctx")
    places = place * row_count + first + jnp.arange(share, dtype=jnp.int32)
    my_tokens = lax.dynamic_slice_in_dim(tokens[:, 0], first, share, 1)
    my_cotangent = lax.dynamic_slice_in_dim(cotangent[:, 0], first, share, 1)
    key_places = jnp.concatenate(
        [
            (place ^ block) * row_count + whose * share + jnp.arange(share, dtype=jnp.int32)
            for whose in (core, 1 - core)
            for block in range(lax.axis_size("ctx"))
        ]
    )
    starts = doc_starts[:, 0, None, :]
    begins = jnp.max(jnp.where(starts <= places[None, :, None], starts, 0), axis=2)
    places_all = jnp.tile(places, micro_count)
    cos_all, sin_all = tables(begins.reshape(-1), places_all)
    visible = (key_places[None, :, None] <= places[None, None, :]) & (
        key_places[None, :, None] >= begins[:, None, :]
    )
    bias_all = jnp.where(visible, 0.0, masked).astype(f32)
    context = [
        (
            Part(bias_all, 0, n),
            Part(cos_all.reshape(micro_count, share, lanes), 0, n),
            Part(sin_all.reshape(micro_count, share, lanes), 0, n),
        )
        for n in range(micro_count)
    ]

    kept = [[SimpleNamespace() for _ in range(micro_count)] for _ in layers]
    for n in range(micro_count):
        kept[1][n].above = Part(my_cotangent, 0, n)
    def kv_steps(ks, kv):
        def give(*parts):
            whole = jnp.concatenate(parts)
            theirs = other(whole)
            for n, k in enumerate(ks):
                k.kva, k.kvb = [
                    Part(part.reshape(-1, len(ks), share, 2 * kv_width), 1, n)
                    for part in (whole, theirs)
                ]

        yield from gather_steps(kv[None], "ctx", give)

    def run_q_all():
        flow = Flow(weights_steps(0, attn_halves[0], gate_up_halves[0]), weight_slack)
        while not hasattr(params[0], "qkv"):
            flow.move()
        kept[0][0].weights = flow
        tokens_in = turn_of(my_tokens.reshape(-1, width))
        rows = qkv_rows(tokens_in, params[0], cos_all, sin_all, kv_width)
        done(rows[0])
        normed, queries = [part.reshape(micro_count, share, -1) for part in rows[:2]]
        for n in range(micro_count):
            k = kept[0][n]
            k.x, k.normed, k.queries = [
                Part(part, 0, n) for part in (my_tokens, normed, queries)
            ]
        flow = Flow(kv_steps(kept[0], rows[2]), 1)
        for n in range(micro_count):
            kept[0][n].kv = flow
        halves = after((attn_halves[1], gate_up_halves[1]), list(last))
        kept[1][0].weights = Flow(weights_steps(1, *halves), 1)

    def run_q(n):
        k = kept[1][n]
        kept[0][n].scatter.finish()
        while not hasattr(params[1], "qkv"):
            kept[1][0].weights.move()
        k.x = turn_of(kept[0][n].result)
        k.normed, k.queries, kv = qkv_rows(k.x, params[1], *context[n][1:], kv_width)
        done(k.normed)
        k.kv = Flow(kv_steps([k], kv), 2)

    def run_a(layer, n):
        k, p = kept[layer][n], params[layer]
        k.kv.finish()
        k.attended, k.residual, mixing = attend(
            k.queries, k.kva, k.kvb, context[n][0], k.x, p, turn_of
        )
        done(mixing)
        k.gather = Flow(gather_steps(mixing, "dp", lambda *got: k.__dict__.update(mixing=got)), 2)

    def run_f(layer, n):
        k, p = kept[layer][n], params[layer]
        k.gather.finish()
        kept[layer][0].weights.finish()
        lower, upper = k.mixing
        part_low, part_up, k.hidden, k.gate, k.up = ffn(lower, turn_of(upper), p)
        done(k.gate)

        def give(low, got):
            k.result = (k.residual + low + got.astype(f32)).astype(bf16)

        k.scatter = Flow(scatter_steps(part_low, part_up, "dp", give), 2 if layer == 0 else 6)
        if layer:
            k.after = k.scatter

    def run_c():
        def give(*parts):
            for n in range(micro_count):
                kept[1][n].grad_ffn = [
                    Part(part.reshape(-1, micro_count, share, width), 1, n) for part in parts
                ]

        rows = after(my_cotangent[None], last)
        kept[1][0].cotangent = Flow(gather_steps(rows, "dp", give), 4)

    def run_d(layer, n):
        k, p = kept[layer][n], params[layer]
        if layer:
            kept[1][0].cotangent.finish()
        else:
            k.gather.finish()
        lower, upper = k.grad_ffn
        part_low, part_up, k.grad_gate, k.grad_up = ffn_back(
            lower, upper, turn_of(k.gate), k.up, p
        )
        done(k.grad_gate)
        k.scatter = Flow(
            scatter_steps(part_low, part_up, "dp", lambda *got: k.__dict__.update(scattered=got)), 2
        )

    def run_b(layer, n):
        k, p = kept[layer][n], params[layer]
        k.scatter.finish()
        bias, cos_table, sin_table = context[n]
        low, got = k.scattered
        k.dq, dkva, dkvb, k.grad_residual, k.grad_attended, k.gain_two = attend_back(
            k.queries,
            k.kva,
            k.kvb,
            bias,
            low,
            turn_of(got),
            k.residual,
            k.above,
            p,
            cos_table,
            sin_table,
        )
        done(k.dq)
        pair = dkva.astype(f32) + other(dkvb).astype(f32)
        middle = pair.shape[0] // 2
        k.scatter = Flow(
            scatter_steps(
                pair[:middle], pair[middle:], "ctx", lambda *got: k.__dict__.update(grad_kv=got)
            ),
            2,
        )

    def run_k(layer, n):
        k, p = kept[layer][n], params[layer]
        k.scatter.finish()
        low, got = k.grad_kv
        k.grad_qkv, k.grad_in, grad_low, k.gain_one, k.bias = qkv_back(
            k.dq, low, turn_of(got), k.x, k.grad_residual, p, *context[n][1:]
        )
        done(k.grad_qkv)
        if layer:
            below = kept[0][n]
            below.above = k.grad_in
            below.gather = Flow(
                gather_steps(grad_low, "dp", lambda *got: below.__dict__.update(grad_ffn=got)), 2
            )

    ends = (place == 0) | (place == 3)
    hops = [[(0, 1), (3, 2)], [(1, 2), (2, 1)], [(1, 0), (2, 3)]]
    sums = {}

    def ctx_steps(name, value):
        for hop, route in enumerate(hops):
            got = lax.ppermute(value, "ctx", route)
            yield got
            if hop == 2:
                sums[name] = jnp.where(ends, got, value)
            else:
                value = (value.astype(f32) + got.astype(f32)).astype(bf16)

    waiting, moving, exchanges = {}, [], {}

    def tick(*names):
        for flow in list(moving):
            pins.append(flow.value)
            flow.move()
            if flow.value is None:
                moving.remove(flow)
        for name in names:
            if name not in waiting:
                exchanges.pop(name).finish()
            moving.append(Flow(ctx_steps(name, waiting.pop(name)), 1000))

    def column_of(layer, name):
        return [getattr(k, name) for k in kept[layer]]

    def parts_of(layer, name):
        return [part for k in kept[layer] for part in getattr(k, name)]

    def over_cores(keep, send):
        return keep.astype(f32) + other(send).astype(f32)

    def run_pd(layer):
        hidden = column_of(layer, "hidden")
        hidden[0] = turn_of(hidden[0])
        keep, send = down_product(info, hidden, parts_of(layer, "grad_ffn"), slice_ff)
        done(keep)
        waiting["down", layer] = over_cores(keep, send).astype(bf16)

    def run_pg(layer):
        grads = column_of(layer, "grad_gate")
        grads[0] = turn_of(grads[0])
        keep, send = gate_up_product(
            info, parts_of(layer, "mixing"), grads, column_of(layer, "grad_up"), spread
        )
        done(keep)
        blocks = over_cores(keep, send).astype(bf16)
        before = kept[layer][micro_count - 1].scatter.value

        def steps():
            sent = after(blocks, before) if before is not None else blocks
            parts = [sent[0]] + [direct(sent[mask], "dp", mask) for mask in range(1, spread)]
            yield parts[1:]
            middle = spread // 2
            waiting["low", layer] = jnp.stack(parts[:middle])
            waiting["high", layer] = jnp.stack(parts[middle:])

        exchanges["low", layer] = Flow(steps(), 3)

    def run_pa(layer):
        bias = sum(column_of(layer, "bias"))[0]

        def column_sum(vector):
            return jnp.pad(vector.reshape(spread, -1), ((0, 0), (0, shard - per))).reshape(-1)

        vectors = jnp.stack(
            [
                sum(column_of(layer, "gain_one"))[0],
                sum(column_of(layer, "gain_two"))[0],
                bias[:query_width],
                column_sum(bias[query_width : query_width + kv_width]),
                column_sum(bias[query_width + kv_width :]),
            ]
            + [jnp.zeros((width,), f32)] * 3
        )
        keep, send = attn_product(
            info,
            column_of(layer, "normed"),
            column_of(layer, "grad_qkv"),
            column_of(layer, "attended"),
            column_of(layer, "grad_attended"),
            turn_of(vectors),
            spread,
        )
        done(keep)
        attn = over_cores(keep, send).reshape(spread * half, -1)


        def give(low, got):
            waiting["attn", layer] = (low + got.astype(f32)).astype(bf16)

        exchanges["attn", layer] = Flow(scatter_steps(*jnp.split(attn, 2), "dp", give), 2)

    steps = dict(
        q=run_q,
        a=run_a,
        f=run_f,
        c=run_c,
        d=run_d,
        b=run_b,
        k=run_k,
        D=run_pd,
        G=run_pg,
        P=run_pa,
    )
    run_q_all()
    names = dict(d="down", l="low", h="high", a="attn")
    for word in order:
        if word[0] == "z":
            tick(*[(names[word[n]], int(word[n + 1])) for n in range(1, len(word), 2)])
        else:
            steps[word[0]](*[int(digit) for digit in word[1:]])
    while moving:
        tick()
    for k in kept[1]:
        if not hasattr(k, "result"):
            k.after.finish()

    section_out = both_rows([jnp.stack(column_of(layer, "result")) for layer in layers])
    section_grad = both_rows([jnp.stack(column_of(layer, "grad_in")) for layer in layers])

    final = [[sums[name, layer] for name in ("attn", "low", "high", "down")] for layer in layers]
    mine = [by_section(*pair) for pair in zip(*final)]
    theirs = [other(by_section(*pair[::-1])) for pair in zip(*final)]
    gate, up = spread_gate_up(info, mine[1:3], theirs[1:3], slice_ff, spread)

    def in_order(mine, theirs):
        return by_section(
            jnp.concatenate([mine, theirs]), jnp.concatenate([theirs, mine])
        ).astype(f32)

    attn = in_order(*after((mine[0], theirs[0]), gate))
    down = in_order(mine[3], theirs[3])
    small = attn[:, edge + width :]
    return (
        section_out,
        section_grad,
        small[None, :, 0],
        attn[None, :, :query_width],
        small[None, :, 2],
        attn[None, :, query_width : query_width + kv_width],
        small[None, :per, 3],
        attn[None, :, query_width + kv_width : edge],
        small[None, :per, 4],
        attn[None, :, edge : edge + width],
        small[None, :, 1],
        gate[None],
        up[None],
        down[None],
    )


weight_slack = 2
order = (
    "a00", "a01", "f00", "a02", "f01", "q0", "f02", "q1", "a10", "q2", "a11", "c", "f10", "a12", "f11", "d10",
    "f12", "d11", "b10", "d12", "D1", "zd1", "G1", "b11", "z", "k10", "b12", "zl1", "k11", "d00", "zh1",
    "k12", "d01", "z", "P1", "d02", "D0", "zd0a1", "G0", "b00", "zl0", "b01", "zh0", "k00", "b02", "z", "k01",
    "k02", "z", "P0", "za0",
)


def both_rows(per_layer):
    first, second = per_layer
    got = other(by_section(second, first))
    return by_section(
        jnp.concatenate([first, got], axis=1), jnp.concatenate([got, second], axis=1)
    )[None, :, None]


def solution(mesh):
    return jax.shard_map(
        local,
        mesh=mesh,
        in_specs=(
            P(None, "dp", "ctx", None),
            P(None, "dp", None),
            P(None, "dp", "ctx", None),
            P("section", "dp"),
            P("section", "dp", None),
            P("section", "dp"),
            P("section", "dp", None),
            P("section", "dp"),
            P("section", "dp", None),
            P("section", "dp"),
            P("section", "dp", None),
            P("section", "dp"),
            P("section", "dp", None),
            P("section", "dp", None),
            P("section", "dp", None),
        ),
        out_specs=(
            P("section", None, "dp", "ctx", None),
            P("section", None, "dp", "ctx", None),
            P("section", "dp"),
            P("section", "dp", None),
            P("section", "dp"),
            P("section", "dp", None),
            P("section", "dp"),
            P("section", "dp", None),
            P("section", "dp"),
            P("section", "dp", None),
            P("section", "dp"),
            P("section", "dp", None),
            P("section", "dp", None),
            P("section", "dp", None),
        ),
        check_vma=False,
    )
```
